256 devices in a mesh: ctx: 64 (over x, z, core), tp: 4 (over y).
Axes of the slice: x: 4, y: 4, z: 8, core: 2. Of those that a mesh axis runs over, the one named last changes fastest.
Arguments:
- queries: bfloat16 [64, 2, 256, 2048], P('ctx', None, None, 'tp'), may hold values from -6 to 6
- keys: bfloat16 [64, 2, 256, 512], P('ctx', None, None, 'tp'), may hold values from -6 to 6
- values: bfloat16 [64, 2, 256, 512], P('ctx', None, None, 'tp'), may hold values from -24 to 24
- column_block_table: int32 [4, 64], P('tp'), may hold values from 0 to 255, as said below
- slash_offsets: int32 [16, 64], P('tp'), may hold values from 1 to 256, as said below
- out_weight: bfloat16 [2048, 4096], P('tp'), may hold values from -0.125 to 0.125
Outputs:
- mixed: bfloat16 [64, 2, 256, 4096], P('ctx', None, None, 'tp')
The draws below stay inside these ranges and needn't reach their ends.
Inputs may be any that keep to these rules, and one draw needn't show every extreme that they name: `column_block_table`: each row holds 64 distinct block numbers below 256, block b holding positions b * 128 to b * 128 + 127 and lying on the ctx device that holds its stretch. For each row, a quarter of the ctx devices hold exactly 2 of its blocks, half hold exactly one, the rest none. `slash_offsets`: each row holds 64 distinct offsets, and 1 and 256 are in every row.
All inputs are finite; a program needn't handle non-finite values.
Results may differ from the reference program's by a relative error of at most 0.00185.
The reference program's roundings to bfloat16 on the way count: a program that leaves them out, or rounds other values in their place, can miss the bound.
Values may be sent and summed in bfloat16 or wider, within the bound.
No kernel may reach another device: no remote copies, remote signals or barrier semaphores. Data moves between devices by JAX's collectives and lax.ppermute only.
A program may use at most 128 MiB of HBM per device.

```python
import jax
import jax.numpy as jnp
from jax import lax

D = 4096
LOCAL_Q_HEADS = 16
LOCAL_KV_HEADS = 4
HEAD_SIZE = 128
STRETCH_TOKENS = 256
KEY_BLOCK_TOKENS = 128
NS = 64
COLUMN_BLOCKS = 64
N_CTX = 64


def starting_plane(key, shape):
    return jax.random.truncated_normal(key, -6.0, 6.0, shape, jnp.float32)


def draw_queries(key, part):
    signal_plane = starting_plane(jax.random.fold_in(key, 11), (N_CTX, 2, STRETCH_TOKENS, LOCAL_Q_HEADS * HEAD_SIZE))
    return signal_plane.astype(jnp.bfloat16)


def draw_keys(key, part):
    signal_plane = starting_plane(jax.random.fold_in(key, 13), (N_CTX, 2, STRETCH_TOKENS, LOCAL_KV_HEADS * HEAD_SIZE))
    return signal_plane.astype(jnp.bfloat16)


def draw_column_block_table(key, part):
    ctx_count = N_CTX
    stretch_blocks = STRETCH_TOKENS // KEY_BLOCK_TOKENS
    local_total = 2 * stretch_blocks
    hot_count = ctx_count // 4
    rows_list = []
    for group_number in range(LOCAL_KV_HEADS):
        group_key = jax.random.fold_in(jax.random.fold_in(key, 101), group_number)
        order_key, pick_key, shuffle_key = jax.random.split(group_key, 3)
        device_order = jax.random.permutation(order_key, ctx_count).astype(jnp.int32)
        raw_scores = jax.random.randint(pick_key, (ctx_count, local_total), 0, 1 << 20)
        scores = raw_scores * local_total + jnp.arange(local_total, dtype=jnp.int32)[None, :]
        local_order = jnp.argsort(scores, axis=1).astype(jnp.int32)
        hot_devices = device_order[:hot_count]
        warm_devices = device_order[hot_count:3 * hot_count]
        devices_all = jnp.concatenate([hot_devices, hot_devices, warm_devices])
        locals_all = jnp.concatenate([local_order[hot_devices, 0], local_order[hot_devices, 1], local_order[warm_devices, 0]])
        stretch_ids = jnp.where(locals_all < stretch_blocks, devices_all, 2 * ctx_count - 1 - devices_all)
        block_ids = stretch_ids * stretch_blocks + locals_all % stretch_blocks
        rows_list.append(jax.random.permutation(shuffle_key, block_ids))
    return jnp.stack(rows_list).astype(jnp.int32)


def draw_slash_offsets(key, part):
    rows_list = []
    for head_index in range(LOCAL_Q_HEADS):
        head_key = jax.random.fold_in(jax.random.fold_in(key, 202), head_index)
        raw_scores = jax.random.randint(head_key, (STRETCH_TOKENS - 2,), 0, 1 << 18)
        scores = raw_scores * (STRETCH_TOKENS - 2) + jnp.arange(STRETCH_TOKENS - 2, dtype=jnp.int32)
        middle = jnp.argsort(scores)[:NS - 2].astype(jnp.int32) + 2
        rows_list.append(jnp.concatenate([jnp.array([1, STRETCH_TOKENS], jnp.int32), middle]))
    return jnp.stack(rows_list).astype(jnp.int32)


def levels(stream_key, shape, cuts, smallest, largest):
    loudness, own = 1.0, jax.random.fold_in(stream_key, 6)
    for dim, parts in cuts:
        steps = jnp.exp(jax.random.uniform(jax.random.fold_in(own, dim), (parts,), jnp.float32, smallest / len(cuts), largest / len(cuts)))
        loudness = loudness * jnp.repeat(steps, shape[dim] // parts).reshape([-1 if axis == dim else 1 for axis in range(len(shape))])
    return loudness


def gaussian(own_key, extent, scale, bound, cuts=(), kind=jnp.bfloat16):
    gain = levels(own_key, extent, cuts, -0.22, 0.18) if cuts else 1.0
    result = jax.random.normal(own_key, extent, jnp.float32) * scale * gain
    return jnp.minimum(jnp.maximum(result, -bound), bound).astype(kind)


def setup_inputs(seed: int = 0) -> dict:
    splits = jax.random.split(jax.random.key(seed), 7)
    return {
        "queries": draw_queries(jax.random.fold_in(splits[6], 71), 0),
        "keys": draw_keys(jax.random.fold_in(splits[6], 71), 0),
        "values": gaussian(splits[2], (N_CTX, 2, STRETCH_TOKENS, LOCAL_KV_HEADS * HEAD_SIZE), 4.0, 24.0, ((0, 64), (3, 4))),
        "column_block_table": draw_column_block_table(jax.random.fold_in(splits[6], 71), 0),
        "slash_offsets": draw_slash_offsets(jax.random.fold_in(splits[6], 71), 0),
        "out_weight": gaussian(splits[5], (LOCAL_Q_HEADS * HEAD_SIZE, D), (LOCAL_Q_HEADS * HEAD_SIZE) ** -0.5, 0.125, ((0, 4),)),
    }


def into_sequence_order(array):
    return jnp.concatenate([array[:, 0], array[::-1, 1]], axis=0)


def reference(queries, keys, values, column_block_table, slash_offsets, out_weight):
    stretches_overall = 2 * N_CTX
    heads_per_group = LOCAL_Q_HEADS // LOCAL_KV_HEADS
    scale = HEAD_SIZE ** -0.5
    head_group = jnp.arange(LOCAL_Q_HEADS, dtype=jnp.int32) // heads_per_group
    seq_query = into_sequence_order(queries).astype(jnp.float32).reshape(stretches_overall, STRETCH_TOKENS, LOCAL_Q_HEADS, HEAD_SIZE)
    sequence_keys = into_sequence_order(keys).astype(jnp.float32).reshape(stretches_overall, STRETCH_TOKENS, LOCAL_KV_HEADS, HEAD_SIZE)
    sequence_values = into_sequence_order(values).astype(jnp.float32).reshape(stretches_overall, STRETCH_TOKENS, LOCAL_KV_HEADS, HEAD_SIZE)
    flattened_keys = sequence_keys.reshape(stretches_overall * STRETCH_TOKENS, LOCAL_KV_HEADS, HEAD_SIZE)
    flattened_values = sequence_values.reshape(stretches_overall * STRETCH_TOKENS, LOCAL_KV_HEADS, HEAD_SIZE)
    column_position = (column_block_table[:, :, None] * KEY_BLOCK_TOKENS + jnp.arange(KEY_BLOCK_TOKENS, dtype=jnp.int32)[None, None, :]).reshape(LOCAL_KV_HEADS, COLUMN_BLOCKS * KEY_BLOCK_TOKENS)
    group_query_rows = jnp.arange(LOCAL_KV_HEADS, dtype=jnp.int32)[:, None]
    column_keys = flattened_keys[column_position, group_query_rows][head_group]
    column_vals = flattened_values[column_position, group_query_rows][head_group]
    head_pos = column_position[head_group]
    relative = jnp.arange(3 * STRETCH_TOKENS, dtype=jnp.int32) - STRETCH_TOKENS
    slash_table = jnp.any(relative[None, None, :] == slash_offsets[:, :, None], axis=1) | (relative == 0)[None, :]

    def one_stretch(stretch_index):
        query_pos = stretch_index * STRETCH_TOKENS + jnp.arange(STRETCH_TOKENS, dtype=jnp.int32)
        band_pos = (stretch_index - 1) * STRETCH_TOKENS + jnp.arange(2 * STRETCH_TOKENS, dtype=jnp.int32)
        before = jnp.maximum(stretch_index - 1, 0)
        band_keys = jnp.concatenate([sequence_keys[before], sequence_keys[stretch_index]], axis=0)[:, head_group]
        band_vals = jnp.concatenate([sequence_values[before], sequence_values[stretch_index]], axis=0)[:, head_group]
        stretch_query = seq_query[stretch_index]
        col_scores = jnp.einsum("ihd,hjd->hij", stretch_query, column_keys) * scale
        col_mask = head_pos[:, None, :] <= query_pos[None, :, None]
        band_scores = jnp.einsum("ihd,jhd->hij", stretch_query, band_keys) * scale
        distance = query_pos[:, None] - band_pos[None, :]
        listed_band = jnp.any((band_pos // KEY_BLOCK_TOKENS)[None, :, None] == column_block_table[:, None, :], axis=2)[head_group]
        band_mask = slash_table[:, distance + STRETCH_TOKENS] & (band_pos >= 0)[None, None, :] & (~listed_band)[:, None, :]
        col_max = jnp.max(jnp.where(col_mask, col_scores, -jnp.inf), axis=2)
        band_max = jnp.max(jnp.where(band_mask, band_scores, -jnp.inf), axis=2)
        row_max = jnp.maximum(col_max, band_max)
        col_exp = jnp.where(col_mask, jnp.exp(col_scores - row_max[:, :, None]), 0.0)
        band_exp = jnp.where(band_mask, jnp.exp(band_scores - row_max[:, :, None]), 0.0)
        row_total = jnp.sum(col_exp, axis=2) + jnp.sum(band_exp, axis=2)
        col_weight = lax.optimization_barrier(col_exp.astype(jnp.bfloat16)).astype(jnp.float32)
        band_weight = lax.optimization_barrier(band_exp.astype(jnp.bfloat16)).astype(jnp.float32)
        weighted = jnp.einsum("hij,hjd->hid", col_weight, column_vals) + jnp.einsum("hij,jhd->hid", band_weight, band_vals)
        head_out = (weighted / row_total[:, :, None]).astype(jnp.bfloat16)
        attended = head_out.transpose(1, 0, 2).reshape(STRETCH_TOKENS, LOCAL_Q_HEADS * HEAD_SIZE)
        return jnp.dot(attended, out_weight, preferred_element_type=jnp.float32).astype(jnp.bfloat16)

    mixed_seq = lax.map(one_stretch, jnp.arange(stretches_overall, dtype=jnp.int32))
    return jnp.stack([mixed_seq[:N_CTX], mixed_seq[N_CTX:][::-1]], axis=1)
```

```python
import functools
import math

import jax
import jax.numpy as jnp
from jax import lax
from jax.experimental import pallas as pl
from jax.experimental.pallas import tpu as pltpu
from jax.sharding import PartitionSpec as P

HEAD = 128
BLOCK = 128
STRETCH = 256
CAP = 2
GROUP = 4
SPAN = GROUP * BLOCK
LISTED = 64
HEADS = 4
EXP_SCALE = math.log2(math.e) * HEAD ** (-0.5)
VMEM_LIMIT = 48 * 1024 * 1024

SMEM = functools.partial(pl.BlockSpec, memory_space=pltpu.SMEM)
VMEM = functools.partial(pl.BlockSpec, memory_space=pltpu.VMEM)
ANY = functools.partial(pl.BlockSpec, memory_space=pl.ANY)
PARAMS = pltpu.CompilerParams(vmem_limit_bytes=VMEM_LIMIT)
F32 = jnp.float32
BF16 = jnp.bfloat16


def dot_t(a, b):
    return lax.dot_general(a, b, (((1,), (1,)), ((), ())), preferred_element_type=F32)


def plan_kernel(ctx_count, me_ref, table_ref, k_ref, v_ref, pay_ref, ahead_ref, back_ref, blk_ref, ent_ref, meta_ref, count, place):
    me = me_ref[0]
    stretches = 2 * ctx_count
    near, far = me, stretches - 1 - me

    def clear(i, _):
        place[4 * i] = -1
        place[4 * i + 1] = -1
        place[4 * i + 2] = -1
        place[4 * i + 3] = -1
        count[i] = 0
        return 0

    lax.fori_loop(0, ctx_count, clear, 0)

    def assign(j, carry):
        loc0, loc1 = carry
        b = table_ref[0, j]
        stretch = b // 2
        first = stretch < ctx_count
        owner = jnp.where(first, stretch, stretches - 1 - stretch)
        local = jnp.where(first, 0, 2) + b % 2
        rank = count[owner]
        count[owner] = rank + 1
        place[b] = owner * CAP + rank
        mine = owner == me
        loc0 = jnp.where(mine & (rank == 0), local, loc0)
        loc1 = jnp.where(mine & (rank == 1), local, loc1)
        return loc0, loc1

    loc0, loc1 = lax.fori_loop(0, LISTED, assign, (jnp.int32(0), jnp.int32(0)))
    for slot, loc in enumerate((loc0, loc1)):
        pay_ref[slot, 0] = k_ref[loc]
        pay_ref[slot, 1] = v_ref[loc]
    for half, ref in ((0, ahead_ref), (1, back_ref)):
        for part in range(2):
            ref[0, part * BLOCK : (part + 1) * BLOCK] = k_ref[2 * half + part]
            ref[1, part * BLOCK : (part + 1) * BLOCK] = v_ref[2 * half + part]

    def order(b, carry):
        at, full0, seen0, full1, seen1 = carry
        e = place[b]
        blk_ref[at] = b
        ent_ref[at] = e
        hit = jnp.where(e >= 0, 1, 0)
        one = lambda test: jnp.where(test, hit, 0)
        return (
            at + hit,
            full0 + one(b < 2 * near),
            seen0 + one(b <= 2 * near + 1),
            full1 + one(b < 2 * far),
            seen1 + one(b <= 2 * far + 1),
        )

    zero = jnp.int32(0)
    _, full0, seen0, full1, seen1 = lax.fori_loop(0, 4 * ctx_count, order, (zero,) * 5)
    for st, (s, full, seen) in enumerate(((near, full0, seen0), (far, full1, seen1))):
        meta_ref[8 * st] = full
        meta_ref[8 * st + 1] = seen
        meta_ref[8 * st + 2] = s
        meta_ref[8 * st + 3] = me
        for n in range(4):
            b = 2 * (s - 1) + n
            free = place[jnp.maximum(b, 0)] < 0
            meta_ref[8 * st + 4 + n] = jnp.where((b >= 0) & free, 1, 0)


def band_halves(own_ref, ahead_ref, back_ref, which, st, me, ctx_count):
    if st == 0:
        return ahead_ref[which]
    return jnp.where(me == ctx_count - 1, own_ref[0], back_ref[which])


def band_kernel(ctx_count, meta_ref, slash_ref, q_ref, k_ref, ahead_ref, back_ref, mask_ref, top_ref):
    behind = STRETCH - lax.broadcasted_iota(jnp.int32, (8, 2 * STRETCH), 1)
    for h in range(HEADS):
        def listed(n, hit):
            return hit | (behind == slash_ref[h, n])

        hit = behind == 0
        for n in range(LISTED):
            hit = listed(n, hit)
        row = jnp.where(hit, 1.0, 0.0).astype(F32)[:1]
        spread = jnp.broadcast_to(row, (STRETCH, 2 * STRETCH))
        mask_ref[h] = pltpu.roll(spread, 0, 1, stride=1, stride_axis=0)
    me = meta_ref[3]
    for st in range(2):
        before = band_halves(k_ref, ahead_ref, back_ref, 0, st, me, ctx_count)
        for h in range(HEADS):
            q = q_ref[st, :, h * HEAD : (h + 1) * HEAD]
            top = jnp.full((STRETCH, BLOCK), -jnp.inf, F32)
            for n in range(4):
                part = before if n < 2 else k_ref[st]
                s = dot_t(q, part[(n % 2) * BLOCK : (n % 2 + 1) * BLOCK])
                ok = (mask_ref[h, :, n * BLOCK : (n + 1) * BLOCK] > 0.5) & (meta_ref[8 * st + 4 + n] > 0)
                top = jnp.maximum(top, jnp.where(ok, s, -jnp.inf))
            top_ref[st, h] = top


def fetch(ent_ref, source_ref, which, target_ref, sems, groups):
    def start(j, _):
        e = ent_ref[j]
        pltpu.make_async_copy(source_ref.at[e // CAP, e % CAP, which], target_ref.at[j], sems.at[j // GROUP]).start()
        return 0

    lax.fori_loop(0, groups * GROUP, start, 0)


def arrived(target_ref, sems, g):
    part = target_ref.at[pl.ds(g * GROUP, GROUP)]
    pltpu.make_async_copy(part, part, sems.at[g]).wait()


def causal(blk_ref, s, g):
    lead = lax.broadcasted_iota(jnp.int32, (STRETCH, BLOCK), 1) - lax.broadcasted_iota(jnp.int32, (STRETCH, BLOCK), 0)
    return [lead <= s * STRETCH - blk_ref[g * GROUP + n] * BLOCK for n in range(GROUP)]


def top_kernel(meta_ref, blk_ref, ent_ref, q_ref, top_in_ref, source_ref, keys_ref, top_ref, sems):
    fetch(ent_ref, source_ref, 0, keys_ref, sems, LISTED // GROUP)

    def ready(g, _):
        arrived(keys_ref, sems, g)
        return 0

    lax.fori_loop(0, LISTED // GROUP, ready, 0)
    for st in range(2):
        full, seen, s = meta_ref[8 * st], meta_ref[8 * st + 1], meta_ref[8 * st + 2]
        plain, groups = full // GROUP, (seen + GROUP - 1) // GROUP
        for h in range(HEADS):
            top_ref[st, h] = top_in_ref[st, h]

        def step(masked, g, _):
            keys = keys_ref[pl.ds(g * GROUP, GROUP)].reshape(SPAN, HEAD)
            ok = causal(blk_ref, s, g) if masked else None
            for h in range(HEADS):
                scores = dot_t(q_ref[st, :, h * HEAD : (h + 1) * HEAD], keys)
                tops = []
                for n in range(GROUP):
                    part = scores[:, n * BLOCK : (n + 1) * BLOCK]
                    tops.append(jnp.where(ok[n], part, -jnp.inf) if masked else part)
                top = functools.reduce(jnp.maximum, tops)
                top_ref[st, h] = jnp.maximum(top_ref[st, h], top)
            return 0

        lax.fori_loop(0, plain, functools.partial(step, False), 0)
        lax.fori_loop(plain, groups, functools.partial(step, True), 0)
        for h in range(HEADS):
            row = jnp.max(top_ref[st, h], axis=1, keepdims=True)
            top_ref[st, h] = jnp.broadcast_to(row, (STRETCH, BLOCK))


def out_kernel(ctx_count, st, meta_ref, blk_ref, ent_ref, q_ref, keys_ref, top_ref, mask_ref, k_ref, v_ref, ahead_ref, back_ref, source_ref, out_ref, vals, total, acc, sems):
    full, seen, s = meta_ref[8 * st], meta_ref[8 * st + 1], meta_ref[8 * st + 2]
    me = meta_ref[8 * st + 3]
    plain, groups = full // GROUP, (seen + GROUP - 1) // GROUP
    fetch(ent_ref, source_ref, 1, vals, sems, groups)
    k_before = band_halves(k_ref, ahead_ref, back_ref, 0, st, me, ctx_count)
    v_before = band_halves(v_ref, ahead_ref, back_ref, 1, st, me, ctx_count)

    for h in range(HEADS):
        q = q_ref[0, :, h * HEAD : (h + 1) * HEAD]
        scores = [dot_t(q, k_before), dot_t(q, k_ref[st])]
        expos = []
        for n in range(4):
            part = scores[n // 2][:, (n % 2) * BLOCK : (n % 2 + 1) * BLOCK]
            ok = (mask_ref[h, :, n * BLOCK : (n + 1) * BLOCK] > 0.5) & (meta_ref[8 * st + 4 + n] > 0)
            expos.append(jnp.where(ok, jnp.exp2((part - top_ref[0, h]) * EXP_SCALE), 0.0))
        total[h] = (expos[0] + expos[1]) + (expos[2] + expos[3])
        weights = [e.astype(BF16) for e in expos]
        acc[h] = jnp.dot(
            jnp.concatenate(weights[:2], axis=1), v_before, preferred_element_type=F32
        ) + jnp.dot(jnp.concatenate(weights[2:], axis=1), v_ref[st], preferred_element_type=F32)

    def step(masked, g, _):
        arrived(vals, sems, g)
        keys = keys_ref[pl.ds(g * GROUP, GROUP)].reshape(SPAN, HEAD)
        values = vals[pl.ds(g * GROUP, GROUP)].reshape(SPAN, HEAD)
        ok = causal(blk_ref, s, g) if masked else None
        for h in range(HEADS):
            scores = dot_t(q_ref[0, :, h * HEAD : (h + 1) * HEAD], keys)
            expos = []
            for n in range(GROUP):
                part = jnp.exp2((scores[:, n * BLOCK : (n + 1) * BLOCK] - top_ref[0, h]) * EXP_SCALE)
                expos.append(jnp.where(ok[n], part, 0.0) if masked else part)
            total[h] += (expos[0] + expos[1]) + (expos[2] + expos[3])
            weights = jnp.concatenate([e.astype(BF16) for e in expos], axis=1)
            acc[h] += jnp.dot(weights, values, preferred_element_type=F32)
        return 0

    lax.fori_loop(0, plain, functools.partial(step, False), 0)
    lax.fori_loop(plain, groups, functools.partial(step, True), 0)
    for h in range(HEADS):
        row = jnp.sum(total[h], axis=1, keepdims=True)
        out_ref[:, h * HEAD : (h + 1) * HEAD] = (acc[h] / row).astype(BF16)


def mix_kernel(a0, a1, a2, a3, w0, w1, w2, w3, *refs):
    out_ref = refs[-1]
    sums = [jnp.dot(a[...], w[...], preferred_element_type=F32) for a, w in ((a0, w0), (a1, w1), (a2, w2), (a3, w3))]
    out_ref[0] = ((sums[0] + sums[1]) + (sums[2] + sums[3])).astype(BF16)


def from_ahead(x, axis, shift):
    n = lax.axis_size(axis)
    return lax.ppermute(x, axis, [((i + shift) % n, i) for i in range(n)])


def per_device(queries, keys, values, column_block_table, slash_offsets, out_weight):
    ctx_count = lax.axis_size("ctx")
    tp = lax.axis_size("tp")
    me = lax.axis_index("ctx")
    tp_index = lax.axis_index("tp")
    q, k, v = queries[0], keys[0], values[0]
    shape = jax.ShapeDtypeStruct
    i32 = jnp.int32

    pay, ahead, back, blk, ent, meta = pl.pallas_call(
        functools.partial(plan_kernel, ctx_count),
        out_shape=[
            shape((CAP, 2, BLOCK, HEAD), BF16),
            shape((2, STRETCH, HEAD), BF16),
            shape((2, STRETCH, HEAD), BF16),
            shape((128,), i32),
            shape((128,), i32),
            shape((16,), i32),
        ],
        in_specs=[SMEM(), SMEM(), VMEM(), VMEM()],
        out_specs=[VMEM(), VMEM(), VMEM(), SMEM(), SMEM(), SMEM()],
        scratch_shapes=[pltpu.SMEM((ctx_count,), i32), pltpu.SMEM((4 * ctx_count,), i32)],
        compiler_params=PARAMS,
        name="plan",
    )(me.reshape(1).astype(i32), column_block_table, k.reshape(4, BLOCK, HEAD), v.reshape(4, BLOCK, HEAD))

    source = lax.all_gather(pay, "ctx", axis=0)

    steps = range(ctx_count - 1)
    before = lax.ppermute(ahead, "ctx", [(i, i + 1) for i in steps])
    after = lax.ppermute(back, "ctx", [(i + 1, i) for i in steps])

    width = out_weight.shape[1] // tp
    slabs = []
    for shift in range(tp):
        target = lax.rem(tp_index + tp - shift, tp)
        slab = lax.dynamic_slice(out_weight, (0, target * width), (out_weight.shape[0], width))
        slabs.append(slab if shift == 0 else from_ahead(slab, "tp", shift))

    mask, top = pl.pallas_call(
        functools.partial(band_kernel, ctx_count),
        out_shape=[shape((HEADS, STRETCH, 2 * STRETCH), F32), shape((2, HEADS, STRETCH, BLOCK), F32)],
        in_specs=[SMEM(), SMEM(), VMEM(), VMEM(), VMEM(), VMEM()],
        out_specs=[VMEM(), VMEM()],
        compiler_params=PARAMS,
        name="band",
    )(meta, slash_offsets, q, k, before, after)

    columns, top = pl.pallas_call(
        top_kernel,
        out_shape=[shape((LISTED, BLOCK, HEAD), BF16), shape((2, HEADS, STRETCH, BLOCK), F32)],
        in_specs=[SMEM(), SMEM(), SMEM(), VMEM(), VMEM(), ANY()],
        out_specs=[VMEM(), VMEM()],
        scratch_shapes=[pltpu.SemaphoreType.DMA((LISTED // GROUP,))],
        compiler_params=PARAMS,
        name="top",
    )(meta, blk, ent, q, top, source)

    mixed = None
    for st in range(2):
        head_out = pl.pallas_call(
            functools.partial(out_kernel, ctx_count, st),
            grid=(1,),
            out_shape=shape((STRETCH, HEADS * HEAD), BF16),
            in_specs=[
                SMEM(), SMEM(), SMEM(),
                pl.BlockSpec((1, STRETCH, HEADS * HEAD), lambda i, st=st: (st, 0, 0)),
                VMEM(),
                pl.BlockSpec((1, HEADS, STRETCH, BLOCK), lambda i, st=st: (st, 0, 0, 0)),
                VMEM(), VMEM(), VMEM(), VMEM(), VMEM(), ANY(),
            ],
            out_specs=VMEM(),
            scratch_shapes=[
                pltpu.VMEM((LISTED, BLOCK, HEAD), BF16),
                pltpu.VMEM((HEADS, STRETCH, BLOCK), F32),
                pltpu.VMEM((HEADS, STRETCH, HEAD), F32),
                pltpu.SemaphoreType.DMA((LISTED // GROUP,)),
            ],
            compiler_params=PARAMS,
            name=f"attend{st}",
        )(meta, blk, ent, q, columns, top, mask, k, v, before, after, source)
        parts = [head_out] + [from_ahead(head_out, "tp", shift) for shift in range(1, tp)]
        mixed = pl.pallas_call(
            mix_kernel,
            grid=(1,),
            out_shape=shape((2, STRETCH, width), BF16),
            in_specs=[VMEM()] * 8 + ([ANY()] if st else []),
            out_specs=pl.BlockSpec((1, STRETCH, width), lambda i, st=st: (st, 0, 0)),
            input_output_aliases={8: 0} if st else {},
            compiler_params=PARAMS,
            name=f"mix{st}",
        )(*parts, *slabs, *([mixed] if st else []))
    return mixed[None]


def solution(mesh):
    in_specs = (
        P("ctx", None, None, "tp"),
        P("ctx", None, None, "tp"),
        P("ctx", None, None, "tp"),
        P("tp", None),
        P("tp", None),
        P("tp", None),
    )
    out_specs = P("ctx", None, None, "tp")
    return jax.shard_map(
        per_device, mesh=mesh, in_specs=in_specs, out_specs=out_specs, check_vma=False
    )
```

```python
import functools
import math

import jax
import jax.numpy as jnp
from jax import lax
from jax.experimental import pallas as pl
from jax.experimental.pallas import tpu as pltpu
from jax.sharding import PartitionSpec as P

HEAD = 128
BLOCK = 128
STRETCH = 256
CAP = 2
GROUP = 8
SPAN = GROUP * BLOCK
LISTED = 64
X_CHIPS = 4
HEADS = 4
EXP_SCALE = math.log2(math.e) * HEAD ** (-0.5)
VMEM_LIMIT = 48 * 1024 * 1024

SMEM = functools.partial(pl.BlockSpec, memory_space=pltpu.SMEM)
VMEM = functools.partial(pl.BlockSpec, memory_space=pltpu.VMEM)
ANY = functools.partial(pl.BlockSpec, memory_space=pl.ANY)
PARAMS = pltpu.CompilerParams(vmem_limit_bytes=VMEM_LIMIT)
F32 = jnp.float32
BF16 = jnp.bfloat16


def dot_t(a, b):
    return lax.dot_general(a, b, (((1,), (1,)), ((), ())), preferred_element_type=F32)


def pack_kernel(ctx_count, me_ref, table_ref, k_ref, v_ref, keys_ref, vals_ref, ahead_ref, back_ref):
    me = me_ref[0]
    table = table_ref[...]
    stretch = table // 2
    first = stretch < ctx_count
    owner = jnp.where(first, stretch, 2 * ctx_count - 1 - stretch)
    local = jnp.where(first, 0, 2) + table % 2
    at = lax.broadcasted_iota(jnp.int32, table.shape, 1)
    mine = owner == me
    for slot in range(CAP):
        found = jnp.min(jnp.where(mine, at, LISTED))
        loc = jnp.sum(jnp.where(at == found, local, 0))
        mine = mine & (at > found)
        keys_ref[slot] = k_ref[loc]
        vals_ref[slot] = v_ref[loc]
    for half, ref in ((0, ahead_ref), (1, back_ref)):
        for part in range(2):
            ref[0, part * BLOCK : (part + 1) * BLOCK] = k_ref[2 * half + part]
            ref[1, part * BLOCK : (part + 1) * BLOCK] = v_ref[2 * half + part]


def plan_kernel(ctx_count, me_ref, table_ref, blk_ref, inv_ref, meta_ref, count, place):
    me = me_ref[0]
    stretches = 2 * ctx_count
    near, far = me, stretches - 1 - me

    def clear(i, _):
        for n in range(4):
            place[4 * i + n] = -1
        for n in range(CAP):
            inv_ref[CAP * i + n] = -1
        count[i] = 0
        return 0

    lax.fori_loop(0, ctx_count, clear, 0)

    def assign(j, _):
        b = table_ref[0, j]
        stretch = b // 2
        owner = jnp.where(stretch < ctx_count, stretch, stretches - 1 - stretch)
        rank = count[owner]
        count[owner] = rank + 1
        place[b] = owner * CAP + rank
        return 0

    lax.fori_loop(0, LISTED, assign, 0)

    def order(b, carry):
        at, full0, seen0, full1, seen1 = carry
        e = place[b]
        blk_ref[at] = b
        inv_ref[jnp.where(e >= 0, e, CAP * ctx_count)] = at
        hit = jnp.where(e >= 0, 1, 0)
        one = lambda test: jnp.where(test, hit, 0)
        return (
            at + hit,
            full0 + one(b < 2 * near),
            seen0 + one(b <= 2 * near + 1),
            full1 + one(b < 2 * far),
            seen1 + one(b <= 2 * far + 1),
        )

    zero = jnp.int32(0)
    _, full0, seen0, full1, seen1 = lax.fori_loop(0, 4 * ctx_count, order, (zero,) * 5)
    for st, (s, full, seen) in enumerate(((near, full0, seen0), (far, full1, seen1))):
        meta_ref[8 * st] = full
        meta_ref[8 * st + 1] = seen
        meta_ref[8 * st + 2] = s
        meta_ref[8 * st + 3] = me
        for n in range(4):
            b = 2 * (s - 1) + n
            free = place[jnp.maximum(b, 0)] < 0
            meta_ref[8 * st + 4 + n] = jnp.where((b >= 0) & free, 1, 0)


def band_halves(own_ref, ahead_ref, back_ref, which, st, me, ctx_count):
    if st == 0:
        return ahead_ref[which]
    return jnp.where(me == ctx_count - 1, own_ref[0], back_ref[which])


def band_kernel(ctx_count, meta_ref, slash_ref, q_ref, k_ref, ahead_ref, back_ref, mask_ref, top_ref):
    behind = STRETCH - lax.broadcasted_iota(jnp.int32, (8, 2 * STRETCH), 1)
    for h in range(HEADS):
        def listed(n, hit):
            return hit | (behind == slash_ref[h, n])

        hit = behind == 0
        for n in range(LISTED):
            hit = listed(n, hit)
        row = jnp.where(hit, 1.0, 0.0).astype(F32)[:1]
        spread = jnp.broadcast_to(row, (STRETCH, 2 * STRETCH))
        mask_ref[h] = pltpu.roll(spread, 0, 1, stride=1, stride_axis=0)
    me = meta_ref[3]
    for st in range(2):
        before = band_halves(k_ref, ahead_ref, back_ref, 0, st, me, ctx_count)
        for h in range(HEADS):
            q = q_ref[st, :, h * HEAD : (h + 1) * HEAD]
            top = jnp.full((STRETCH, BLOCK), -jnp.inf, F32)
            for n in range(4):
                part = before if n < 2 else k_ref[st]
                s = dot_t(q, part[(n % 2) * BLOCK : (n % 2 + 1) * BLOCK])
                ok = (mask_ref[h, :, n * BLOCK : (n + 1) * BLOCK] > 0.5) & (meta_ref[8 * st + 4 + n] > 0)
                top = jnp.maximum(top, jnp.where(ok, s, -jnp.inf))
            top_ref[st, h] = top


def fetch(inv_ref, me, pieces, origins, target_ref, sems):
    for ref, origin in zip(pieces, origins):
        def start(i, _, ref=ref, origin=origin):
            at = inv_ref[origin(me, i)]

            @pl.when(at >= 0)
            def _():
                pltpu.make_async_copy(ref.at[i], target_ref.at[at], sems.at[at // GROUP]).start()

            return 0

        lax.fori_loop(0, ref.shape[0], start, 0)


def arrived(target_ref, sems, g):
    part = target_ref.at[pl.ds(g * GROUP, GROUP)]
    pltpu.make_async_copy(part, part, sems.at[g]).wait()


def causal(blk_ref, s, g):
    lead = lax.broadcasted_iota(jnp.int32, (STRETCH, BLOCK), 1) - lax.broadcasted_iota(jnp.int32, (STRETCH, BLOCK), 0)
    return [lead <= s * STRETCH - blk_ref[g * GROUP + n] * BLOCK for n in range(GROUP)]


def top_kernel(origins, meta_ref, blk_ref, inv_ref, q_ref, top_in_ref, *refs):
    pieces, (keys_ref, top_ref, sems) = refs[:-3], refs[-3:]
    fetch(inv_ref, meta_ref[3], pieces, origins, keys_ref, sems)

    def ready(g, _):
        arrived(keys_ref, sems, g)
        return 0

    lax.fori_loop(0, LISTED // GROUP, ready, 0)
    for st in range(2):
        full, seen, s = meta_ref[8 * st], meta_ref[8 * st + 1], meta_ref[8 * st + 2]
        plain, groups = full // GROUP, (seen + GROUP - 1) // GROUP
        for h in range(HEADS):
            top_ref[st, h] = top_in_ref[st, h]

        def step(masked, g, _):
            keys = keys_ref[pl.ds(g * GROUP, GROUP)].reshape(SPAN, HEAD)
            ok = causal(blk_ref, s, g) if masked else None
            for h in range(HEADS):
                scores = dot_t(q_ref[st, :, h * HEAD : (h + 1) * HEAD], keys)
                tops = []
                for n in range(GROUP):
                    part = scores[:, n * BLOCK : (n + 1) * BLOCK]
                    tops.append(jnp.where(ok[n], part, -jnp.inf) if masked else part)
                top = functools.reduce(jnp.maximum, tops)
                top_ref[st, h] = jnp.maximum(top_ref[st, h], top)
            return 0

        lax.fori_loop(0, plain, functools.partial(step, False), 0)
        lax.fori_loop(plain, groups, functools.partial(step, True), 0)
        for h in range(HEADS):
            row = jnp.max(top_ref[st, h], axis=1, keepdims=True)
            top_ref[st, h] = jnp.broadcast_to(row, (STRETCH, BLOCK))


def out_kernel(ctx_count, st, origins, meta_ref, blk_ref, inv_ref, q_ref, keys_ref, top_ref, mask_ref, k_ref, v_ref, ahead_ref, back_ref, *refs):
    full, seen, s = meta_ref[8 * st], meta_ref[8 * st + 1], meta_ref[8 * st + 2]
    me = meta_ref[8 * st + 3]
    plain, groups = full // GROUP, (seen + GROUP - 1) // GROUP
    if origins:
        pieces, (out_ref, vals, total, acc, sems) = refs[:-5], refs[-5:]
        fetch(inv_ref, me, pieces, origins, vals, sems)
    else:
        vals, out_ref, total, acc = refs
    k_before = band_halves(k_ref, ahead_ref, back_ref, 0, st, me, ctx_count)
    v_before = band_halves(v_ref, ahead_ref, back_ref, 1, st, me, ctx_count)

    for h in range(HEADS):
        q = q_ref[0, :, h * HEAD : (h + 1) * HEAD]
        scores = [dot_t(q, k_before), dot_t(q, k_ref[st])]
        expos = []
        for n in range(4):
            part = scores[n // 2][:, (n % 2) * BLOCK : (n % 2 + 1) * BLOCK]
            ok = (mask_ref[h, :, n * BLOCK : (n + 1) * BLOCK] > 0.5) & (meta_ref[8 * st + 4 + n] > 0)
            expos.append(jnp.where(ok, jnp.exp2((part - top_ref[0, h]) * EXP_SCALE), 0.0))
        total[h] = (expos[0] + expos[1]) + (expos[2] + expos[3])
        weights = [e.astype(BF16) for e in expos]
        acc[h] = jnp.dot(
            jnp.concatenate(weights[:2], axis=1), v_before, preferred_element_type=F32
        ) + jnp.dot(jnp.concatenate(weights[2:], axis=1), v_ref[st], preferred_element_type=F32)

    def step(masked, g, _):
        if origins:
            arrived(vals, sems, g)
        keys = keys_ref[pl.ds(g * GROUP, GROUP)].reshape(SPAN, HEAD)
        values = vals[pl.ds(g * GROUP, GROUP)].reshape(SPAN, HEAD)
        ok = causal(blk_ref, s, g) if masked else None
        for h in range(HEADS):
            scores = dot_t(q_ref[0, :, h * HEAD : (h + 1) * HEAD], keys)
            expos = []
            for n in range(GROUP):
                part = jnp.exp2((scores[:, n * BLOCK : (n + 1) * BLOCK] - top_ref[0, h]) * EXP_SCALE)
                expos.append(jnp.where(ok[n], part, 0.0) if masked else part)
            total[h] += functools.reduce(jnp.add, expos)
            weights = jnp.concatenate([e.astype(BF16) for e in expos], axis=1)
            acc[h] += jnp.dot(weights, values, preferred_element_type=F32)
        return 0

    lax.fori_loop(0, plain, functools.partial(step, False), 0)
    lax.fori_loop(plain, groups, functools.partial(step, True), 0)
    if origins:
        def ready(g, _):
            arrived(vals, sems, g)
            return 0

        lax.fori_loop(groups, LISTED // GROUP, ready, 0)
    for h in range(HEADS):
        row = jnp.sum(total[h], axis=1, keepdims=True)
        out_ref[:, h * HEAD : (h + 1) * HEAD] = (acc[h] / row).astype(BF16)


def mix_kernel(a0, a1, a2, a3, w0, w1, w2, w3, *refs):
    out_ref = refs[-1]
    sums = [jnp.dot(a[...], w[...], preferred_element_type=F32) for a, w in ((a0, w0), (a1, w1), (a2, w2), (a3, w3))]
    out_ref[0] = ((sums[0] + sums[1]) + (sums[2] + sums[3])).astype(BF16)


def from_ahead(x, axis, shift):
    n = lax.axis_size(axis)
    return lax.ppermute(x, axis, [((i + shift) % n, i) for i in range(n)])


def gather_columns(mesh_sizes, keys, vals):
    nx, nz = mesh_sizes
    place = lambda x, z, c: ((x % nx) * nz + z % nz) * 2 + c
    every = [(x, z, c) for x in range(nx) for z in range(nz) for c in range(2)]
    route = lambda f: [(place(*d), place(*f(*d))) for d in every]
    across = route(lambda x, z, c: (x, z, 1 - c))
    along_x = route(lambda x, z, c: (x + 1 - 2 * c, z, c))
    along_z = route(lambda x, z, c: (x, z + 1 - 2 * c, c))
    send = lambda a, r: lax.ppermute(a, "ctx", r)
    lines = [[place(x, z, c) for z in range(nz)] for x in range(nx) for c in range(2)]

    line = [vals] + [send(vals, route(lambda x, z, c, n=n: (x - n, z, c))) for n in range(1, nx)]
    own = jnp.stack(line)
    chip = jnp.stack([own, send(own, across)])
    v_pieces = [chip]
    own_k = lax.all_to_all(jnp.broadcast_to(keys[None], (nz,) + keys.shape), "ctx", 0, 0, axis_index_groups=lines)
    moving = chip
    for n in range(1, nz // 2):
        moving = send(moving, along_z)
        v_pieces += [moving, send(moving, across)]
    last = send(moving[0], along_z)
    v_pieces += [last, send(last, across)]

    chip_k = jnp.stack([own_k, send(own_k, across)])
    one = send(chip_k, along_x)
    two = send(one[0], along_x)
    k_pieces = [chip_k, one, send(one, across), two, send(two, across)]

    def where(me):
        return me // (2 * nz), (me // 2) % nz, me % 2

    def entry(x, z, c, slot):
        return (((x + nx) % nx * nz + (z + nz) % nz) * 2 + c) * CAP + slot

    def k_origin(hops, mirrored, half):
        def origin(me, i):
            x, z, c = where(me)
            side = (2 * c - 1) * hops
            h = half if half is not None else i // (nz * CAP)
            core = jnp.where(h == 0, c, 1 - c)
            i = i % (nz * CAP)
            if mirrored:
                side, core = -side, 1 - core
            return entry(x + side, i // CAP, core, i % CAP)

        return origin

    def v_origin(hops, mirrored, half):
        def origin(me, i):
            x, z, c = where(me)
            side = (2 * c - 1) * hops
            h = half if half is not None else i // (nx * CAP)
            core = jnp.where(h == 0, c, 1 - c)
            i = i % (nx * CAP)
            if mirrored:
                side, core = -side, 1 - core
            return entry(x + i // CAP, z + side, core, i % CAP)

        return origin

    k_origins = [
        k_origin(0, False, None),
        k_origin(1, False, None),
        k_origin(1, True, None),
        k_origin(2, False, 0),
        k_origin(2, True, 0),
    ]
    v_origins = [v_origin(0, False, None)]
    for n in range(1, nz // 2):
        v_origins += [v_origin(n, False, None), v_origin(n, True, None)]
    v_origins += [v_origin(nz // 2, False, 0), v_origin(nz // 2, True, 0)]
    flat = lambda pieces: [p.reshape(-1, BLOCK, HEAD) for p in pieces]
    return flat(k_pieces), tuple(k_origins), flat(v_pieces), tuple(v_origins)


def per_device(queries, keys, values, column_block_table, slash_offsets, out_weight):
    ctx_count = lax.axis_size("ctx")
    tp = lax.axis_size("tp")
    me = lax.axis_index("ctx").reshape(1).astype(jnp.int32)
    tp_index = lax.axis_index("tp")
    q, k, v = queries[0], keys[0], values[0]
    shape = jax.ShapeDtypeStruct
    i32 = jnp.int32

    send_keys, send_vals, ahead, back = pl.pallas_call(
        functools.partial(pack_kernel, ctx_count),
        out_shape=[shape((CAP, BLOCK, HEAD), BF16)] * 2 + [shape((2, STRETCH, HEAD), BF16)] * 2,
        in_specs=[SMEM(), VMEM(), VMEM(), VMEM()],
        out_specs=[VMEM()] * 4,
        compiler_params=PARAMS,
        name="pack",
    )(me, column_block_table, k.reshape(4, BLOCK, HEAD), v.reshape(4, BLOCK, HEAD))

    k_pieces, k_origins, v_pieces, v_origins = gather_columns((X_CHIPS, ctx_count // (2 * X_CHIPS)), send_keys, send_vals)

    blk, inv, meta = pl.pallas_call(
        functools.partial(plan_kernel, ctx_count),
        out_shape=[shape((128,), i32), shape((256,), i32), shape((16,), i32)],
        in_specs=[SMEM(), SMEM()],
        out_specs=[SMEM()] * 3,
        scratch_shapes=[pltpu.SMEM((ctx_count,), i32), pltpu.SMEM((4 * ctx_count,), i32)],
        compiler_params=PARAMS,
        name="plan",
    )(me, column_block_table)

    steps = range(ctx_count - 1)
    before = lax.ppermute(ahead, "ctx", [(i, i + 1) for i in steps])
    after = lax.ppermute(back, "ctx", [(i + 1, i) for i in steps])

    width = out_weight.shape[1] // tp
    slabs = []
    for shift in range(tp):
        target = lax.rem(tp_index + tp - shift, tp)
        slab = lax.dynamic_slice(out_weight, (0, target * width), (out_weight.shape[0], width))
        slabs.append(slab if shift == 0 else from_ahead(slab, "tp", shift))

    mask, top = pl.pallas_call(
        functools.partial(band_kernel, ctx_count),
        out_shape=[shape((HEADS, STRETCH, 2 * STRETCH), F32), shape((2, HEADS, STRETCH, BLOCK), F32)],
        in_specs=[SMEM(), SMEM(), VMEM(), VMEM(), VMEM(), VMEM()],
        out_specs=[VMEM(), VMEM()],
        compiler_params=PARAMS,
        name="band",
    )(meta, slash_offsets, q, k, before, after)

    columns, top = pl.pallas_call(
        functools.partial(top_kernel, k_origins),
        out_shape=[shape((LISTED, BLOCK, HEAD), BF16), shape((2, HEADS, STRETCH, BLOCK), F32)],
        in_specs=[SMEM(), SMEM(), SMEM(), VMEM(), VMEM()] + [ANY()] * len(k_pieces),
        out_specs=[VMEM(), VMEM()],
        scratch_shapes=[pltpu.SemaphoreType.DMA((LISTED // GROUP,))],
        compiler_params=PARAMS,
        name="top",
    )(meta, blk, inv, q, top, *k_pieces)

    mixed = column_vals = None
    for st in range(2):
        arriving = st == 0
        result = pl.pallas_call(
            functools.partial(out_kernel, ctx_count, st, v_origins if arriving else ()),
            grid=(1,),
            out_shape=[shape((STRETCH, HEADS * HEAD), BF16)] + [shape((LISTED, BLOCK, HEAD), BF16)] * arriving,
            in_specs=[
                SMEM(), SMEM(), SMEM(),
                pl.BlockSpec((1, STRETCH, HEADS * HEAD), lambda i, st=st: (st, 0, 0)),
                VMEM(),
                pl.BlockSpec((1, HEADS, STRETCH, BLOCK), lambda i, st=st: (st, 0, 0, 0)),
                VMEM(), VMEM(), VMEM(), VMEM(), VMEM(),
            ] + ([ANY()] * len(v_pieces) if arriving else [VMEM()]),
            out_specs=[VMEM()] * (1 + arriving),
            scratch_shapes=[
                pltpu.VMEM((HEADS, STRETCH, BLOCK), F32),
                pltpu.VMEM((HEADS, STRETCH, HEAD), F32),
            ] + [pltpu.SemaphoreType.DMA((LISTED // GROUP,))] * arriving,
            compiler_params=PARAMS,
            name=f"attend{st}",
        )(meta, blk, inv, q, columns, top, mask, k, v, before, after, *(v_pieces if arriving else [column_vals]))
        head_out = result[0]
        if arriving:
            column_vals = result[1]
        parts = [head_out] + [from_ahead(head_out, "tp", shift) for shift in range(1, tp)]
        tile = width // 4
        mixed = pl.pallas_call(
            mix_kernel,
            grid=(width // tile,),
            out_shape=shape((2, STRETCH, width), BF16),
            in_specs=[VMEM()] * 4
            + [pl.BlockSpec((HEADS * HEAD, tile), lambda i: (0, i))] * 4
            + ([ANY()] if st else []),
            out_specs=pl.BlockSpec((1, STRETCH, tile), lambda i, st=st: (st, 0, i)),
            input_output_aliases={8: 0} if st else {},
            compiler_params=PARAMS,
            name=f"mix{st}",
        )(*parts, *slabs, *([mixed] if st else []))
    return mixed[None]


def solution(mesh):
    in_specs = (
        P("ctx", None, None, "tp"),
        P("ctx", None, None, "tp"),
        P("ctx", None, None, "tp"),
        P("tp", None),
        P("tp", None),
        P("tp", None),
    )
    out_specs = P("ctx", None, None, "tp")
    return jax.shard_map(
        per_device, mesh=mesh, in_specs=in_specs, out_specs=out_specs, check_vma=False
    )
```

```python
import functools
import math

import jax
import jax.numpy as jnp
from jax import lax
from jax.experimental import pallas as pl
from jax.experimental.pallas import tpu as pltpu
from jax.sharding import PartitionSpec as P

HEAD = 128
BLOCK = 128
STRETCH = 256
CAP = 2
GROUP = 8
SPAN = GROUP * BLOCK
LISTED = 64
UNROLL = 4
X_CHIPS = 4
HEADS = 4
EXP_SCALE = math.log2(math.e) * HEAD ** (-0.5)
VMEM_LIMIT = 48 * 1024 * 1024

SMEM = functools.partial(pl.BlockSpec, memory_space=pltpu.SMEM)
VMEM = functools.partial(pl.BlockSpec, memory_space=pltpu.VMEM)
ANY = functools.partial(pl.BlockSpec, memory_space=pl.ANY)
PARAMS = pltpu.CompilerParams(vmem_limit_bytes=VMEM_LIMIT)
F32 = jnp.float32
BF16 = jnp.bfloat16


def dot_t(a, b):
    return lax.dot_general(a, b, (((1,), (1,)), ((), ())), preferred_element_type=F32)


def pack_kernel(ctx_count, me_ref, table_ref, k_ref, v_ref, pay_ref, ahead_ref, back_ref):
    me = me_ref[0]
    table = table_ref[...]
    stretch = table // 2
    first = stretch < ctx_count
    owner = jnp.where(first, stretch, 2 * ctx_count - 1 - stretch)
    local = jnp.where(first, 0, 2) + table % 2
    at = lax.broadcasted_iota(jnp.int32, table.shape, 1)
    mine = owner == me
    for slot in range(CAP):
        found = jnp.min(jnp.where(mine, at, LISTED))
        loc = jnp.sum(jnp.where(at == found, local, 0))
        mine = mine & (at > found)
        pay_ref[0, slot] = k_ref[loc]
        pay_ref[1, slot] = v_ref[loc]
    for half, ref in ((0, ahead_ref), (1, back_ref)):
        for part in range(2):
            ref[0, part * BLOCK : (part + 1) * BLOCK] = k_ref[2 * half + part]
            ref[1, part * BLOCK : (part + 1) * BLOCK] = v_ref[2 * half + part]


def plan_kernel(ctx_count, arrivals, me_ref, table_ref, blk_ref, at_ref, meta_ref, count, place, inv_ref):
    me = me_ref[0]
    stretches = 2 * ctx_count
    near, far = me, stretches - 1 - me

    def clear(i, _):
        for n in range(4):
            place[4 * i + n] = -1
        for n in range(CAP):
            inv_ref[CAP * i + n] = -1
        count[i] = 0
        return 0

    lax.fori_loop(0, ctx_count, clear, 0)

    def assign(j, _):
        b = table_ref[0, j]
        stretch = lax.div(b, 2)
        owner = jnp.where(stretch < ctx_count, stretch, stretches - 1 - stretch)
        rank = count[owner]
        count[owner] = rank + 1
        place[b] = owner * CAP + rank
        return 0

    lax.fori_loop(0, LISTED, assign, 0)

    def order(b, carry):
        at, full0, seen0, full1, seen1 = carry
        e = place[b]
        blk_ref[at] = b
        inv_ref[jnp.where(e >= 0, e, CAP * ctx_count)] = at
        hit = jnp.where(e >= 0, 1, 0)
        one = lambda test: jnp.where(test, hit, 0)
        return (
            at + hit,
            full0 + one(b < 2 * near),
            seen0 + one(b <= 2 * near + 1),
            full1 + one(b < 2 * far),
            seen1 + one(b <= 2 * far + 1),
        )

    zero = jnp.int32(0)
    _, full0, seen0, full1, seen1 = lax.fori_loop(0, 4 * ctx_count, order, (zero,) * 5)
    for i, (owner, slot) in enumerate(arrivals(me)):
        at_ref[i] = inv_ref[owner * CAP + slot]
    for st, (s, full, seen) in enumerate(((near, full0, seen0), (far, full1, seen1))):
        meta_ref[8 * st] = full
        meta_ref[8 * st + 1] = seen
        meta_ref[8 * st + 2] = s
        meta_ref[8 * st + 3] = me
        for n in range(4):
            b = 2 * (s - 1) + n
            free = place[jnp.maximum(b, 0)] < 0
            meta_ref[8 * st + 4 + n] = jnp.where((b >= 0) & free, 1, 0)


def band_halves(own_ref, ahead_ref, back_ref, which, st, me, ctx_count):
    if st == 0:
        return ahead_ref[which]
    return jnp.where(me == ctx_count - 1, own_ref[0], back_ref[which])


def band_kernel(ctx_count, meta_ref, slash_ref, q_ref, k_ref, ahead_ref, back_ref, mask_ref, top_ref):
    behind = STRETCH - lax.broadcasted_iota(jnp.int32, (8, 2 * STRETCH), 1)
    for h in range(HEADS):
        def listed(n, hit):
            return hit | (behind == slash_ref[h, n])

        hit = behind == 0
        for n in range(LISTED):
            hit = listed(n, hit)
        row = jnp.where(hit, 1.0, 0.0).astype(F32)[:1]
        spread = jnp.broadcast_to(row, (STRETCH, 2 * STRETCH))
        mask_ref[h] = pltpu.roll(spread, 0, 1, stride=1, stride_axis=0)
    me = meta_ref[3]
    for st in range(2):
        before = band_halves(k_ref, ahead_ref, back_ref, 0, st, me, ctx_count)
        for h in range(HEADS):
            q = q_ref[st, :, h * HEAD : (h + 1) * HEAD]
            top = jnp.full((STRETCH, BLOCK), -jnp.inf, F32)
            for n in range(4):
                part = before if n < 2 else k_ref[st]
                s = dot_t(q, part[(n % 2) * BLOCK : (n % 2 + 1) * BLOCK])
                ok = (mask_ref[h, :, n * BLOCK : (n + 1) * BLOCK] > 0.5) & (meta_ref[8 * st + 4 + n] > 0)
                top = jnp.maximum(top, jnp.where(ok, s, -jnp.inf))
            top_ref[st, h] = top


def fetch(at_ref, pieces, target_ref, sems):
    base = 0
    for ref in pieces:
        def start(i, _, ref=ref, base=base):
            for n in range(UNROLL):
                at = at_ref[base + i * UNROLL + n]

                @pl.when(at >= 0)
                def _(n=n, at=at):
                    pltpu.make_async_copy(
                        ref.at[i * UNROLL + n], target_ref.at[at], sems.at[lax.div(at, GROUP)]
                    ).start()

            return 0

        lax.fori_loop(0, ref.shape[0] // UNROLL, start, 0)
        base += ref.shape[0]


def arrived(target_ref, sems, g):
    part = target_ref.at[pl.ds(g * GROUP, GROUP)]
    pltpu.make_async_copy(part, part, sems.at[g]).wait()


def causal(blk_ref, s, g):
    lead = lax.broadcasted_iota(jnp.int32, (STRETCH, BLOCK), 1) - lax.broadcasted_iota(jnp.int32, (STRETCH, BLOCK), 0)
    return [lead <= s * STRETCH - blk_ref[g * GROUP + n] * BLOCK for n in range(GROUP)]


def top_kernel(meta_ref, blk_ref, at_ref, q_ref, top_in_ref, *refs):
    pieces, (keys_ref, top_ref, sems) = refs[:-3], refs[-3:]
    fetch(at_ref, pieces, keys_ref, sems)

    def ready(g, _):
        arrived(keys_ref, sems, g)
        return 0

    lax.fori_loop(0, LISTED // GROUP, ready, 0)
    for st in range(2):
        full, seen, s = meta_ref[8 * st], meta_ref[8 * st + 1], meta_ref[8 * st + 2]
        plain, groups = full // GROUP, (seen + GROUP - 1) // GROUP
        for h in range(HEADS):
            top_ref[st, h] = top_in_ref[st, h]

        def step(masked, g, _):
            keys = keys_ref[pl.ds(g * GROUP, GROUP)].reshape(SPAN, HEAD)
            ok = causal(blk_ref, s, g) if masked else None
            for h in range(HEADS):
                scores = dot_t(q_ref[st, :, h * HEAD : (h + 1) * HEAD], keys)
                tops = []
                for n in range(GROUP):
                    part = scores[:, n * BLOCK : (n + 1) * BLOCK]
                    tops.append(jnp.where(ok[n], part, -jnp.inf) if masked else part)
                top = functools.reduce(jnp.maximum, tops)
                top_ref[st, h] = jnp.maximum(top_ref[st, h], top)
            return 0

        lax.fori_loop(0, plain, functools.partial(step, False), 0)
        lax.fori_loop(plain, groups, functools.partial(step, True), 0)
        for h in range(HEADS):
            row = jnp.max(top_ref[st, h], axis=1, keepdims=True)
            top_ref[st, h] = jnp.broadcast_to(row, (STRETCH, BLOCK))


def out_kernel(ctx_count, st, arriving, meta_ref, blk_ref, at_ref, q_ref, keys_ref, top_ref, mask_ref, k_ref, v_ref, ahead_ref, back_ref, *refs):
    full, seen, s = meta_ref[8 * st], meta_ref[8 * st + 1], meta_ref[8 * st + 2]
    me = meta_ref[8 * st + 3]
    plain, groups = full // GROUP, (seen + GROUP - 1) // GROUP
    if arriving:
        pieces, (out_ref, vals, total, acc, sems) = refs[:arriving], refs[-5:]
        fetch(at_ref, pieces, vals, sems)
    else:
        vals, out_ref, total, acc = refs
    k_before = band_halves(k_ref, ahead_ref, back_ref, 0, st, me, ctx_count)
    v_before = band_halves(v_ref, ahead_ref, back_ref, 1, st, me, ctx_count)

    for h in range(HEADS):
        q = q_ref[0, :, h * HEAD : (h + 1) * HEAD]
        scores = [dot_t(q, k_before), dot_t(q, k_ref[st])]
        expos = []
        for n in range(4):
            part = scores[n // 2][:, (n % 2) * BLOCK : (n % 2 + 1) * BLOCK]
            ok = (mask_ref[h, :, n * BLOCK : (n + 1) * BLOCK] > 0.5) & (meta_ref[8 * st + 4 + n] > 0)
            expos.append(jnp.where(ok, jnp.exp2((part - top_ref[0, h]) * EXP_SCALE), 0.0))
        total[h] = (expos[0] + expos[1]) + (expos[2] + expos[3])
        weights = [e.astype(BF16) for e in expos]
        acc[h] = jnp.dot(
            jnp.concatenate(weights[:2], axis=1), v_before, preferred_element_type=F32
        ) + jnp.dot(jnp.concatenate(weights[2:], axis=1), v_ref[st], preferred_element_type=F32)

    def step(masked, g, _):
        if arriving:
            arrived(vals, sems, g)
        keys = keys_ref[pl.ds(g * GROUP, GROUP)].reshape(SPAN, HEAD)
        values = vals[pl.ds(g * GROUP, GROUP)].reshape(SPAN, HEAD)
        ok = causal(blk_ref, s, g) if masked else None
        for h in range(HEADS):
            scores = dot_t(q_ref[0, :, h * HEAD : (h + 1) * HEAD], keys)
            expos = []
            for n in range(GROUP):
                part = jnp.exp2((scores[:, n * BLOCK : (n + 1) * BLOCK] - top_ref[0, h]) * EXP_SCALE)
                expos.append(jnp.where(ok[n], part, 0.0) if masked else part)
            total[h] += functools.reduce(jnp.add, expos)
            weights = jnp.concatenate([e.astype(BF16) for e in expos], axis=1)
            acc[h] += jnp.dot(weights, values, preferred_element_type=F32)
        return 0

    lax.fori_loop(0, plain, functools.partial(step, False), 0)
    lax.fori_loop(plain, groups, functools.partial(step, True), 0)
    if arriving:
        def ready(g, _):
            arrived(vals, sems, g)
            return 0

        lax.fori_loop(groups, LISTED // GROUP, ready, 0)
    for h in range(HEADS):
        row = jnp.sum(total[h], axis=1, keepdims=True)
        out_ref[:, h * HEAD : (h + 1) * HEAD] = (acc[h] / row).astype(BF16)


def mix_kernel(a0, a1, a2, a3, w0, w1, w2, w3, *refs):
    out_ref = refs[-1]
    sums = [jnp.dot(a[...], w[...], preferred_element_type=F32) for a, w in ((a0, w0), (a1, w1), (a2, w2), (a3, w3))]
    out_ref[0] = ((sums[0] + sums[1]) + (sums[2] + sums[3])).astype(BF16)


def from_ahead(x, axis, shift):
    n = lax.axis_size(axis)
    return lax.ppermute(x, axis, [((i + shift) % n, i) for i in range(n)])


def line_kernel(*refs):
    pieces, out_ref = refs[:-1], refs[-1]
    for n, ref in enumerate(pieces):
        for which in range(2):
            out_ref[which, n * CAP : (n + 1) * CAP] = ref[which]


def chip_kernel(own_ref, other_ref, keys_ref, vals_ref):
    count = own_ref.shape[1]
    for which, ref in ((0, keys_ref), (1, vals_ref)):
        ref[:count] = own_ref[which]
        ref[count:] = other_ref[which]


def half_kernel(keys_ref, vals_ref, *refs):
    for source, target in ((keys_ref, refs[-2]), (vals_ref, refs[-1])):
        target[...] = source[...]


def gather_columns(nx, nz, payload, ready):
    place = lambda x, z, c: ((x % nx) * nz + z % nz) * 2 + c
    every = [(x, z, c) for x in range(nx) for z in range(nz) for c in range(2)]
    route = lambda f: [(place(*d), place(*f(*d))) for d in every]
    across = route(lambda x, z, c: (x, z, 1 - c))
    along = route(lambda x, z, c: (x, z + 1 - 2 * c, c))
    send = lambda a, r: lax.ppermute(a, "ctx", r)

    shape = jax.ShapeDtypeStruct
    call = functools.partial(pl.pallas_call, compiler_params=PARAMS)
    size = nx * CAP
    line = [payload] + [send(payload, route(lambda x, z, c, n=n: (x - n, z, c))) for n in range(1, nx)]
    own = call(
        line_kernel,
        out_shape=shape((2, size, BLOCK, HEAD), BF16),
        in_specs=[VMEM()] * nx,
        out_specs=VMEM(),
        name="line",
    )(*line)
    moving = call(
        chip_kernel,
        out_shape=[shape((2 * size, BLOCK, HEAD), BF16)] * 2,
        in_specs=[VMEM()] * 2,
        out_specs=[VMEM()] * 2,
        name="chip",
    )(own, send(own, across))
    pieces = [[m] for m in moving]
    for n in range(1, nz // 2 + 1):
        if n == nz // 2:
            moving = call(
                half_kernel,
                grid=(1,),
                out_shape=[shape((size, BLOCK, HEAD), BF16)] * 2,
                in_specs=[pl.BlockSpec((size, BLOCK, HEAD), lambda i: (0, 0, 0))] * 2 + [ANY()] * len(ready),
                out_specs=[VMEM()] * 2,
                name="half",
            )(*moving, *ready)
        moving = [send(m, along) for m in moving]
        for which in range(2):
            pieces[which] += [moving[which], send(moving[which], across)]

    return pieces


def arrivals(nx, nz, me):
    x, z, c = lax.div(me, 2 * nz), lax.rem(lax.div(me, 2), nz), lax.rem(me, 2)
    lines = [lax.rem(x + n, nx) * nz for n in range(nx)]
    entries = []

    def piece(hops, mirrored, halves):
        side = (2 * c - 1) * hops
        at = lax.rem(z + nz + (-side if mirrored else side), nz)
        for half in range(halves):
            core = 1 - c if mirrored != (half == 1) else c
            for n in range(nx):
                entries.extend(((lines[n] + at) * 2 + core, slot) for slot in range(CAP))

    piece(0, False, 2)
    for n in range(1, nz // 2 + 1):
        for mirrored in (False, True):
            piece(n, mirrored, 2 if n < nz // 2 else 1)
    return entries


def cost(us):
    return pl.CostEstimate(flops=0, bytes_accessed=int(us * 3.0e6), transcendentals=0)


def per_device(queries, keys, values, column_block_table, slash_offsets, out_weight):
    ctx_count = lax.axis_size("ctx")
    tp = lax.axis_size("tp")
    me = lax.axis_index("ctx").reshape(1).astype(jnp.int32)
    tp_index = lax.axis_index("tp")
    q, k, v = queries[0], keys[0], values[0]
    shape = jax.ShapeDtypeStruct
    i32 = jnp.int32

    payload, ahead, back = pl.pallas_call(
        functools.partial(pack_kernel, ctx_count),
        out_shape=[shape((2, CAP, BLOCK, HEAD), BF16)] + [shape((2, STRETCH, HEAD), BF16)] * 2,
        in_specs=[SMEM(), VMEM(), VMEM(), VMEM()],
        out_specs=[VMEM()] * 3,
        compiler_params=PARAMS,
        name="pack",
    )(me, column_block_table, k.reshape(4, BLOCK, HEAD), v.reshape(4, BLOCK, HEAD))

    sides = (X_CHIPS, ctx_count // (2 * X_CHIPS))
    blk, at, meta = pl.pallas_call(
        functools.partial(plan_kernel, ctx_count, functools.partial(arrivals, *sides)),
        out_shape=[shape((128,), i32), shape((CAP * ctx_count,), i32), shape((16,), i32)],
        in_specs=[SMEM(), SMEM()],
        out_specs=[SMEM()] * 3,
        scratch_shapes=[pltpu.SMEM((ctx_count,), i32), pltpu.SMEM((4 * ctx_count,), i32), pltpu.SMEM((4 * ctx_count,), i32)],
        compiler_params=PARAMS,
        cost_estimate=cost(8),
        name="plan",
    )(me, column_block_table)

    steps = range(ctx_count - 1)
    before = lax.ppermute(ahead, "ctx", [(i, i + 1) for i in steps])
    after = lax.ppermute(back, "ctx", [(i + 1, i) for i in steps])

    width = out_weight.shape[1] // tp
    slabs = []
    for shift in range(tp):
        target = lax.rem(tp_index + tp - shift, tp)
        slab = lax.dynamic_slice(out_weight, (0, target * width), (out_weight.shape[0], width))
        slabs.append(slab if shift == 0 else from_ahead(slab, "tp", shift))

    mask, top = pl.pallas_call(
        functools.partial(band_kernel, ctx_count),
        out_shape=[shape((HEADS, STRETCH, 2 * STRETCH), F32), shape((2, HEADS, STRETCH, BLOCK), F32)],
        in_specs=[SMEM(), SMEM(), VMEM(), VMEM(), VMEM(), VMEM()],
        out_specs=[VMEM(), VMEM()],
        compiler_params=PARAMS,
        cost_estimate=cost(3),
        name="band",
    )(meta, slash_offsets, q, k, before, after)

    k_pieces, v_pieces = gather_columns(*sides, payload, [mask])

    columns, top = pl.pallas_call(
        top_kernel,
        out_shape=[shape((LISTED, BLOCK, HEAD), BF16), shape((2, HEADS, STRETCH, BLOCK), F32)],
        in_specs=[SMEM(), SMEM(), SMEM(), VMEM(), VMEM()] + [ANY()] * len(k_pieces),
        out_specs=[VMEM(), VMEM()],
        scratch_shapes=[pltpu.SemaphoreType.DMA((LISTED // GROUP,))],
        compiler_params=PARAMS,
        cost_estimate=cost(9),
        name="top",
    )(meta, blk, at, q, top, *k_pieces)

    mixed = column_vals = None
    for st in range(2):
        first = st == 0
        extra = [*v_pieces, *slabs] if first else [column_vals]
        result = pl.pallas_call(
            functools.partial(out_kernel, ctx_count, st, len(v_pieces) if first else 0),
            grid=(1,),
            out_shape=[shape((STRETCH, HEADS * HEAD), BF16)] + [shape((LISTED, BLOCK, HEAD), BF16)] * first,
            in_specs=[
                SMEM(), SMEM(), SMEM(),
                pl.BlockSpec((1, STRETCH, HEADS * HEAD), lambda i, st=st: (st, 0, 0)),
                VMEM(),
                pl.BlockSpec((1, HEADS, STRETCH, BLOCK), lambda i, st=st: (st, 0, 0, 0)),
                VMEM(), VMEM(), VMEM(), VMEM(), VMEM(),
            ] + ([ANY()] * len(extra) if first else [VMEM()]),
            out_specs=[VMEM()] * (1 + first),
            scratch_shapes=[
                pltpu.VMEM((HEADS, STRETCH, BLOCK), F32),
                pltpu.VMEM((HEADS, STRETCH, HEAD), F32),
            ] + [pltpu.SemaphoreType.DMA((LISTED // GROUP,))] * first,
            compiler_params=PARAMS,
            cost_estimate=cost(8),
            name=f"attend{st}",
        )(meta, blk, at, q, columns, top, mask, k, v, before, after, *extra)
        head_out = result[0]
        if first:
            column_vals = result[1]
        parts = [head_out] + [from_ahead(head_out, "tp", shift) for shift in range(1, tp)]
        tile = width // 4
        mixed = pl.pallas_call(
            mix_kernel,
            grid=(width // tile,),
            out_shape=shape((2, STRETCH, width), BF16),
            in_specs=[VMEM()] * 4
            + [pl.BlockSpec((HEADS * HEAD, tile), lambda i: (0, i))] * 4
            + ([ANY()] if st else []),
            out_specs=pl.BlockSpec((1, STRETCH, tile), lambda i, st=st: (st, 0, i)),
            input_output_aliases={8: 0} if st else {},
            compiler_params=PARAMS,
            cost_estimate=cost(3),
            name=f"mix{st}",
        )(*parts, *slabs, *([mixed] if st else []))
    return mixed[None]


def solution(mesh):
    in_specs = (
        P("ctx", None, None, "tp"),
        P("ctx", None, None, "tp"),
        P("ctx", None, None, "tp"),
        P("tp", None),
        P("tp", None),
        P("tp", None),
    )
    out_specs = P("ctx", None, None, "tp")
    return jax.shard_map(
        per_device, mesh=mesh, in_specs=in_specs, out_specs=out_specs, check_vma=False
    )
```

```python
import functools
import math

import jax
import jax.numpy as jnp
from jax import lax
from jax.experimental import pallas as pl
from jax.experimental.pallas import tpu as pltpu
from jax.sharding import PartitionSpec as P

HEAD = 128
BLOCK = 128
STRETCH = 256
CAP = 2
GROUP = 8
SPAN = GROUP * BLOCK
LISTED = 64
ROOM = LISTED + 1
UNROLL = 4
X_CHIPS = 4
HEADS = 4
EXP_SCALE = math.log2(math.e) * HEAD ** (-0.5)
VMEM_LIMIT = 48 * 1024 * 1024

SMEM = functools.partial(pl.BlockSpec, memory_space=pltpu.SMEM)
VMEM = functools.partial(pl.BlockSpec, memory_space=pltpu.VMEM)
ANY = functools.partial(pl.BlockSpec, memory_space=pl.ANY)
PARAMS = pltpu.CompilerParams(vmem_limit_bytes=VMEM_LIMIT)
F32 = jnp.float32
BF16 = jnp.bfloat16


def dot_t(a, b):
    return lax.dot_general(a, b, (((1,), (1,)), ((), ())), preferred_element_type=F32)


def pack_kernel(ctx_count, me_ref, table_ref, k_ref, v_ref, pay_ref, ahead_ref, back_ref):
    me = me_ref[0]
    table = table_ref[...]
    owner = owned(table, ctx_count)
    local = jnp.where(table // 2 < ctx_count, 0, 2) + table % 2
    at = lax.broadcasted_iota(jnp.int32, table.shape, 1)
    mine = owner == me
    for slot in range(CAP):
        found = jnp.min(jnp.where(mine, at, LISTED))
        loc = jnp.sum(jnp.where(at == found, local, 0))
        mine = mine & (at > found)
        pay_ref[0, slot] = k_ref[loc]
        pay_ref[1, slot] = v_ref[loc]
    for half, ref in ((0, ahead_ref), (1, back_ref)):
        for part in range(2):
            ref[0, part * BLOCK : (part + 1) * BLOCK] = k_ref[2 * half + part]
            ref[1, part * BLOCK : (part + 1) * BLOCK] = v_ref[2 * half + part]


def owned(table, ctx_count):
    stretch = table // 2
    return jnp.where(stretch < ctx_count, stretch, 2 * ctx_count - 1 - stretch)


def plan_kernel(ctx_count, sides, me_ref, row_ref, col_ref, blk_ref, at_ref, meta_ref):
    me = me_ref[0]
    row, col = row_ref[...], col_ref[...]
    square = (LISTED, LISTED)
    iota = lax.broadcasted_iota
    total = functools.partial(jnp.sum, keepdims=True)
    pick = lambda test, value, axis: total(jnp.where(test, value, 0), axis=axis)
    place = pick(row < col, jnp.int32(1), 1)
    earlier = iota(jnp.int32, square, 1) < iota(jnp.int32, square, 0)
    owner = owned(col, ctx_count)
    rank = pick((owned(row, ctx_count) == owner) & earlier, jnp.int32(1), 1)
    blk_ref[...] = pick(place == iota(jnp.int32, square, 1), col, 0)
    entry = arrivals(*sides, me, iota(jnp.int32, (1, CAP * ctx_count), 1))
    at_ref[...] = LISTED + pick(owner * CAP + rank == entry, place - LISTED, 0)
    lane = iota(jnp.int32, (1, 16), 1)
    meta = jnp.where(lane % 8 == 3, me, 0)
    for st, s in enumerate((me, 2 * ctx_count - 1 - me)):
        found = [jnp.sum(jnp.where(row < 2 * s, 1, 0)), jnp.sum(jnp.where(row <= 2 * s + 1, 1, 0)), s]
        for n, value in enumerate(found):
            meta = jnp.where(lane == 8 * st + n, value, meta)
        for n in range(4):
            b = 2 * (s - 1) + n
            free = 1 - jnp.max(jnp.where(row == b, 1, 0))
            meta = jnp.where(lane == 8 * st + 4 + n, jnp.where(b >= 0, free, 0), meta)
    meta_ref[...] = meta


def band_halves(own_ref, ahead_ref, back_ref, which, st, me, ctx_count):
    if st == 0:
        return ahead_ref[which]
    return jnp.where(me == ctx_count - 1, own_ref[0], back_ref[which])


def band_kernel(ctx_count, meta_ref, slash_ref, q_ref, k_ref, ahead_ref, back_ref, mask_ref, top_ref):
    behind = STRETCH - lax.broadcasted_iota(jnp.int32, (8, 2 * STRETCH), 1)
    for h in range(HEADS):
        def listed(n, hit):
            return hit | (behind == slash_ref[h, n])

        hit = behind == 0
        for n in range(LISTED):
            hit = listed(n, hit)
        row = jnp.where(hit, 1.0, 0.0).astype(F32)[:1]
        spread = jnp.broadcast_to(row, (STRETCH, 2 * STRETCH))
        mask_ref[h] = pltpu.roll(spread, 0, 1, stride=1, stride_axis=0)
    me = meta_ref[0, 3]
    for st in range(2):
        before = band_halves(k_ref, ahead_ref, back_ref, 0, st, me, ctx_count)
        for h in range(HEADS):
            q = q_ref[st, :, h * HEAD : (h + 1) * HEAD]
            top = jnp.full((STRETCH, BLOCK), -jnp.inf, F32)
            for n in range(4):
                part = before if n < 2 else k_ref[st]
                s = dot_t(q, part[(n % 2) * BLOCK : (n % 2 + 1) * BLOCK])
                ok = (mask_ref[h, :, n * BLOCK : (n + 1) * BLOCK] > 0.5) & (meta_ref[0, 8 * st + 4 + n] > 0)
                top = jnp.maximum(top, jnp.where(ok, s, -jnp.inf))
            top_ref[st, h] = top


def fetch(at_ref, pieces, target_ref):
    base = 0
    for ref in pieces:
        def copy(i, _, ref=ref, base=base):
            for n in range(UNROLL):
                target_ref[at_ref[0, base + i * UNROLL + n]] = ref[i * UNROLL + n]
            return 0

        lax.fori_loop(0, ref.shape[0] // UNROLL, copy, 0)
        base += ref.shape[0]


def causal(blk_ref, s, g):
    lead = lax.broadcasted_iota(jnp.int32, (STRETCH, BLOCK), 1) - lax.broadcasted_iota(jnp.int32, (STRETCH, BLOCK), 0)
    return [lead <= s * STRETCH - blk_ref[0, g * GROUP + n] * BLOCK for n in range(GROUP)]


def top_kernel(meta_ref, blk_ref, at_ref, q_ref, top_in_ref, *refs):
    pieces, (keys_ref, top_ref) = refs[:-2], refs[-2:]
    fetch(at_ref, pieces, keys_ref)
    for st in range(2):
        full, seen, s = meta_ref[0, 8 * st], meta_ref[0, 8 * st + 1], meta_ref[0, 8 * st + 2]
        plain, groups = full // GROUP, (seen + GROUP - 1) // GROUP
        for h in range(HEADS):
            top_ref[st, h] = top_in_ref[st, h]

        def step(masked, g, _):
            keys = keys_ref[pl.ds(g * GROUP, GROUP)].reshape(SPAN, HEAD)
            ok = causal(blk_ref, s, g) if masked else None
            for h in range(HEADS):
                scores = dot_t(q_ref[st, :, h * HEAD : (h + 1) * HEAD], keys)
                tops = []
                for n in range(GROUP):
                    part = scores[:, n * BLOCK : (n + 1) * BLOCK]
                    tops.append(jnp.where(ok[n], part, -jnp.inf) if masked else part)
                top = functools.reduce(jnp.maximum, tops)
                top_ref[st, h] = jnp.maximum(top_ref[st, h], top)
            return 0

        lax.fori_loop(0, plain, functools.partial(step, False), 0)
        lax.fori_loop(plain, groups, functools.partial(step, True), 0)
        for h in range(HEADS):
            row = jnp.max(top_ref[st, h], axis=1, keepdims=True)
            top_ref[st, h] = jnp.broadcast_to(row, (STRETCH, BLOCK))


def out_kernel(ctx_count, st, arriving, meta_ref, blk_ref, at_ref, q_ref, keys_ref, top_ref, mask_ref, k_ref, v_ref, ahead_ref, back_ref, *refs):
    full, seen, s = meta_ref[0, 8 * st], meta_ref[0, 8 * st + 1], meta_ref[0, 8 * st + 2]
    me = meta_ref[0, 8 * st + 3]
    plain, groups = full // GROUP, (seen + GROUP - 1) // GROUP
    if arriving:
        pieces, (out_ref, vals, total, acc) = refs[:arriving], refs[-4:]
        fetch(at_ref, pieces, vals)
    else:
        vals, out_ref, total, acc = refs
    k_before = band_halves(k_ref, ahead_ref, back_ref, 0, st, me, ctx_count)
    v_before = band_halves(v_ref, ahead_ref, back_ref, 1, st, me, ctx_count)

    for h in range(HEADS):
        q = q_ref[0, :, h * HEAD : (h + 1) * HEAD]
        scores = [dot_t(q, k_before), dot_t(q, k_ref[st])]
        expos = []
        for n in range(4):
            part = scores[n // 2][:, (n % 2) * BLOCK : (n % 2 + 1) * BLOCK]
            ok = (mask_ref[h, :, n * BLOCK : (n + 1) * BLOCK] > 0.5) & (meta_ref[0, 8 * st + 4 + n] > 0)
            expos.append(jnp.where(ok, jnp.exp2((part - top_ref[0, h]) * EXP_SCALE), 0.0))
        total[h] = (expos[0] + expos[1]) + (expos[2] + expos[3])
        weights = [e.astype(BF16) for e in expos]
        acc[h] = jnp.dot(
            jnp.concatenate(weights[:2], axis=1), v_before, preferred_element_type=F32
        ) + jnp.dot(jnp.concatenate(weights[2:], axis=1), v_ref[st], preferred_element_type=F32)

    def step(masked, g, _):
        keys = keys_ref[pl.ds(g * GROUP, GROUP)].reshape(SPAN, HEAD)
        values = vals[pl.ds(g * GROUP, GROUP)].reshape(SPAN, HEAD)
        ok = causal(blk_ref, s, g) if masked else None
        for h in range(HEADS):
            scores = dot_t(q_ref[0, :, h * HEAD : (h + 1) * HEAD], keys)
            expos = []
            for n in range(GROUP):
                part = jnp.exp2((scores[:, n * BLOCK : (n + 1) * BLOCK] - top_ref[0, h]) * EXP_SCALE)
                expos.append(jnp.where(ok[n], part, 0.0) if masked else part)
            total[h] += functools.reduce(jnp.add, expos)
            weights = jnp.concatenate([e.astype(BF16) for e in expos], axis=1)
            acc[h] += jnp.dot(weights, values, preferred_element_type=F32)
        return 0

    lax.fori_loop(0, plain, functools.partial(step, False), 0)
    lax.fori_loop(plain, groups, functools.partial(step, True), 0)
    for h in range(HEADS):
        row = jnp.sum(total[h], axis=1, keepdims=True)
        out_ref[:, h * HEAD : (h + 1) * HEAD] = (acc[h] / row).astype(BF16)


def mix_kernel(a0, a1, a2, a3, w0, w1, w2, w3, *refs):
    out_ref = refs[-1]
    sums = [jnp.dot(a[...], w[...], preferred_element_type=F32) for a, w in ((a0, w0), (a1, w1), (a2, w2), (a3, w3))]
    out_ref[0] = ((sums[0] + sums[1]) + (sums[2] + sums[3])).astype(BF16)


def from_ahead(x, axis, shift):
    n = lax.axis_size(axis)
    return lax.ppermute(x, axis, [((i + shift) % n, i) for i in range(n)])


def line_kernel(*refs):
    pieces, out_ref = refs[:X_CHIPS], refs[-1]
    for n, ref in enumerate(pieces):
        for which in range(2):
            out_ref[which, n * CAP : (n + 1) * CAP] = ref[which]


def chip_kernel(which, own_ref, other_ref, *refs):
    count = own_ref.shape[1]
    refs[-1][:count] = own_ref[which]
    refs[-1][count:] = other_ref[which]


def gather_columns(nx, nz, payload, first, later):
    place = lambda x, z, c: ((x % nx) * nz + z % nz) * 2 + c
    every = [(x, z, c) for x in range(nx) for z in range(nz) for c in range(2)]
    route = lambda f: [(place(*d), place(*f(*d))) for d in every]
    across = route(lambda x, z, c: (x, z, 1 - c))
    along = route(lambda x, z, c: (x, z + 1 - 2 * c, c))
    send = lambda a, r: lax.ppermute(a, "ctx", r)

    shape = jax.ShapeDtypeStruct
    call = functools.partial(pl.pallas_call, compiler_params=PARAMS)
    size = nx * CAP
    line = [payload] + [send(payload, route(lambda x, z, c, n=n: (x - n, z, c))) for n in range(1, nx)]
    own = call(
        line_kernel,
        out_shape=shape((2, size, BLOCK, HEAD), BF16),
        in_specs=[VMEM()] * nx + [ANY()] * len(first),
        out_specs=VMEM(),
        name="line",
    )(*line, *first)
    other = send(own, across)
    pieces = []
    waited = []
    for which in range(2):
        moving = call(
            functools.partial(chip_kernel, which),
            out_shape=shape((2 * size, BLOCK, HEAD), BF16),
            in_specs=[VMEM()] * 2 + [ANY()] * len(waited),
            out_specs=VMEM(),
            name=f"chip{which}",
        )(own, other, *waited)
        held = [moving]
        for n in range(1, nz // 2 + 1):
            moving = send(moving, along)
            held += [moving] + ([send(moving, across)] if n < nz // 2 else [])
            if n == 1:
                waited = [moving, *later]
        pieces.append(held)
    return pieces


def arrivals(nx, nz, me, entry):
    x, z, c = lax.div(me, 2 * nz), lax.rem(lax.div(me, 2), nz), lax.rem(me, 2)
    size = nx * CAP
    at = entry % (2 * size)
    piece = entry // (2 * size)
    hops = jnp.where(piece == 0, 0, (piece + 1) // 2)
    mirrored = jnp.where(piece == 0, 0, (piece + 1) % 2)
    half = at // size
    side = jnp.where(mirrored == 1, 1 - 2 * c, 2 * c - 1) * hops
    core = jnp.where(mirrored == half, c, 1 - c)
    line = at % size // CAP
    return (((x + line) % nx * nz + (z + nz + side) % nz) * 2 + core) * CAP + at % CAP


def cost(us):
    return pl.CostEstimate(flops=0, bytes_accessed=int(us * 3.0e6), transcendentals=0)


def per_device(queries, keys, values, column_block_table, slash_offsets, out_weight):
    ctx_count = lax.axis_size("ctx")
    tp = lax.axis_size("tp")
    me = lax.axis_index("ctx").reshape(1).astype(jnp.int32)
    tp_index = lax.axis_index("tp")
    q, k, v = queries[0], keys[0], values[0]
    shape = jax.ShapeDtypeStruct
    i32 = jnp.int32

    payload, ahead, back = pl.pallas_call(
        functools.partial(pack_kernel, ctx_count),
        out_shape=[shape((2, CAP, BLOCK, HEAD), BF16)] + [shape((2, STRETCH, HEAD), BF16)] * 2,
        in_specs=[SMEM(), VMEM(), VMEM(), VMEM()],
        out_specs=[VMEM()] * 3,
        compiler_params=PARAMS,
        name="pack",
    )(me, column_block_table, k.reshape(4, BLOCK, HEAD), v.reshape(4, BLOCK, HEAD))

    sides = (X_CHIPS, ctx_count // (2 * X_CHIPS))
    blk, at, meta = pl.pallas_call(
        functools.partial(plan_kernel, ctx_count, sides),
        out_shape=[shape((1, LISTED), i32), shape((1, CAP * ctx_count), i32), shape((1, 16), i32)],
        in_specs=[SMEM(), VMEM(), VMEM()],
        out_specs=[VMEM()] * 3,
        compiler_params=PARAMS,
        cost_estimate=cost(2),
        name="plan",
    )(me, column_block_table, column_block_table.reshape(LISTED, 1))

    steps = range(ctx_count - 1)
    before = lax.ppermute(ahead, "ctx", [(i, i + 1) for i in steps])
    after = lax.ppermute(back, "ctx", [(i + 1, i) for i in steps])

    width = out_weight.shape[1] // tp
    slabs = []
    for shift in range(tp):
        target = lax.rem(tp_index + tp - shift, tp)
        slab = lax.dynamic_slice(out_weight, (0, target * width), (out_weight.shape[0], width))
        slabs.append(slab if shift == 0 else from_ahead(slab, "tp", shift))

    mask, top = pl.pallas_call(
        functools.partial(band_kernel, ctx_count),
        out_shape=[shape((HEADS, STRETCH, 2 * STRETCH), F32), shape((2, HEADS, STRETCH, BLOCK), F32)],
        in_specs=[SMEM(), SMEM(), VMEM(), VMEM(), VMEM(), VMEM()],
        out_specs=[VMEM(), VMEM()],
        compiler_params=PARAMS,
        cost_estimate=cost(3),
        name="band",
    )(meta, slash_offsets, q, k, before, after)

    k_pieces, v_pieces = gather_columns(*sides, payload, [before, after], [mask])

    columns, top = pl.pallas_call(
        top_kernel,
        out_shape=[shape((ROOM, BLOCK, HEAD), BF16), shape((2, HEADS, STRETCH, BLOCK), F32)],
        in_specs=[SMEM(), SMEM(), SMEM(), VMEM(), VMEM()] + [VMEM()] * len(k_pieces),
        out_specs=[VMEM(), VMEM()],
        compiler_params=PARAMS,
        cost_estimate=cost(9),
        name="top",
    )(meta, blk, at, q, top, *k_pieces)

    mixed = column_vals = None
    for st in range(2):
        first = st == 0
        extra = [*v_pieces, *slabs] if first else [column_vals]
        result = pl.pallas_call(
            functools.partial(out_kernel, ctx_count, st, len(v_pieces) if first else 0),
            grid=(1,),
            out_shape=[shape((STRETCH, HEADS * HEAD), BF16)] + [shape((ROOM, BLOCK, HEAD), BF16)] * first,
            in_specs=[
                SMEM(), SMEM(), SMEM(),
                pl.BlockSpec((1, STRETCH, HEADS * HEAD), lambda i, st=st: (st, 0, 0)),
                VMEM(),
                pl.BlockSpec((1, HEADS, STRETCH, BLOCK), lambda i, st=st: (st, 0, 0, 0)),
                VMEM(), VMEM(), VMEM(), VMEM(), VMEM(),
            ] + ([VMEM()] * len(v_pieces) + [ANY()] * tp if first else [VMEM()]),
            out_specs=[VMEM()] * (1 + first),
            scratch_shapes=[
                pltpu.VMEM((HEADS, STRETCH, BLOCK), F32),
                pltpu.VMEM((HEADS, STRETCH, HEAD), F32),
            ],
            compiler_params=PARAMS,
            cost_estimate=cost(8),
            name=f"attend{st}",
        )(meta, blk, at, q, columns, top, mask, k, v, before, after, *extra)
        head_out = result[0]
        if first:
            column_vals = result[1]
        parts = [head_out] + [from_ahead(head_out, "tp", shift) for shift in range(1, tp)]
        tile = width // 4
        mixed = pl.pallas_call(
            mix_kernel,
            grid=(width // tile,),
            out_shape=shape((2, STRETCH, width), BF16),
            in_specs=[VMEM()] * 4
            + [pl.BlockSpec((HEADS * HEAD, tile), lambda i: (0, i))] * 4
            + ([ANY()] if st else []),
            out_specs=pl.BlockSpec((1, STRETCH, tile), lambda i, st=st: (st, 0, i)),
            input_output_aliases={8: 0} if st else {},
            compiler_params=PARAMS,
            cost_estimate=cost(3),
            name=f"mix{st}",
        )(*parts, *slabs, *([mixed] if st else []))
    return mixed[None]


def solution(mesh):
    in_specs = (
        P("ctx", None, None, "tp"),
        P("ctx", None, None, "tp"),
        P("ctx", None, None, "tp"),
        P("tp", None),
        P("tp", None),
        P("tp", None),
    )
    out_specs = P("ctx", None, None, "tp")
    return jax.shard_map(
        per_device, mesh=mesh, in_specs=in_specs, out_specs=out_specs, check_vma=False
    )
```

```python
import functools
import math

import jax
import jax.numpy as jnp
from jax import lax
from jax.experimental import pallas as pl
from jax.experimental.pallas import tpu as pltpu
from jax.sharding import PartitionSpec as P

HEAD = 128
BLOCK = 128
STRETCH = 256
CAP = 2
GROUP = 8
SPAN = GROUP * BLOCK
LISTED = 64
ROOM = LISTED + 1
UNROLL = 4
X_CHIPS = 4
HEADS = 4
EXP_SCALE = math.log2(math.e) * HEAD ** (-0.5)
VMEM_LIMIT = 48 * 1024 * 1024

SMEM = functools.partial(pl.BlockSpec, memory_space=pltpu.SMEM)
VMEM = functools.partial(pl.BlockSpec, memory_space=pltpu.VMEM)
ANY = functools.partial(pl.BlockSpec, memory_space=pl.ANY)
PARAMS = pltpu.CompilerParams(vmem_limit_bytes=VMEM_LIMIT)
F32 = jnp.float32
BF16 = jnp.bfloat16


def dot_t(a, b):
    return lax.dot_general(a, b, (((1,), (1,)), ((), ())), preferred_element_type=F32)


def pack_kernel(ctx_count, me_ref, table_ref, k_ref, v_ref, keys_ref, vals_ref, ahead_ref, back_ref):
    me = me_ref[0]
    table = table_ref[...]
    owner = owned(table, ctx_count)
    local = jnp.where(table // 2 < ctx_count, 0, 2) + table % 2
    at = lax.broadcasted_iota(jnp.int32, table.shape, 1)
    mine = owner == me
    for slot in range(CAP):
        found = jnp.min(jnp.where(mine, at, LISTED))
        loc = jnp.sum(jnp.where(at == found, local, 0))
        mine = mine & (at > found)
        keys_ref[slot] = k_ref[loc]
        vals_ref[slot] = v_ref[loc]
    for half, ref in ((0, ahead_ref), (1, back_ref)):
        for part in range(2):
            ref[0, part * BLOCK : (part + 1) * BLOCK] = k_ref[2 * half + part]
            ref[1, part * BLOCK : (part + 1) * BLOCK] = v_ref[2 * half + part]


def owned(table, ctx_count):
    stretch = table // 2
    return jnp.where(stretch < ctx_count, stretch, 2 * ctx_count - 1 - stretch)


def plan_kernel(ctx_count, sides, me_ref, row_ref, col_ref, blk_ref, key_at_ref, val_at_ref, meta_ref):
    me = me_ref[0]
    row, col = row_ref[...], col_ref[...]
    square = (LISTED, LISTED)
    iota = lax.broadcasted_iota
    total = functools.partial(jnp.sum, keepdims=True)
    pick = lambda test, value, axis: total(jnp.where(test, value, 0), axis=axis)
    place = pick(row < col, jnp.int32(1), 1)
    earlier = iota(jnp.int32, square, 1) < iota(jnp.int32, square, 0)
    owner = owned(col, ctx_count)
    rank = pick((owned(row, ctx_count) == owner) & earlier, jnp.int32(1), 1)
    blk_ref[...] = pick(place == iota(jnp.int32, square, 1), col, 0)
    entry = iota(jnp.int32, (1, CAP * ctx_count), 1)
    for origin, ref in ((key_origin, key_at_ref), (val_origin, val_at_ref)):
        ref[...] = LISTED + pick(owner * CAP + rank == origin(*sides, me, entry), place - LISTED, 0)
    lane = iota(jnp.int32, (1, 16), 1)
    meta = jnp.where(lane % 8 == 3, me, 0)
    for st, s in enumerate((me, 2 * ctx_count - 1 - me)):
        found = [jnp.sum(jnp.where(row < 2 * s, 1, 0)), jnp.sum(jnp.where(row <= 2 * s + 1, 1, 0)), s]
        for n, value in enumerate(found):
            meta = jnp.where(lane == 8 * st + n, value, meta)
        for n in range(4):
            b = 2 * (s - 1) + n
            free = 1 - jnp.max(jnp.where(row == b, 1, 0))
            meta = jnp.where(lane == 8 * st + 4 + n, jnp.where(b >= 0, free, 0), meta)
    meta_ref[...] = meta


def band_halves(own_ref, ahead_ref, back_ref, which, st, me, ctx_count):
    if st == 0:
        return ahead_ref[which]
    return jnp.where(me == ctx_count - 1, own_ref[0], back_ref[which])


def band_kernel(ctx_count, meta_ref, slash_ref, q_ref, k_ref, ahead_ref, back_ref, mask_ref, top_ref):
    behind = STRETCH - lax.broadcasted_iota(jnp.int32, (8, 2 * STRETCH), 1)
    for h in range(HEADS):
        def listed(n, hit):
            return hit | (behind == slash_ref[h, n])

        hit = behind == 0
        for n in range(LISTED):
            hit = listed(n, hit)
        row = jnp.where(hit, 1.0, 0.0).astype(F32)[:1]
        spread = jnp.broadcast_to(row, (STRETCH, 2 * STRETCH))
        mask_ref[h] = pltpu.roll(spread, 0, 1, stride=1, stride_axis=0)
    me = meta_ref[0, 3]
    for st in range(2):
        before = band_halves(k_ref, ahead_ref, back_ref, 0, st, me, ctx_count)
        for h in range(HEADS):
            q = q_ref[st, :, h * HEAD : (h + 1) * HEAD]
            top = jnp.full((STRETCH, BLOCK), -jnp.inf, F32)
            for n in range(4):
                part = before if n < 2 else k_ref[st]
                s = dot_t(q, part[(n % 2) * BLOCK : (n % 2 + 1) * BLOCK])
                ok = (mask_ref[h, :, n * BLOCK : (n + 1) * BLOCK] > 0.5) & (meta_ref[0, 8 * st + 4 + n] > 0)
                top = jnp.maximum(top, jnp.where(ok, s, -jnp.inf))
            top_ref[st, h] = top


def fetch(at_ref, pieces, target_ref):
    base = 0
    for ref in pieces:
        def copy(i, _, ref=ref, base=base):
            for n in range(UNROLL):
                target_ref[at_ref[0, base + i * UNROLL + n]] = ref[i * UNROLL + n]
            return 0

        lax.fori_loop(0, ref.shape[0] // UNROLL, copy, 0)
        base += ref.shape[0]


def causal(blk_ref, s, g):
    lead = lax.broadcasted_iota(jnp.int32, (STRETCH, BLOCK), 1) - lax.broadcasted_iota(jnp.int32, (STRETCH, BLOCK), 0)
    return [lead <= s * STRETCH - blk_ref[0, g * GROUP + n] * BLOCK for n in range(GROUP)]


def top_kernel(meta_ref, blk_ref, at_ref, q_ref, top_in_ref, *refs):
    pieces, (keys_ref, top_ref) = refs[:-2], refs[-2:]
    fetch(at_ref, pieces, keys_ref)
    for st in range(2):
        full, seen, s = meta_ref[0, 8 * st], meta_ref[0, 8 * st + 1], meta_ref[0, 8 * st + 2]
        plain, groups = full // GROUP, (seen + GROUP - 1) // GROUP
        for h in range(HEADS):
            top_ref[st, h] = top_in_ref[st, h]

        def step(masked, g, _):
            keys = keys_ref[pl.ds(g * GROUP, GROUP)].reshape(SPAN, HEAD)
            ok = causal(blk_ref, s, g) if masked else None
            for h in range(HEADS):
                scores = dot_t(q_ref[st, :, h * HEAD : (h + 1) * HEAD], keys)
                tops = []
                for n in range(GROUP):
                    part = scores[:, n * BLOCK : (n + 1) * BLOCK]
                    tops.append(jnp.where(ok[n], part, -jnp.inf) if masked else part)
                top = functools.reduce(jnp.maximum, tops)
                top_ref[st, h] = jnp.maximum(top_ref[st, h], top)
            return 0

        lax.fori_loop(0, plain, functools.partial(step, False), 0)
        lax.fori_loop(plain, groups, functools.partial(step, True), 0)
        for h in range(HEADS):
            row = jnp.max(top_ref[st, h], axis=1, keepdims=True)
            top_ref[st, h] = jnp.broadcast_to(row, (STRETCH, BLOCK))


def out_kernel(ctx_count, st, arriving, meta_ref, blk_ref, at_ref, q_ref, keys_ref, top_ref, mask_ref, k_ref, v_ref, ahead_ref, back_ref, *refs):
    full, seen, s = meta_ref[0, 8 * st], meta_ref[0, 8 * st + 1], meta_ref[0, 8 * st + 2]
    me = meta_ref[0, 8 * st + 3]
    plain, groups = full // GROUP, (seen + GROUP - 1) // GROUP
    if arriving:
        pieces, (out_ref, vals, total, acc) = refs[:arriving], refs[-4:]
        fetch(at_ref, pieces, vals)
    else:
        vals, out_ref, total, acc = refs
    k_before = band_halves(k_ref, ahead_ref, back_ref, 0, st, me, ctx_count)
    v_before = band_halves(v_ref, ahead_ref, back_ref, 1, st, me, ctx_count)

    for h in range(HEADS):
        q = q_ref[0, :, h * HEAD : (h + 1) * HEAD]
        scores = [dot_t(q, k_before), dot_t(q, k_ref[st])]
        expos = []
        for n in range(4):
            part = scores[n // 2][:, (n % 2) * BLOCK : (n % 2 + 1) * BLOCK]
            ok = (mask_ref[h, :, n * BLOCK : (n + 1) * BLOCK] > 0.5) & (meta_ref[0, 8 * st + 4 + n] > 0)
            expos.append(jnp.where(ok, jnp.exp2((part - top_ref[0, h]) * EXP_SCALE), 0.0))
        total[h] = (expos[0] + expos[1]) + (expos[2] + expos[3])
        weights = [e.astype(BF16) for e in expos]
        acc[h] = jnp.dot(
            jnp.concatenate(weights[:2], axis=1), v_before, preferred_element_type=F32
        ) + jnp.dot(jnp.concatenate(weights[2:], axis=1), v_ref[st], preferred_element_type=F32)

    def step(masked, g, _):
        keys = keys_ref[pl.ds(g * GROUP, GROUP)].reshape(SPAN, HEAD)
        values = vals[pl.ds(g * GROUP, GROUP)].reshape(SPAN, HEAD)
        ok = causal(blk_ref, s, g) if masked else None
        for h in range(HEADS):
            scores = dot_t(q_ref[0, :, h * HEAD : (h + 1) * HEAD], keys)
            expos = []
            for n in range(GROUP):
                part = jnp.exp2((scores[:, n * BLOCK : (n + 1) * BLOCK] - top_ref[0, h]) * EXP_SCALE)
                expos.append(jnp.where(ok[n], part, 0.0) if masked else part)
            total[h] += functools.reduce(jnp.add, expos)
            weights = jnp.concatenate([e.astype(BF16) for e in expos], axis=1)
            acc[h] += jnp.dot(weights, values, preferred_element_type=F32)
        return 0

    lax.fori_loop(0, plain, functools.partial(step, False), 0)
    lax.fori_loop(plain, groups, functools.partial(step, True), 0)
    for h in range(HEADS):
        row = jnp.sum(total[h], axis=1, keepdims=True)
        out_ref[:, h * HEAD : (h + 1) * HEAD] = (acc[h] / row).astype(BF16)


def mix_kernel(a0, a1, a2, a3, w0, w1, w2, w3, *refs):
    out_ref = refs[-1]
    sums = [jnp.dot(a[...], w[...], preferred_element_type=F32) for a, w in ((a0, w0), (a1, w1), (a2, w2), (a3, w3))]
    out_ref[0] = ((sums[0] + sums[1]) + (sums[2] + sums[3])).astype(BF16)


def from_ahead(x, axis, shift):
    n = lax.axis_size(axis)
    return lax.ppermute(x, axis, [((i + shift) % n, i) for i in range(n)])


def join_kernel(count, *refs):
    out_ref = refs[-1]
    base = 0
    for ref in refs[:count]:
        size = ref.shape[0]
        out_ref[base : base + size] = ref[...]
        base += size


def line_kernel(count, *refs):
    pieces, (mine_ref, other_ref) = refs[:count], refs[-2:]
    for n, ref in enumerate(pieces):
        swapped = count // 2 <= n < count - 1
        for half, out in ((0, other_ref if swapped else mine_ref), (1, mine_ref if swapped else other_ref)):
            out[n * CAP : (n + 1) * CAP] = ref[half * CAP : (half + 1) * CAP]


def gather_columns(nx, nz, keys, vals, later):
    place = lambda x, z, c: ((x % nx) * nz + z % nz) * 2 + c
    every = [(x, z, c) for x in range(nx) for z in range(nz) for c in range(2)]
    route = lambda f: [(place(*d), place(*f(*d))) for d in every]
    across = route(lambda x, z, c: (x, z, 1 - c))
    along_x = route(lambda x, z, c: (x + 1 - 2 * c, z, c))
    along_z = route(lambda x, z, c: (x, z + 1 - 2 * c, c))
    send = lambda a, r: lax.ppermute(a, "ctx", r)

    def call(kernel, name, sizes, operands, extra=()):
        return pl.pallas_call(
            kernel,
            out_shape=[jax.ShapeDtypeStruct((size, BLOCK, HEAD), BF16) for size in sizes],
            in_specs=[VMEM()] * len(operands) + [ANY()] * len(extra),
            out_specs=[VMEM()] * len(sizes),
            compiler_params=PARAMS,
            name=name,
        )(*operands, *extra)

    join = lambda name, operands, extra=(): call(
        functools.partial(join_kernel, len(operands)), name, [sum(o.shape[0] for o in operands)], operands, extra
    )[0]

    def ring(held, moving, before):
        own, swapped = [], []
        for n in range(1, nz // 2):
            if n in before:
                moving = join(f"after{n}", [moving], before[n])
            if n > 1:
                moving = send(moving, along_z)
            own.append(moving)
            swapped.append(send(moving, across))
        return [held], own, swapped, send(moving, along_z)

    line = [keys] + [send(keys, route(lambda x, z, c, n=n: (x - n, z, c))) for n in range(1, nx)]
    chip_v = join("chip_vals", [vals, send(vals, across)])
    line = join("line_keys", line, [chip_v])
    first_v = send(chip_v, along_z)
    chip_k = join("chip_keys", [line, send(line, across)], [first_v])
    held, k_own, swapped, opposite = ring(chip_k, send(chip_k, along_z), {})
    k_pieces = held + [p for pair in zip(k_own, swapped) for p in pair] + [opposite]

    held, own, swapped, opposite = ring(chip_v, first_v, {nz // 2 - 1: k_own[:1]})
    pieces = held + own + swapped + [opposite]
    mine, other = call(
        functools.partial(line_kernel, nz), "line_vals", [nz * CAP] * 2, pieces, [*later, k_own[1]]
    )
    mine_1, other_1 = send(mine, along_x), send(other, along_x)
    mine_2 = send(mine_1, along_x)
    v_pieces = [mine, other, mine_1, other_1, send(mine_1, across), send(other_1, across), mine_2, send(mine_2, across)]
    return k_pieces, v_pieces


def key_origin(nx, nz, me, entry):
    x, z, c = lax.div(me, 2 * nz), lax.rem(lax.div(me, 2), nz), lax.rem(me, 2)
    size = nx * CAP
    at = entry % (2 * size)
    piece = entry // (2 * size)
    hops = jnp.where(piece == 0, 0, (piece + 1) // 2)
    mirrored = jnp.where(piece == 0, 0, (piece + 1) % 2)
    half = at // size
    side = jnp.where(mirrored == 1, 1 - 2 * c, 2 * c - 1) * hops
    core = jnp.where(mirrored == half, c, 1 - c)
    line = at % size // CAP
    return (((x + line) % nx * nz + (z + nz + side) % nz) * 2 + core) * CAP + at % CAP


def val_origin(nx, nz, me, entry):
    x, z, c = lax.div(me, 2 * nz), lax.rem(lax.div(me, 2), nz), lax.rem(me, 2)
    size = nz * CAP
    at = entry % size
    piece = entry // size
    hops = mirrored = half = jnp.zeros_like(entry)
    for n, (h, m, f) in enumerate(((0, 0, 0), (0, 0, 1), (1, 0, 0), (1, 0, 1), (1, 1, 0), (1, 1, 1), (2, 0, 0), (2, 1, 0))):
        hops, mirrored, half = (jnp.where(piece == n, a, b) for a, b in ((h, hops), (m, mirrored), (f, half)))
    via = jnp.where(mirrored == 1, 1 - c, c)
    sign = 2 * via - 1
    core = jnp.where(half == 1, 1 - via, via)
    n = at // CAP
    far = nz // 2
    round_z = jnp.where(n < far, n * sign, jnp.where(n < nz - 1, (far - 1 - n) * sign, far))
    return (((x + nx + hops * sign) % nx * nz + (z + nz + round_z) % nz) * 2 + core) * CAP + at % CAP


def cost(us):
    return pl.CostEstimate(flops=0, bytes_accessed=int(us * 3.0e6), transcendentals=0)


def per_device(queries, keys, values, column_block_table, slash_offsets, out_weight):
    ctx_count = lax.axis_size("ctx")
    tp = lax.axis_size("tp")
    me = lax.axis_index("ctx").reshape(1).astype(jnp.int32)
    tp_index = lax.axis_index("tp")
    q, k, v = queries[0], keys[0], values[0]
    shape = jax.ShapeDtypeStruct
    i32 = jnp.int32

    send_keys, send_vals, ahead, back = pl.pallas_call(
        functools.partial(pack_kernel, ctx_count),
        out_shape=[shape((CAP, BLOCK, HEAD), BF16)] * 2 + [shape((2, STRETCH, HEAD), BF16)] * 2,
        in_specs=[SMEM(), VMEM(), VMEM(), VMEM()],
        out_specs=[VMEM()] * 4,
        compiler_params=PARAMS,
        name="pack",
    )(me, column_block_table, k.reshape(4, BLOCK, HEAD), v.reshape(4, BLOCK, HEAD))

    sides = (X_CHIPS, ctx_count // (2 * X_CHIPS))
    blk, key_at, val_at, meta = pl.pallas_call(
        functools.partial(plan_kernel, ctx_count, sides),
        out_shape=[shape((1, LISTED), i32)] + [shape((1, CAP * ctx_count), i32)] * 2 + [shape((1, 16), i32)],
        in_specs=[SMEM(), VMEM(), VMEM()],
        out_specs=[VMEM()] * 4,
        compiler_params=PARAMS,
        cost_estimate=cost(2),
        name="plan",
    )(me, column_block_table, column_block_table.reshape(LISTED, 1))

    steps = range(ctx_count - 1)
    before = lax.ppermute(ahead, "ctx", [(i, i + 1) for i in steps])
    after = lax.ppermute(back, "ctx", [(i + 1, i) for i in steps])

    width = out_weight.shape[1] // tp
    slabs = []
    for shift in range(tp):
        target = lax.rem(tp_index + tp - shift, tp)
        slab = lax.dynamic_slice(out_weight, (0, target * width), (out_weight.shape[0], width))
        slabs.append(slab if shift == 0 else from_ahead(slab, "tp", shift))

    mask, top = pl.pallas_call(
        functools.partial(band_kernel, ctx_count),
        out_shape=[shape((HEADS, STRETCH, 2 * STRETCH), F32), shape((2, HEADS, STRETCH, BLOCK), F32)],
        in_specs=[SMEM(), SMEM(), VMEM(), VMEM(), VMEM(), VMEM()],
        out_specs=[VMEM(), VMEM()],
        compiler_params=PARAMS,
        cost_estimate=cost(3),
        name="band",
    )(meta, slash_offsets, q, k, before, after)

    k_pieces, v_pieces = gather_columns(*sides, send_keys, send_vals, [mask])

    columns, top = pl.pallas_call(
        top_kernel,
        out_shape=[shape((ROOM, BLOCK, HEAD), BF16), shape((2, HEADS, STRETCH, BLOCK), F32)],
        in_specs=[SMEM(), SMEM(), SMEM(), VMEM(), VMEM()] + [VMEM()] * len(k_pieces),
        out_specs=[VMEM(), VMEM()],
        compiler_params=PARAMS,
        cost_estimate=cost(9),
        name="top",
    )(meta, blk, key_at, q, top, *k_pieces)

    mixed = column_vals = None
    for st in range(2):
        first = st == 0
        extra = [*v_pieces, *slabs] if first else [column_vals]
        result = pl.pallas_call(
            functools.partial(out_kernel, ctx_count, st, len(v_pieces) if first else 0),
            grid=(1,),
            out_shape=[shape((STRETCH, HEADS * HEAD), BF16)] + [shape((ROOM, BLOCK, HEAD), BF16)] * first,
            in_specs=[
                SMEM(), SMEM(), SMEM(),
                pl.BlockSpec((1, STRETCH, HEADS * HEAD), lambda i, st=st: (st, 0, 0)),
                VMEM(),
                pl.BlockSpec((1, HEADS, STRETCH, BLOCK), lambda i, st=st: (st, 0, 0, 0)),
                VMEM(), VMEM(), VMEM(), VMEM(), VMEM(),
            ] + ([VMEM()] * len(v_pieces) + [ANY()] * tp if first else [VMEM()]),
            out_specs=[VMEM()] * (1 + first),
            scratch_shapes=[
                pltpu.VMEM((HEADS, STRETCH, BLOCK), F32),
                pltpu.VMEM((HEADS, STRETCH, HEAD), F32),
            ],
            compiler_params=PARAMS,
            cost_estimate=cost(8),
            name=f"attend{st}",
        )(meta, blk, val_at, q, columns, top, mask, k, v, before, after, *extra)
        head_out = result[0]
        if first:
            column_vals = result[1]
        parts = [head_out] + [from_ahead(head_out, "tp", shift) for shift in range(1, tp)]
        tile = width // 4
        mixed = pl.pallas_call(
            mix_kernel,
            grid=(width // tile,),
            out_shape=shape((2, STRETCH, width), BF16),
            in_specs=[VMEM()] * 4
            + [pl.BlockSpec((HEADS * HEAD, tile), lambda i: (0, i))] * 4
            + ([ANY()] if st else []),
            out_specs=pl.BlockSpec((1, STRETCH, tile), lambda i, st=st: (st, 0, i)),
            input_output_aliases={8: 0} if st else {},
            compiler_params=PARAMS,
            cost_estimate=cost(3),
            name=f"mix{st}",
        )(*parts, *slabs, *([mixed] if st else []))
    return mixed[None]


def solution(mesh):
    in_specs = (
        P("ctx", None, None, "tp"),
        P("ctx", None, None, "tp"),
        P("ctx", None, None, "tp"),
        P("tp", None),
        P("tp", None),
        P("tp", None),
    )
    out_specs = P("ctx", None, None, "tp")
    return jax.shard_map(
        per_device, mesh=mesh, in_specs=in_specs, out_specs=out_specs, check_vma=False
    )
```

```python
import functools
import math

import jax
import jax.numpy as jnp
from jax import lax
from jax.experimental import pallas as pl
from jax.experimental.pallas import tpu as pltpu
from jax.sharding import PartitionSpec as P

HEAD = 128
BLOCK = 128
STRETCH = 256
CAP = 2
GROUP = 8
SPAN = GROUP * BLOCK
LISTED = 64
ROOM = LISTED + 1
UNROLL = 4
X_CHIPS = 4
HEADS = 4
EXP_SCALE = math.log2(math.e) * HEAD ** (-0.5)
VMEM_LIMIT = 48 * 1024 * 1024

SMEM = functools.partial(pl.BlockSpec, memory_space=pltpu.SMEM)
VMEM = functools.partial(pl.BlockSpec, memory_space=pltpu.VMEM)
ANY = functools.partial(pl.BlockSpec, memory_space=pl.ANY)
PARAMS = pltpu.CompilerParams(vmem_limit_bytes=VMEM_LIMIT)
F32 = jnp.float32
BF16 = jnp.bfloat16


def dot_t(a, b):
    return lax.dot_general(a, b, (((1,), (1,)), ((), ())), preferred_element_type=F32)


def pack_kernel(ctx_count, me_ref, table_hbm, k_hbm, v_hbm, pay_ref, ahead_ref, back_ref, table_ref, k_ref, v_ref, sems):
    copies = [
        pltpu.make_async_copy(source, target, sems.at[n])
        for n, (source, target) in enumerate(((table_hbm, table_ref), (k_hbm, k_ref), (v_hbm, v_ref)))
    ]
    for copy in copies:
        copy.start()
    for copy in copies:
        copy.wait()
    me = me_ref[0]
    table = table_ref[...]
    owner = owned(table, ctx_count)
    local = jnp.where(table // 2 < ctx_count, 0, 2) + table % 2
    at = lax.broadcasted_iota(jnp.int32, table.shape, 1)
    mine = owner == me
    for slot in range(CAP):
        found = jnp.min(jnp.where(mine, at, LISTED))
        loc = jnp.sum(jnp.where(at == found, local, 0))
        mine = mine & (at > found)
        pay_ref[0, slot] = k_ref[loc]
        pay_ref[1, slot] = v_ref[loc]
    for half, ref in ((0, ahead_ref), (1, back_ref)):
        for part in range(2):
            ref[0, part * BLOCK : (part + 1) * BLOCK] = k_ref[2 * half + part]
            ref[1, part * BLOCK : (part + 1) * BLOCK] = v_ref[2 * half + part]


def owned(table, ctx_count):
    stretch = table // 2
    return jnp.where(stretch < ctx_count, stretch, 2 * ctx_count - 1 - stretch)


def plan_kernel(ctx_count, sides, me_ref, row_ref, col_ref, blk_ref, key_at_ref, val_at_ref, meta_ref):
    me = me_ref[0]
    row, col = row_ref[...], col_ref[...]
    square = (LISTED, LISTED)
    iota = lax.broadcasted_iota
    total = functools.partial(jnp.sum, keepdims=True)
    pick = lambda test, value, axis: total(jnp.where(test, value, 0), axis=axis)
    place = pick(row < col, jnp.int32(1), 1)
    earlier = iota(jnp.int32, square, 1) < iota(jnp.int32, square, 0)
    owner = owned(col, ctx_count)
    rank = pick((owned(row, ctx_count) == owner) & earlier, jnp.int32(1), 1)
    blk_ref[...] = pick(place == iota(jnp.int32, square, 1), col, 0)
    for halves, ref in ((True, key_at_ref), (False, val_at_ref)):
        entry = arrivals(*sides, halves, me, iota(jnp.int32, (1, CAP * ctx_count), 1))
        ref[...] = LISTED + pick(owner * CAP + rank == entry, place - LISTED, 0)
    lane = iota(jnp.int32, (1, 16), 1)
    meta = jnp.where(lane % 8 == 3, me, 0)
    for st, s in enumerate((me, 2 * ctx_count - 1 - me)):
        found = [jnp.sum(jnp.where(row < 2 * s, 1, 0)), jnp.sum(jnp.where(row <= 2 * s + 1, 1, 0)), s]
        for n, value in enumerate(found):
            meta = jnp.where(lane == 8 * st + n, value, meta)
        for n in range(4):
            b = 2 * (s - 1) + n
            free = 1 - jnp.max(jnp.where(row == b, 1, 0))
            meta = jnp.where(lane == 8 * st + 4 + n, jnp.where(b >= 0, free, 0), meta)
    meta_ref[...] = meta


def band_halves(own_ref, ahead_ref, back_ref, which, st, me, ctx_count):
    if st == 0:
        return ahead_ref[which]
    return jnp.where(me == ctx_count - 1, own_ref[0], back_ref[which])


def band_kernel(ctx_count, meta_ref, slash_ref, q_ref, k_ref, ahead_ref, back_ref, mask_ref, top_ref):
    behind = STRETCH - lax.broadcasted_iota(jnp.int32, (8, 2 * STRETCH), 1)
    for h in range(HEADS):
        def listed(n, hit):
            return hit | (behind == slash_ref[h, n])

        hit = behind == 0
        for n in range(LISTED):
            hit = listed(n, hit)
        row = jnp.where(hit, 1.0, 0.0).astype(F32)[:1]
        spread = jnp.broadcast_to(row, (STRETCH, 2 * STRETCH))
        mask_ref[h] = pltpu.roll(spread, 0, 1, stride=1, stride_axis=0)
    me = meta_ref[0, 3]
    for st in range(2):
        before = band_halves(k_ref, ahead_ref, back_ref, 0, st, me, ctx_count)
        for h in range(HEADS):
            q = q_ref[st, :, h * HEAD : (h + 1) * HEAD]
            top = jnp.full((STRETCH, BLOCK), -jnp.inf, F32)
            for n in range(4):
                part = before if n < 2 else k_ref[st]
                s = dot_t(q, part[(n % 2) * BLOCK : (n % 2 + 1) * BLOCK])
                ok = (mask_ref[h, :, n * BLOCK : (n + 1) * BLOCK] > 0.5) & (meta_ref[0, 8 * st + 4 + n] > 0)
                top = jnp.maximum(top, jnp.where(ok, s, -jnp.inf))
            top_ref[st, h] = top


def fetch(at_ref, pieces, target_ref):
    base = 0
    for ref in pieces:
        def copy(i, _, ref=ref, base=base):
            for n in range(UNROLL):
                target_ref[at_ref[0, base + i * UNROLL + n]] = ref[i * UNROLL + n]
            return 0

        lax.fori_loop(0, ref.shape[0] // UNROLL, copy, 0)
        base += ref.shape[0]


def causal(blk_ref, s, g):
    lead = lax.broadcasted_iota(jnp.int32, (STRETCH, BLOCK), 1) - lax.broadcasted_iota(jnp.int32, (STRETCH, BLOCK), 0)
    return [lead <= s * STRETCH - blk_ref[0, g * GROUP + n] * BLOCK for n in range(GROUP)]


def top_kernel(meta_ref, blk_ref, at_ref, q_ref, top_in_ref, *refs):
    pieces, (keys_ref, top_ref) = refs[:-2], refs[-2:]
    fetch(at_ref, pieces, keys_ref)
    for st in range(2):
        full, seen, s = meta_ref[0, 8 * st], meta_ref[0, 8 * st + 1], meta_ref[0, 8 * st + 2]
        plain, groups = full // GROUP, (seen + GROUP - 1) // GROUP
        for h in range(HEADS):
            top_ref[st, h] = top_in_ref[st, h]

        def step(masked, g, _):
            keys = keys_ref[pl.ds(g * GROUP, GROUP)].reshape(SPAN, HEAD)
            ok = causal(blk_ref, s, g) if masked else None
            for h in range(HEADS):
                scores = dot_t(q_ref[st, :, h * HEAD : (h + 1) * HEAD], keys)
                tops = []
                for n in range(GROUP):
                    part = scores[:, n * BLOCK : (n + 1) * BLOCK]
                    tops.append(jnp.where(ok[n], part, -jnp.inf) if masked else part)
                top = functools.reduce(jnp.maximum, tops)
                top_ref[st, h] = jnp.maximum(top_ref[st, h], top)
            return 0

        lax.fori_loop(0, plain, functools.partial(step, False), 0)
        lax.fori_loop(plain, groups, functools.partial(step, True), 0)
        for h in range(HEADS):
            row = jnp.max(top_ref[st, h], axis=1, keepdims=True)
            top_ref[st, h] = jnp.broadcast_to(row, (STRETCH, BLOCK))


def out_kernel(ctx_count, st, arriving, meta_ref, blk_ref, at_ref, q_ref, keys_ref, top_ref, mask_ref, k_ref, v_ref, ahead_ref, back_ref, *refs):
    full, seen, s = meta_ref[0, 8 * st], meta_ref[0, 8 * st + 1], meta_ref[0, 8 * st + 2]
    me = meta_ref[0, 8 * st + 3]
    plain, groups = full // GROUP, (seen + GROUP - 1) // GROUP
    if arriving:
        pieces, (out_ref, vals, total, acc) = refs[:arriving], refs[-4:]
        fetch(at_ref, pieces, vals)
    else:
        vals, out_ref, total, acc = refs
    k_before = band_halves(k_ref, ahead_ref, back_ref, 0, st, me, ctx_count)
    v_before = band_halves(v_ref, ahead_ref, back_ref, 1, st, me, ctx_count)

    for h in range(HEADS):
        q = q_ref[0, :, h * HEAD : (h + 1) * HEAD]
        scores = [dot_t(q, k_before), dot_t(q, k_ref[st])]
        expos = []
        for n in range(4):
            part = scores[n // 2][:, (n % 2) * BLOCK : (n % 2 + 1) * BLOCK]
            ok = (mask_ref[h, :, n * BLOCK : (n + 1) * BLOCK] > 0.5) & (meta_ref[0, 8 * st + 4 + n] > 0)
            expos.append(jnp.where(ok, jnp.exp2((part - top_ref[0, h]) * EXP_SCALE), 0.0))
        total[h] = (expos[0] + expos[1]) + (expos[2] + expos[3])
        weights = [e.astype(BF16) for e in expos]
        acc[h] = jnp.dot(
            jnp.concatenate(weights[:2], axis=1), v_before, preferred_element_type=F32
        ) + jnp.dot(jnp.concatenate(weights[2:], axis=1), v_ref[st], preferred_element_type=F32)

    def step(masked, g, _):
        keys = keys_ref[pl.ds(g * GROUP, GROUP)].reshape(SPAN, HEAD)
        values = vals[pl.ds(g * GROUP, GROUP)].reshape(SPAN, HEAD)
        ok = causal(blk_ref, s, g) if masked else None
        for h in range(HEADS):
            scores = dot_t(q_ref[0, :, h * HEAD : (h + 1) * HEAD], keys)
            expos = []
            for n in range(GROUP):
                part = jnp.exp2((scores[:, n * BLOCK : (n + 1) * BLOCK] - top_ref[0, h]) * EXP_SCALE)
                expos.append(jnp.where(ok[n], part, 0.0) if masked else part)
            total[h] += functools.reduce(jnp.add, expos)
            weights = jnp.concatenate([e.astype(BF16) for e in expos], axis=1)
            acc[h] += jnp.dot(weights, values, preferred_element_type=F32)
        return 0

    lax.fori_loop(0, plain, functools.partial(step, False), 0)
    lax.fori_loop(plain, groups, functools.partial(step, True), 0)
    for h in range(HEADS):
        row = jnp.sum(total[h], axis=1, keepdims=True)
        out_ref[:, h * HEAD : (h + 1) * HEAD] = (acc[h] / row).astype(BF16)


def mix_kernel(a0, a1, a2, a3, w0, w1, w2, w3, *refs):
    out_ref = refs[-1]
    sums = [jnp.dot(a[...], w[...], preferred_element_type=F32) for a, w in ((a0, w0), (a1, w1), (a2, w2), (a3, w3))]
    out_ref[0] = ((sums[0] + sums[1]) + (sums[2] + sums[3])).astype(BF16)


def from_ahead(x, axis, shift):
    n = lax.axis_size(axis)
    return lax.ppermute(x, axis, [((i + shift) % n, i) for i in range(n)])


def line_kernel(*refs):
    pieces, out_ref = refs[:X_CHIPS], refs[-1]
    for n, ref in enumerate(pieces):
        for which in range(2):
            out_ref[which, n * CAP : (n + 1) * CAP] = ref[which]


def chip_kernel(which, own_ref, other_ref, *refs):
    count = own_ref.shape[1]
    refs[-1][:count] = own_ref[which]
    refs[-1][count:] = other_ref[which]


def copy_kernel(source_ref, out_ref):
    out_ref[...] = source_ref[...]


def gather_columns(nx, nz, payload, later):
    place = lambda x, z, c: ((x % nx) * nz + z % nz) * 2 + c
    every = [(x, z, c) for x in range(nx) for z in range(nz) for c in range(2)]
    route = lambda f: [(place(*d), place(*f(*d))) for d in every]
    across = route(lambda x, z, c: (x, z, 1 - c))
    along = route(lambda x, z, c: (x, z + 1 - 2 * c, c))
    send = lambda a, r: lax.ppermute(a, "ctx", r)

    shape = jax.ShapeDtypeStruct
    call = functools.partial(pl.pallas_call, compiler_params=PARAMS)
    size = nx * CAP
    line = [payload] + [send(payload, route(lambda x, z, c, n=n: (x - n, z, c))) for n in range(1, nx)]
    own = call(
        line_kernel,
        out_shape=shape((2, size, BLOCK, HEAD), BF16),
        in_specs=[VMEM()] * nx,
        out_specs=VMEM(),
        name="line",
    )(*line)
    other = send(own, across)
    pieces = []
    waited = []
    for which in range(2):
        moving = call(
            functools.partial(chip_kernel, which),
            out_shape=shape((2 * size, BLOCK, HEAD), BF16),
            in_specs=[VMEM()] * 2 + [ANY()] * len(waited),
            out_specs=VMEM(),
            name=f"chip{which}",
        )(own, other, *waited)
        held = [moving]
        for n in range(1, nz // 2 + 1):
            last = n == nz // 2
            if which == 0 and last:
                moving = call(
                    copy_kernel,
                    grid=(1,),
                    out_shape=shape((size, BLOCK, HEAD), BF16),
                    in_specs=[pl.BlockSpec((size, BLOCK, HEAD), lambda i: (0, 0, 0))],
                    out_specs=VMEM(),
                    name="half",
                )(moving)
            moving = send(moving, along)
            held += [moving] + ([] if which == 1 and last else [send(moving, across)])
            if n == 1:
                waited = [moving, *later]
        pieces.append(held)
    return pieces


def arrivals(nx, nz, halves, me, entry):
    x, z, c = lax.div(me, 2 * nz), lax.rem(lax.div(me, 2), nz), lax.rem(me, 2)
    size = nx * CAP
    at = entry % (2 * size)
    piece = entry // (2 * size)
    hops = jnp.where(piece == 0, 0, (piece + 1) // 2)
    mirrored = jnp.where(piece == 0, 0, (piece + 1) % 2)
    half = at // size
    if halves:
        last = piece == nz - 1
        mirrored, half = jnp.where(last, half, mirrored), jnp.where(last, 0, half)
    side = jnp.where(mirrored == 1, 1 - 2 * c, 2 * c - 1) * hops
    core = jnp.where(mirrored == half, c, 1 - c)
    line = at % size // CAP
    return (((x + line) % nx * nz + (z + nz + side) % nz) * 2 + core) * CAP + at % CAP


def cost(us):
    return pl.CostEstimate(flops=0, bytes_accessed=int(us * 3.0e6), transcendentals=0)


def per_device(queries, keys, values, column_block_table, slash_offsets, out_weight):
    ctx_count = lax.axis_size("ctx")
    tp = lax.axis_size("tp")
    me = lax.axis_index("ctx").reshape(1).astype(jnp.int32)
    tp_index = lax.axis_index("tp")
    q, k, v = queries[0], keys[0], values[0]
    shape = jax.ShapeDtypeStruct
    i32 = jnp.int32

    payload, ahead, back = pl.pallas_call(
        functools.partial(pack_kernel, ctx_count),
        out_shape=[shape((2, CAP, BLOCK, HEAD), BF16)] + [shape((2, STRETCH, HEAD), BF16)] * 2,
        in_specs=[SMEM()] + [ANY()] * 3,
        out_specs=[VMEM()] * 3,
        scratch_shapes=[
            pltpu.VMEM(column_block_table.shape, i32),
            pltpu.VMEM((4, BLOCK, HEAD), BF16),
            pltpu.VMEM((4, BLOCK, HEAD), BF16),
            pltpu.SemaphoreType.DMA((3,)),
        ],
        compiler_params=pltpu.CompilerParams(vmem_limit_bytes=60 * 1024 * 1024),
        name="pack",
    )(me, column_block_table, k.reshape(4, BLOCK, HEAD), v.reshape(4, BLOCK, HEAD))

    sides = (X_CHIPS, ctx_count // (2 * X_CHIPS))
    blk, key_at, val_at, meta = pl.pallas_call(
        functools.partial(plan_kernel, ctx_count, sides),
        out_shape=[shape((1, LISTED), i32)] + [shape((1, CAP * ctx_count), i32)] * 2 + [shape((1, 16), i32)],
        in_specs=[SMEM(), VMEM(), VMEM()],
        out_specs=[VMEM()] * 4,
        compiler_params=PARAMS,
        cost_estimate=cost(2),
        name="plan",
    )(me, column_block_table, column_block_table.reshape(LISTED, 1))

    steps = range(ctx_count - 1)
    before = lax.ppermute(ahead, "ctx", [(i, i + 1) for i in steps])
    after = lax.ppermute(back, "ctx", [(i + 1, i) for i in steps])

    width = out_weight.shape[1] // tp
    slabs = []
    for shift in range(tp):
        target = lax.rem(tp_index + tp - shift, tp)
        slab = lax.dynamic_slice(out_weight, (0, target * width), (out_weight.shape[0], width))
        slabs.append(slab if shift == 0 else from_ahead(slab, "tp", shift))

    mask, top = pl.pallas_call(
        functools.partial(band_kernel, ctx_count),
        out_shape=[shape((HEADS, STRETCH, 2 * STRETCH), F32), shape((2, HEADS, STRETCH, BLOCK), F32)],
        in_specs=[SMEM(), SMEM(), VMEM(), VMEM(), VMEM(), VMEM()],
        out_specs=[VMEM(), VMEM()],
        compiler_params=PARAMS,
        cost_estimate=cost(3),
        name="band",
    )(meta, slash_offsets, q, k, before, after)

    k_pieces, v_pieces = gather_columns(*sides, payload, [mask])

    columns, top = pl.pallas_call(
        top_kernel,
        out_shape=[shape((ROOM, BLOCK, HEAD), BF16), shape((2, HEADS, STRETCH, BLOCK), F32)],
        in_specs=[SMEM(), SMEM(), SMEM(), VMEM(), VMEM()] + [VMEM()] * len(k_pieces),
        out_specs=[VMEM(), VMEM()],
        compiler_params=PARAMS,
        cost_estimate=cost(9),
        name="top",
    )(meta, blk, key_at, q, top, *k_pieces)

    mixed = column_vals = None
    for st in range(2):
        first = st == 0
        extra = [*v_pieces, *slabs] if first else [column_vals]
        result = pl.pallas_call(
            functools.partial(out_kernel, ctx_count, st, len(v_pieces) if first else 0),
            grid=(1,),
            out_shape=[shape((STRETCH, HEADS * HEAD), BF16)] + [shape((ROOM, BLOCK, HEAD), BF16)] * first,
            in_specs=[
                SMEM(), SMEM(), SMEM(),
                pl.BlockSpec((1, STRETCH, HEADS * HEAD), lambda i, st=st: (st, 0, 0)),
                VMEM(),
                pl.BlockSpec((1, HEADS, STRETCH, BLOCK), lambda i, st=st: (st, 0, 0, 0)),
                VMEM(), VMEM(), VMEM(), VMEM(), VMEM(),
            ] + ([VMEM()] * len(v_pieces) + [ANY()] * tp if first else [VMEM()]),
            out_specs=[VMEM()] * (1 + first),
            scratch_shapes=[
                pltpu.VMEM((HEADS, STRETCH, BLOCK), F32),
                pltpu.VMEM((HEADS, STRETCH, HEAD), F32),
            ],
            compiler_params=PARAMS,
            cost_estimate=cost(8),
            name=f"attend{st}",
        )(meta, blk, val_at, q, columns, top, mask, k, v, before, after, *extra)
        head_out = result[0]
        if first:
            column_vals = result[1]
        parts = [head_out] + [from_ahead(head_out, "tp", shift) for shift in range(1, tp)]
        tile = width // 4
        mixed = pl.pallas_call(
            mix_kernel,
            grid=(width // tile,),
            out_shape=shape((2, STRETCH, width), BF16),
            in_specs=[VMEM()] * 4
            + [pl.BlockSpec((HEADS * HEAD, tile), lambda i: (0, i))] * 4
            + ([ANY()] if st else []),
            out_specs=pl.BlockSpec((1, STRETCH, tile), lambda i, st=st: (st, 0, i)),
            input_output_aliases={8: 0} if st else {},
            compiler_params=PARAMS,
            cost_estimate=cost(3),
            name=f"mix{st}",
        )(*parts, *slabs, *([mixed] if st else []))
    return mixed[None]


def solution(mesh):
    in_specs = (
        P("ctx", None, None, "tp"),
        P("ctx", None, None, "tp"),
        P("ctx", None, None, "tp"),
        P("tp", None),
        P("tp", None),
        P("tp", None),
    )
    out_specs = P("ctx", None, None, "tp")
    return jax.shard_map(
        per_device, mesh=mesh, in_specs=in_specs, out_specs=out_specs, check_vma=False
    )
```

```python
import functools
import math

import jax
import jax.numpy as jnp
from jax import lax
from jax.experimental import pallas as pl
from jax.experimental.pallas import tpu as pltpu
from jax.sharding import PartitionSpec as P

HEAD = 128
BLOCK = 128
STRETCH = 256
CAP = 2
GROUP = 8
SPAN = GROUP * BLOCK
LISTED = 64
ROOM = LISTED + 1
UNROLL = 4
X_CHIPS = 4
HEADS = 4
EXP_SCALE = math.log2(math.e) * HEAD ** (-0.5)
VMEM_LIMIT = 48 * 1024 * 1024

SMEM = functools.partial(pl.BlockSpec, memory_space=pltpu.SMEM)
VMEM = functools.partial(pl.BlockSpec, memory_space=pltpu.VMEM)
ANY = functools.partial(pl.BlockSpec, memory_space=pl.ANY)
PARAMS = pltpu.CompilerParams(vmem_limit_bytes=VMEM_LIMIT)
F32 = jnp.float32
BF16 = jnp.bfloat16


def dot_t(a, b):
    return lax.dot_general(a, b, (((1,), (1,)), ((), ())), preferred_element_type=F32)


def pack_kernel(ctx_count, me_ref, table_ref, k_ref, v_ref, pay_ref, ahead_ref, back_ref):
    me = me_ref[0]
    table = table_ref[...]
    owner = owned(table, ctx_count)
    local = jnp.where(table // 2 < ctx_count, 0, 2) + table % 2
    at = lax.broadcasted_iota(jnp.int32, table.shape, 1)
    mine = owner == me
    for slot in range(CAP):
        found = jnp.min(jnp.where(mine, at, LISTED))
        loc = jnp.sum(jnp.where(at == found, local, 0))
        mine = mine & (at > found)
        pay_ref[0, slot] = k_ref[loc]
        pay_ref[1, slot] = v_ref[loc]
    for half, ref in ((0, ahead_ref), (1, back_ref)):
        for part in range(2):
            ref[0, part * BLOCK : (part + 1) * BLOCK] = k_ref[2 * half + part]
            ref[1, part * BLOCK : (part + 1) * BLOCK] = v_ref[2 * half + part]


def owned(table, ctx_count):
    stretch = table // 2
    return jnp.where(stretch < ctx_count, stretch, 2 * ctx_count - 1 - stretch)


def plan_kernel(ctx_count, sides, me_ref, row_ref, col_ref, blk_ref, key_at_ref, val_at_ref, meta_ref):
    me = me_ref[0]
    row, col = row_ref[...], col_ref[...]
    square = (LISTED, LISTED)
    iota = lax.broadcasted_iota
    total = functools.partial(jnp.sum, keepdims=True)
    pick = lambda test, value, axis: total(jnp.where(test, value, 0), axis=axis)
    place = pick(row < col, jnp.int32(1), 1)
    earlier = iota(jnp.int32, square, 1) < iota(jnp.int32, square, 0)
    owner = owned(col, ctx_count)
    rank = pick((owned(row, ctx_count) == owner) & earlier, jnp.int32(1), 1)
    blk_ref[...] = pick(place == iota(jnp.int32, square, 1), col, 0)
    for halves, ref in ((True, key_at_ref), (False, val_at_ref)):
        entry = arrivals(*sides, halves, me, iota(jnp.int32, (1, CAP * ctx_count), 1))
        ref[...] = LISTED + pick(owner * CAP + rank == entry, place - LISTED, 0)
    lane = iota(jnp.int32, (1, 16), 1)
    meta = jnp.where(lane % 8 == 3, me, 0)
    for st, s in enumerate((me, 2 * ctx_count - 1 - me)):
        found = [jnp.sum(jnp.where(row < 2 * s, 1, 0)), jnp.sum(jnp.where(row <= 2 * s + 1, 1, 0)), s]
        for n, value in enumerate(found):
            meta = jnp.where(lane == 8 * st + n, value, meta)
        for n in range(4):
            b = 2 * (s - 1) + n
            free = 1 - jnp.max(jnp.where(row == b, 1, 0))
            meta = jnp.where(lane == 8 * st + 4 + n, jnp.where(b >= 0, free, 0), meta)
    meta_ref[...] = meta


def band_halves(own_ref, ahead_ref, back_ref, which, st, me, ctx_count):
    if st == 0:
        return ahead_ref[which]
    return jnp.where(me == ctx_count - 1, own_ref[0], back_ref[which])


def band_kernel(ctx_count, meta_ref, slash_ref, q_ref, k_ref, ahead_ref, back_ref, mask_ref, top_ref):
    behind = STRETCH - lax.broadcasted_iota(jnp.int32, (8, 2 * STRETCH), 1)
    for h in range(HEADS):
        def listed(n, hit):
            return hit | (behind == slash_ref[h, n])

        hit = behind == 0
        for n in range(LISTED):
            hit = listed(n, hit)
        row = jnp.where(hit, 1.0, 0.0).astype(F32)[:1]
        spread = jnp.broadcast_to(row, (STRETCH, 2 * STRETCH))
        mask_ref[h] = pltpu.roll(spread, 0, 1, stride=1, stride_axis=0)
    me = meta_ref[0, 3]
    for st in range(2):
        before = band_halves(k_ref, ahead_ref, back_ref, 0, st, me, ctx_count)
        for h in range(HEADS):
            q = q_ref[st, :, h * HEAD : (h + 1) * HEAD]
            top = jnp.full((STRETCH, BLOCK), -jnp.inf, F32)
            for n in range(4):
                part = before if n < 2 else k_ref[st]
                s = dot_t(q, part[(n % 2) * BLOCK : (n % 2 + 1) * BLOCK])
                ok = (mask_ref[h, :, n * BLOCK : (n + 1) * BLOCK] > 0.5) & (meta_ref[0, 8 * st + 4 + n] > 0)
                top = jnp.maximum(top, jnp.where(ok, s, -jnp.inf))
            top_ref[st, h] = top


def fetch(at_ref, pieces, target_ref):
    base = 0
    for ref in pieces:
        def copy(i, _, ref=ref, base=base):
            for n in range(UNROLL):
                target_ref[at_ref[0, base + i * UNROLL + n]] = ref[i * UNROLL + n]
            return 0

        lax.fori_loop(0, ref.shape[0] // UNROLL, copy, 0)
        base += ref.shape[0]


def causal(blk_ref, s, g):
    lead = lax.broadcasted_iota(jnp.int32, (STRETCH, BLOCK), 1) - lax.broadcasted_iota(jnp.int32, (STRETCH, BLOCK), 0)
    return [lead <= s * STRETCH - blk_ref[0, g * GROUP + n] * BLOCK for n in range(GROUP)]


def top_kernel(meta_ref, blk_ref, at_ref, q_ref, top_in_ref, *refs):
    pieces, (keys_ref, top_ref) = refs[:-2], refs[-2:]
    fetch(at_ref, pieces, keys_ref)
    for st in range(2):
        full, seen, s = meta_ref[0, 8 * st], meta_ref[0, 8 * st + 1], meta_ref[0, 8 * st + 2]
        plain, groups = full // GROUP, (seen + GROUP - 1) // GROUP
        for h in range(HEADS):
            top_ref[st, h] = top_in_ref[st, h]

        def step(masked, g, _):
            keys = keys_ref[pl.ds(g * GROUP, GROUP)].reshape(SPAN, HEAD)
            ok = causal(blk_ref, s, g) if masked else None
            for h in range(HEADS):
                scores = dot_t(q_ref[st, :, h * HEAD : (h + 1) * HEAD], keys)
                tops = []
                for n in range(GROUP):
                    part = scores[:, n * BLOCK : (n + 1) * BLOCK]
                    tops.append(jnp.where(ok[n], part, -jnp.inf) if masked else part)
                top = functools.reduce(jnp.maximum, tops)
                top_ref[st, h] = jnp.maximum(top_ref[st, h], top)
            return 0

        lax.fori_loop(0, plain, functools.partial(step, False), 0)
        lax.fori_loop(plain, groups, functools.partial(step, True), 0)
        for h in range(HEADS):
            row = jnp.max(top_ref[st, h], axis=1, keepdims=True)
            top_ref[st, h] = jnp.broadcast_to(row, (STRETCH, BLOCK))


def out_kernel(ctx_count, st, arriving, meta_ref, blk_ref, at_ref, q_ref, keys_ref, top_ref, mask_ref, k_ref, v_ref, ahead_ref, back_ref, *refs):
    full, seen, s = meta_ref[0, 8 * st], meta_ref[0, 8 * st + 1], meta_ref[0, 8 * st + 2]
    me = meta_ref[0, 8 * st + 3]
    plain, groups = full // GROUP, (seen + GROUP - 1) // GROUP
    if arriving:
        pieces, (out_ref, vals, total, acc) = refs[:arriving], refs[-4:]
        fetch(at_ref, pieces, vals)
    else:
        vals, out_ref, total, acc = refs
    k_before = band_halves(k_ref, ahead_ref, back_ref, 0, st, me, ctx_count)
    v_before = band_halves(v_ref, ahead_ref, back_ref, 1, st, me, ctx_count)

    for h in range(HEADS):
        q = q_ref[0, :, h * HEAD : (h + 1) * HEAD]
        scores = [dot_t(q, k_before), dot_t(q, k_ref[st])]
        expos = []
        for n in range(4):
            part = scores[n // 2][:, (n % 2) * BLOCK : (n % 2 + 1) * BLOCK]
            ok = (mask_ref[h, :, n * BLOCK : (n + 1) * BLOCK] > 0.5) & (meta_ref[0, 8 * st + 4 + n] > 0)
            expos.append(jnp.where(ok, jnp.exp2((part - top_ref[0, h]) * EXP_SCALE), 0.0))
        total[h] = (expos[0] + expos[1]) + (expos[2] + expos[3])
        weights = [e.astype(BF16) for e in expos]
        acc[h] = jnp.dot(
            jnp.concatenate(weights[:2], axis=1), v_before, preferred_element_type=F32
        ) + jnp.dot(jnp.concatenate(weights[2:], axis=1), v_ref[st], preferred_element_type=F32)

    def step(masked, g, _):
        keys = keys_ref[pl.ds(g * GROUP, GROUP)].reshape(SPAN, HEAD)
        values = vals[pl.ds(g * GROUP, GROUP)].reshape(SPAN, HEAD)
        ok = causal(blk_ref, s, g) if masked else None
        for h in range(HEADS):
            scores = dot_t(q_ref[0, :, h * HEAD : (h + 1) * HEAD], keys)
            expos = []
            for n in range(GROUP):
                part = jnp.exp2((scores[:, n * BLOCK : (n + 1) * BLOCK] - top_ref[0, h]) * EXP_SCALE)
                expos.append(jnp.where(ok[n], part, 0.0) if masked else part)
            total[h] += functools.reduce(jnp.add, expos)
            weights = jnp.concatenate([e.astype(BF16) for e in expos], axis=1)
            acc[h] += jnp.dot(weights, values, preferred_element_type=F32)
        return 0

    lax.fori_loop(0, plain, functools.partial(step, False), 0)
    lax.fori_loop(plain, groups, functools.partial(step, True), 0)
    for h in range(HEADS):
        row = jnp.sum(total[h], axis=1, keepdims=True)
        out_ref[:, h * HEAD : (h + 1) * HEAD] = (acc[h] / row).astype(BF16)


def mix_kernel(a0, a1, a2, a3, w0, w1, w2, w3, *refs):
    out_ref = refs[-1]
    sums = [jnp.dot(a[...], w[...], preferred_element_type=F32) for a, w in ((a0, w0), (a1, w1), (a2, w2), (a3, w3))]
    out_ref[0] = ((sums[0] + sums[1]) + (sums[2] + sums[3])).astype(BF16)


def from_ahead(x, axis, shift):
    n = lax.axis_size(axis)
    return lax.ppermute(x, axis, [((i + shift) % n, i) for i in range(n)])


def line_kernel(*refs):
    pieces, out_ref = refs[:X_CHIPS], refs[-1]
    for n, ref in enumerate(pieces):
        for which in range(2):
            out_ref[which, n * CAP : (n + 1) * CAP] = ref[which]


def chip_kernel(which, own_ref, other_ref, *refs):
    count = own_ref.shape[1]
    refs[-1][:count] = own_ref[which]
    refs[-1][count:] = other_ref[which]


def copy_kernel(source_ref, out_ref):
    out_ref[...] = source_ref[...]


def gather_columns(nx, nz, payload, later):
    place = lambda x, z, c: ((x % nx) * nz + z % nz) * 2 + c
    every = [(x, z, c) for x in range(nx) for z in range(nz) for c in range(2)]
    route = lambda f: [(place(*d), place(*f(*d))) for d in every]
    across = route(lambda x, z, c: (x, z, 1 - c))
    along = route(lambda x, z, c: (x, z + 1 - 2 * c, c))
    send = lambda a, r: lax.ppermute(a, "ctx", r)

    shape = jax.ShapeDtypeStruct
    call = functools.partial(pl.pallas_call, compiler_params=PARAMS)
    size = nx * CAP
    line = [payload] + [send(payload, route(lambda x, z, c, n=n: (x - n, z, c))) for n in range(1, nx)]
    own = call(
        line_kernel,
        out_shape=shape((2, size, BLOCK, HEAD), BF16),
        in_specs=[VMEM()] * nx,
        out_specs=VMEM(),
        name="line",
    )(*line)
    other = send(own, across)
    pieces = []
    waited = []
    for which in range(2):
        moving = call(
            functools.partial(chip_kernel, which),
            out_shape=shape((2 * size, BLOCK, HEAD), BF16),
            in_specs=[VMEM()] * 2 + [ANY()] * len(waited),
            out_specs=VMEM(),
            name=f"chip{which}",
        )(own, other, *waited)
        held = [moving]
        for n in range(1, nz // 2 + 1):
            last = n == nz // 2
            if which == 0 and last:
                moving = call(
                    copy_kernel,
                    grid=(1,),
                    out_shape=shape((size, BLOCK, HEAD), BF16),
                    in_specs=[pl.BlockSpec((size, BLOCK, HEAD), lambda i: (0, 0, 0))],
                    out_specs=VMEM(),
                    name="half",
                )(moving)
            moving = send(moving, along)
            held += [moving] + ([] if which == 1 and last else [send(moving, across)])
            if n == 1:
                waited = [moving, *later]
        pieces.append(held)
    return pieces


def arrivals(nx, nz, halves, me, entry):
    x, z, c = lax.div(me, 2 * nz), lax.rem(lax.div(me, 2), nz), lax.rem(me, 2)
    size = nx * CAP
    at = entry % (2 * size)
    piece = entry // (2 * size)
    hops = jnp.where(piece == 0, 0, (piece + 1) // 2)
    mirrored = jnp.where(piece == 0, 0, (piece + 1) % 2)
    half = at // size
    if halves:
        last = piece == nz - 1
        mirrored, half = jnp.where(last, half, mirrored), jnp.where(last, 0, half)
    side = jnp.where(mirrored == 1, 1 - 2 * c, 2 * c - 1) * hops
    core = jnp.where(mirrored == half, c, 1 - c)
    line = at % size // CAP
    return (((x + line) % nx * nz + (z + nz + side) % nz) * 2 + core) * CAP + at % CAP


def slab_kernel(tp, index_ref, weight_ref, *refs):
    width = weight_ref.shape[1] // tp
    for shift, ref in enumerate(refs[1:]):
        target = lax.rem(index_ref[0] + tp - shift, tp)
        ref[...] = weight_ref[:, pl.ds(pl.multiple_of(target * width, width), width)]


def cost(us):
    return pl.CostEstimate(flops=0, bytes_accessed=int(us * 3.0e6), transcendentals=0)


def per_device(queries, keys, values, column_block_table, slash_offsets, out_weight):
    ctx_count = lax.axis_size("ctx")
    tp = lax.axis_size("tp")
    me = lax.axis_index("ctx").reshape(1).astype(jnp.int32)
    tp_index = lax.axis_index("tp")
    q, k, v = queries[0], keys[0], values[0]
    shape = jax.ShapeDtypeStruct
    i32 = jnp.int32

    payload, ahead, back = pl.pallas_call(
        functools.partial(pack_kernel, ctx_count),
        out_shape=[shape((2, CAP, BLOCK, HEAD), BF16)] + [shape((2, STRETCH, HEAD), BF16)] * 2,
        in_specs=[SMEM(), VMEM(), VMEM(), VMEM()],
        out_specs=[VMEM()] * 3,
        compiler_params=PARAMS,
        name="pack",
    )(me, column_block_table, k.reshape(4, BLOCK, HEAD), v.reshape(4, BLOCK, HEAD))

    sides = (X_CHIPS, ctx_count // (2 * X_CHIPS))
    blk, key_at, val_at, meta = pl.pallas_call(
        functools.partial(plan_kernel, ctx_count, sides),
        out_shape=[shape((1, LISTED), i32)] + [shape((1, CAP * ctx_count), i32)] * 2 + [shape((1, 16), i32)],
        in_specs=[SMEM(), VMEM(), VMEM()],
        out_specs=[VMEM()] * 4,
        compiler_params=PARAMS,
        cost_estimate=cost(2),
        name="plan",
    )(me, column_block_table, column_block_table.reshape(LISTED, 1))

    steps = range(ctx_count - 1)
    before = lax.ppermute(ahead, "ctx", [(i, i + 1) for i in steps])
    after = lax.ppermute(back, "ctx", [(i + 1, i) for i in steps])

    mask, top = pl.pallas_call(
        functools.partial(band_kernel, ctx_count),
        out_shape=[shape((HEADS, STRETCH, 2 * STRETCH), F32), shape((2, HEADS, STRETCH, BLOCK), F32)],
        in_specs=[SMEM(), SMEM(), VMEM(), VMEM(), VMEM(), VMEM()],
        out_specs=[VMEM(), VMEM()],
        compiler_params=PARAMS,
        cost_estimate=cost(3),
        name="band",
    )(meta, slash_offsets, q, k, before, after)

    k_pieces, v_pieces = gather_columns(*sides, payload, [mask])

    width = out_weight.shape[1] // tp
    depth = out_weight.shape[0]
    slabs = pl.pallas_call(
        functools.partial(slab_kernel, tp),
        grid=(depth // 128,),
        out_shape=[shape((depth, width), BF16)] * tp,
        in_specs=[SMEM(), pl.BlockSpec((128, out_weight.shape[1]), lambda i: (i, 0)), ANY()],
        out_specs=[pl.BlockSpec((128, width), lambda i: (i, 0))] * tp,
        compiler_params=PARAMS,
        cost_estimate=cost(3),
        name="slabs",
    )(tp_index.reshape(1).astype(i32), out_weight, v_pieces[0])
    slabs = [slabs[0]] + [from_ahead(slabs[shift], "tp", shift) for shift in range(1, tp)]

    columns, top = pl.pallas_call(
        top_kernel,
        out_shape=[shape((ROOM, BLOCK, HEAD), BF16), shape((2, HEADS, STRETCH, BLOCK), F32)],
        in_specs=[SMEM(), SMEM(), SMEM(), VMEM(), VMEM()] + [VMEM()] * len(k_pieces),
        out_specs=[VMEM(), VMEM()],
        compiler_params=PARAMS,
        cost_estimate=cost(9),
        name="top",
    )(meta, blk, key_at, q, top, *k_pieces)

    mixed = column_vals = None
    for st in range(2):
        first = st == 0
        extra = [*v_pieces, slabs[1], slabs[3]] if first else [column_vals]
        result = pl.pallas_call(
            functools.partial(out_kernel, ctx_count, st, len(v_pieces) if first else 0),
            grid=(1,),
            out_shape=[shape((STRETCH, HEADS * HEAD), BF16)] + [shape((ROOM, BLOCK, HEAD), BF16)] * first,
            in_specs=[
                SMEM(), SMEM(), SMEM(),
                pl.BlockSpec((1, STRETCH, HEADS * HEAD), lambda i, st=st: (st, 0, 0)),
                VMEM(),
                pl.BlockSpec((1, HEADS, STRETCH, BLOCK), lambda i, st=st: (st, 0, 0, 0)),
                VMEM(), VMEM(), VMEM(), VMEM(), VMEM(),
            ] + ([VMEM()] * len(v_pieces) + [ANY()] * 2 if first else [VMEM()]),
            out_specs=[VMEM()] * (1 + first),
            scratch_shapes=[
                pltpu.VMEM((HEADS, STRETCH, BLOCK), F32),
                pltpu.VMEM((HEADS, STRETCH, HEAD), F32),
            ],
            compiler_params=PARAMS,
            cost_estimate=cost(8),
            name=f"attend{st}",
        )(meta, blk, val_at, q, columns, top, mask, k, v, before, after, *extra)
        head_out = result[0]
        if first:
            column_vals = result[1]
        parts = [head_out] + [from_ahead(head_out, "tp", shift) for shift in range(1, tp)]
        tile = width // 4
        mixed = pl.pallas_call(
            mix_kernel,
            grid=(width // tile,),
            out_shape=shape((2, STRETCH, width), BF16),
            in_specs=[VMEM()] * 4
            + [pl.BlockSpec((HEADS * HEAD, tile), lambda i: (0, i))] * 4
            + ([ANY()] if st else []),
            out_specs=pl.BlockSpec((1, STRETCH, tile), lambda i, st=st: (st, 0, i)),
            input_output_aliases={8: 0} if st else {},
            compiler_params=PARAMS,
            cost_estimate=cost(3),
            name=f"mix{st}",
        )(*parts, *slabs, *([mixed] if st else []))
    return mixed[None]


def solution(mesh):
    in_specs = (
        P("ctx", None, None, "tp"),
        P("ctx", None, None, "tp"),
        P("ctx", None, None, "tp"),
        P("tp", None),
        P("tp", None),
        P("tp", None),
    )
    out_specs = P("ctx", None, None, "tp")
    return jax.shard_map(
        per_device, mesh=mesh, in_specs=in_specs, out_specs=out_specs, check_vma=False
    )
```

```python
import functools
import math

import jax
import jax.numpy as jnp
from jax import lax
from jax.experimental import pallas as pl
from jax.experimental.pallas import tpu as pltpu
from jax.sharding import PartitionSpec as P

HEAD = 128
BLOCK = 128
STRETCH = 256
CAP = 2
GROUP = 8
SPAN = GROUP * BLOCK
LISTED = 64
ROOM = LISTED + 1
UNROLL = 4
X_CHIPS = 4
HEADS = 4
EXP_SCALE = math.log2(math.e) * HEAD ** (-0.5)
VMEM_LIMIT = 48 * 1024 * 1024

SMEM = functools.partial(pl.BlockSpec, memory_space=pltpu.SMEM)
VMEM = functools.partial(pl.BlockSpec, memory_space=pltpu.VMEM)
ANY = functools.partial(pl.BlockSpec, memory_space=pl.ANY)
PARAMS = pltpu.CompilerParams(vmem_limit_bytes=VMEM_LIMIT)
F32 = jnp.float32
BF16 = jnp.bfloat16


def dot_t(a, b):
    return lax.dot_general(a, b, (((1,), (1,)), ((), ())), preferred_element_type=F32)


def pack_kernel(ctx_count, me_ref, table_ref, k_ref, v_ref, pay_ref, ahead_ref, back_ref):
    me = me_ref[0]
    table = table_ref[...]
    owner = owned(table, ctx_count)
    local = jnp.where(table // 2 < ctx_count, 0, 2) + table % 2
    at = lax.broadcasted_iota(jnp.int32, table.shape, 1)
    mine = owner == me
    for slot in range(CAP):
        found = jnp.min(jnp.where(mine, at, LISTED))
        loc = jnp.sum(jnp.where(at == found, local, 0))
        mine = mine & (at > found)
        pay_ref[0, slot] = k_ref[loc]
        pay_ref[1, slot] = v_ref[loc]
    for half, ref in ((0, ahead_ref), (1, back_ref)):
        for part in range(2):
            ref[0, part * BLOCK : (part + 1) * BLOCK] = k_ref[2 * half + part]
            ref[1, part * BLOCK : (part + 1) * BLOCK] = v_ref[2 * half + part]


def owned(table, ctx_count):
    stretch = table // 2
    return jnp.where(stretch < ctx_count, stretch, 2 * ctx_count - 1 - stretch)


def plan_kernel(ctx_count, sides, me_ref, row_ref, col_ref, blk_ref, key_at_ref, val_at_ref, meta_ref):
    me = me_ref[0]
    row, col = row_ref[...], col_ref[...]
    square = (LISTED, LISTED)
    iota = lax.broadcasted_iota
    total = functools.partial(jnp.sum, keepdims=True)
    pick = lambda test, value, axis: total(jnp.where(test, value, 0), axis=axis)
    place = pick(row < col, jnp.int32(1), 1)
    earlier = iota(jnp.int32, square, 1) < iota(jnp.int32, square, 0)
    owner = owned(col, ctx_count)
    rank = pick((owned(row, ctx_count) == owner) & earlier, jnp.int32(1), 1)
    blk_ref[...] = pick(place == iota(jnp.int32, square, 1), col, 0)
    for halves, ref in ((True, key_at_ref), (False, val_at_ref)):
        entry = arrivals(*sides, halves, me, iota(jnp.int32, (1, CAP * ctx_count), 1))
        ref[...] = LISTED + pick(owner * CAP + rank == entry, place - LISTED, 0)
    lane = iota(jnp.int32, (1, 16), 1)
    meta = jnp.where(lane % 8 == 3, me, 0)
    for st, s in enumerate((me, 2 * ctx_count - 1 - me)):
        found = [jnp.sum(jnp.where(row < 2 * s, 1, 0)), jnp.sum(jnp.where(row <= 2 * s + 1, 1, 0)), s]
        for n, value in enumerate(found):
            meta = jnp.where(lane == 8 * st + n, value, meta)
        for n in range(4):
            b = 2 * (s - 1) + n
            free = 1 - jnp.max(jnp.where(row == b, 1, 0))
            meta = jnp.where(lane == 8 * st + 4 + n, jnp.where(b >= 0, free, 0), meta)
    meta_ref[...] = meta


def band_halves(own_ref, ahead_ref, back_ref, which, st, me, ctx_count):
    if st == 0:
        return ahead_ref[which]
    return jnp.where(me == ctx_count - 1, own_ref[0], back_ref[which])


def band_kernel(ctx_count, meta_ref, slash_ref, q_ref, k_ref, ahead_ref, back_ref, mask_ref, top_ref):
    behind = STRETCH - lax.broadcasted_iota(jnp.int32, (8, 2 * STRETCH), 1)
    for h in range(HEADS):
        def listed(n, hit):
            return hit | (behind == slash_ref[h, n])

        hit = behind == 0
        for n in range(LISTED):
            hit = listed(n, hit)
        row = jnp.where(hit, 1.0, 0.0).astype(F32)[:1]
        spread = jnp.broadcast_to(row, (STRETCH, 2 * STRETCH))
        mask_ref[h] = pltpu.roll(spread, 0, 1, stride=1, stride_axis=0)
    me = meta_ref[0, 3]
    for st in range(2):
        before = band_halves(k_ref, ahead_ref, back_ref, 0, st, me, ctx_count)
        for h in range(HEADS):
            q = q_ref[st, :, h * HEAD : (h + 1) * HEAD]
            top = jnp.full((STRETCH, BLOCK), -jnp.inf, F32)
            for n in range(4):
                part = before if n < 2 else k_ref[st]
                s = dot_t(q, part[(n % 2) * BLOCK : (n % 2 + 1) * BLOCK])
                ok = (mask_ref[h, :, n * BLOCK : (n + 1) * BLOCK] > 0.5) & (meta_ref[0, 8 * st + 4 + n] > 0)
                top = jnp.maximum(top, jnp.where(ok, s, -jnp.inf))
            top_ref[st, h] = top


def fetch(at_ref, pieces, target_ref):
    base = 0
    for ref in pieces:
        def copy(i, _, ref=ref, base=base):
            for n in range(UNROLL):
                target_ref[at_ref[0, base + i * UNROLL + n]] = ref[i * UNROLL + n]
            return 0

        lax.fori_loop(0, ref.shape[0] // UNROLL, copy, 0)
        base += ref.shape[0]


def causal(blk_ref, s, g):
    lead = lax.broadcasted_iota(jnp.int32, (STRETCH, BLOCK), 1) - lax.broadcasted_iota(jnp.int32, (STRETCH, BLOCK), 0)
    return [lead <= s * STRETCH - blk_ref[0, g * GROUP + n] * BLOCK for n in range(GROUP)]


def top_kernel(meta_ref, blk_ref, at_ref, q_ref, top_in_ref, *refs):
    pieces, (keys_ref, top_ref) = refs[:-2], refs[-2:]
    fetch(at_ref, pieces, keys_ref)
    for st in range(2):
        full, seen, s = meta_ref[0, 8 * st], meta_ref[0, 8 * st + 1], meta_ref[0, 8 * st + 2]
        plain, groups = full // GROUP, (seen + GROUP - 1) // GROUP
        for h in range(HEADS):
            top_ref[st, h] = top_in_ref[st, h]

        def step(masked, g, _):
            keys = keys_ref[pl.ds(g * GROUP, GROUP)].reshape(SPAN, HEAD)
            ok = causal(blk_ref, s, g) if masked else None
            for h in range(HEADS):
                scores = dot_t(q_ref[st, :, h * HEAD : (h + 1) * HEAD], keys)
                tops = []
                for n in range(GROUP):
                    part = scores[:, n * BLOCK : (n + 1) * BLOCK]
                    tops.append(jnp.where(ok[n], part, -jnp.inf) if masked else part)
                top = functools.reduce(jnp.maximum, tops)
                top_ref[st, h] = jnp.maximum(top_ref[st, h], top)
            return 0

        lax.fori_loop(0, plain, functools.partial(step, False), 0)
        lax.fori_loop(plain, groups, functools.partial(step, True), 0)
        for h in range(HEADS):
            row = jnp.max(top_ref[st, h], axis=1, keepdims=True)
            top_ref[st, h] = jnp.broadcast_to(row, (STRETCH, BLOCK))


def out_kernel(ctx_count, st, arriving, meta_ref, blk_ref, at_ref, q_ref, keys_ref, top_ref, mask_ref, k_ref, v_ref, ahead_ref, back_ref, *refs):
    full, seen, s = meta_ref[0, 8 * st], meta_ref[0, 8 * st + 1], meta_ref[0, 8 * st + 2]
    me = meta_ref[0, 8 * st + 3]
    plain, groups = full // GROUP, (seen + GROUP - 1) // GROUP
    if arriving:
        pieces, (out_ref, vals, total, acc) = refs[:arriving], refs[-4:]
        fetch(at_ref, pieces, vals)
    else:
        vals, out_ref, total, acc = refs
    k_before = band_halves(k_ref, ahead_ref, back_ref, 0, st, me, ctx_count)
    v_before = band_halves(v_ref, ahead_ref, back_ref, 1, st, me, ctx_count)

    for h in range(HEADS):
        q = q_ref[0, :, h * HEAD : (h + 1) * HEAD]
        scores = [dot_t(q, k_before), dot_t(q, k_ref[st])]
        expos = []
        for n in range(4):
            part = scores[n // 2][:, (n % 2) * BLOCK : (n % 2 + 1) * BLOCK]
            ok = (mask_ref[h, :, n * BLOCK : (n + 1) * BLOCK] > 0.5) & (meta_ref[0, 8 * st + 4 + n] > 0)
            expos.append(jnp.where(ok, jnp.exp2((part - top_ref[0, h]) * EXP_SCALE), 0.0))
        total[h] = (expos[0] + expos[1]) + (expos[2] + expos[3])
        weights = [e.astype(BF16) for e in expos]
        acc[h] = jnp.dot(
            jnp.concatenate(weights[:2], axis=1), v_before, preferred_element_type=F32
        ) + jnp.dot(jnp.concatenate(weights[2:], axis=1), v_ref[st], preferred_element_type=F32)

    def step(masked, g, _):
        keys = keys_ref[pl.ds(g * GROUP, GROUP)].reshape(SPAN, HEAD)
        values = vals[pl.ds(g * GROUP, GROUP)].reshape(SPAN, HEAD)
        ok = causal(blk_ref, s, g) if masked else None
        for h in range(HEADS):
            scores = dot_t(q_ref[0, :, h * HEAD : (h + 1) * HEAD], keys)
            expos = []
            for n in range(GROUP):
                part = jnp.exp2((scores[:, n * BLOCK : (n + 1) * BLOCK] - top_ref[0, h]) * EXP_SCALE)
                expos.append(jnp.where(ok[n], part, 0.0) if masked else part)
            total[h] += functools.reduce(jnp.add, expos)
            weights = jnp.concatenate([e.astype(BF16) for e in expos], axis=1)
            acc[h] += jnp.dot(weights, values, preferred_element_type=F32)
        return 0

    lax.fori_loop(0, plain, functools.partial(step, False), 0)
    lax.fori_loop(plain, groups, functools.partial(step, True), 0)
    for h in range(HEADS):
        row = jnp.sum(total[h], axis=1, keepdims=True)
        out_ref[:, h * HEAD : (h + 1) * HEAD] = (acc[h] / row).astype(BF16)


def mix_kernel(a0, a1, a2, a3, w0, w1, w2, w3, *refs):
    out_ref = refs[-1]
    sums = [jnp.dot(a[...], w[...], preferred_element_type=F32) for a, w in ((a0, w0), (a1, w1), (a2, w2), (a3, w3))]
    out_ref[0] = ((sums[0] + sums[1]) + (sums[2] + sums[3])).astype(BF16)


def from_ahead(x, axis, shift):
    n = lax.axis_size(axis)
    return lax.ppermute(x, axis, [((i + shift) % n, i) for i in range(n)])


def line_kernel(*refs):
    pieces, out_ref = refs[:X_CHIPS], refs[-1]
    for n, ref in enumerate(pieces):
        for which in range(2):
            out_ref[which, n * CAP : (n + 1) * CAP] = ref[which]


def chip_kernel(which, own_ref, other_ref, *refs):
    count = own_ref.shape[1]
    refs[-1][:count] = own_ref[which]
    refs[-1][count:] = other_ref[which]


def copy_kernel(source_ref, out_ref):
    out_ref[...] = source_ref[...]


def gather_columns(nx, nz, payload):
    place = lambda x, z, c: ((x % nx) * nz + z % nz) * 2 + c
    every = [(x, z, c) for x in range(nx) for z in range(nz) for c in range(2)]
    route = lambda f: [(place(*d), place(*f(*d))) for d in every]
    across = route(lambda x, z, c: (x, z, 1 - c))
    along = route(lambda x, z, c: (x, z + 1 - 2 * c, c))
    send = lambda a, r: lax.ppermute(a, "ctx", r)

    shape = jax.ShapeDtypeStruct
    call = functools.partial(pl.pallas_call, compiler_params=PARAMS)
    size = nx * CAP
    line = [payload] + [send(payload, route(lambda x, z, c, n=n: (x - n, z, c))) for n in range(1, nx)]
    own = call(
        line_kernel,
        out_shape=shape((2, size, BLOCK, HEAD), BF16),
        in_specs=[VMEM()] * nx,
        out_specs=VMEM(),
        name="line",
    )(*line)
    other = send(own, across)
    pieces = []
    waited = []
    for which in range(2):
        moving = call(
            functools.partial(chip_kernel, which),
            out_shape=shape((2 * size, BLOCK, HEAD), BF16),
            in_specs=[VMEM()] * 2 + [ANY()] * len(waited),
            out_specs=VMEM(),
            name=f"chip{which}",
        )(own, other, *waited)
        held = [moving]
        for n in range(1, nz // 2 + 1):
            last = n == nz // 2
            if which == 0 and last:
                moving = call(
                    copy_kernel,
                    grid=(1,),
                    out_shape=shape((size, BLOCK, HEAD), BF16),
                    in_specs=[pl.BlockSpec((size, BLOCK, HEAD), lambda i: (0, 0, 0))],
                    out_specs=VMEM(),
                    name="half",
                )(moving)
            moving = send(moving, along)
            held += [moving] + ([] if which == 1 and last else [send(moving, across)])
            if n == 1:
                waited = [moving]
        pieces.append(held)
    return pieces


def arrivals(nx, nz, halves, me, entry):
    x, z, c = lax.div(me, 2 * nz), lax.rem(lax.div(me, 2), nz), lax.rem(me, 2)
    size = nx * CAP
    at = entry % (2 * size)
    piece = entry // (2 * size)
    hops = jnp.where(piece == 0, 0, (piece + 1) // 2)
    mirrored = jnp.where(piece == 0, 0, (piece + 1) % 2)
    half = at // size
    if halves:
        last = piece == nz - 1
        mirrored, half = jnp.where(last, half, mirrored), jnp.where(last, 0, half)
    side = jnp.where(mirrored == 1, 1 - 2 * c, 2 * c - 1) * hops
    core = jnp.where(mirrored == half, c, 1 - c)
    line = at % size // CAP
    return (((x + line) % nx * nz + (z + nz + side) % nz) * 2 + core) * CAP + at % CAP


def slab_kernel(tp, shifts, index_ref, weight_ref, *refs):
    width = weight_ref.shape[1] // tp
    for shift, ref in zip(shifts, refs[-len(shifts):]):
        target = lax.rem(index_ref[0] + tp - shift, tp)
        ref[...] = weight_ref[:, pl.ds(pl.multiple_of(target * width, width), width)]


def cost(us):
    return pl.CostEstimate(flops=0, bytes_accessed=int(us * 3.0e6), transcendentals=0)


def per_device(queries, keys, values, column_block_table, slash_offsets, out_weight):
    ctx_count = lax.axis_size("ctx")
    tp = lax.axis_size("tp")
    me = lax.axis_index("ctx").reshape(1).astype(jnp.int32)
    tp_index = lax.axis_index("tp")
    q, k, v = queries[0], keys[0], values[0]
    shape = jax.ShapeDtypeStruct
    i32 = jnp.int32

    payload, ahead, back = pl.pallas_call(
        functools.partial(pack_kernel, ctx_count),
        out_shape=[shape((2, CAP, BLOCK, HEAD), BF16)] + [shape((2, STRETCH, HEAD), BF16)] * 2,
        in_specs=[SMEM(), VMEM(), VMEM(), VMEM()],
        out_specs=[VMEM()] * 3,
        compiler_params=PARAMS,
        name="pack",
    )(me, column_block_table, k.reshape(4, BLOCK, HEAD), v.reshape(4, BLOCK, HEAD))

    sides = (X_CHIPS, ctx_count // (2 * X_CHIPS))
    blk, key_at, val_at, meta = pl.pallas_call(
        functools.partial(plan_kernel, ctx_count, sides),
        out_shape=[shape((1, LISTED), i32)] + [shape((1, CAP * ctx_count), i32)] * 2 + [shape((1, 16), i32)],
        in_specs=[SMEM(), VMEM(), VMEM()],
        out_specs=[VMEM()] * 4,
        compiler_params=PARAMS,
        cost_estimate=cost(2),
        name="plan",
    )(me, column_block_table, column_block_table.reshape(LISTED, 1))

    steps = range(ctx_count - 1)
    before = lax.ppermute(ahead, "ctx", [(i, i + 1) for i in steps])
    after = lax.ppermute(back, "ctx", [(i + 1, i) for i in steps])

    mask, top = pl.pallas_call(
        functools.partial(band_kernel, ctx_count),
        out_shape=[shape((HEADS, STRETCH, 2 * STRETCH), F32), shape((2, HEADS, STRETCH, BLOCK), F32)],
        in_specs=[SMEM(), SMEM(), VMEM(), VMEM(), VMEM(), VMEM()],
        out_specs=[VMEM(), VMEM()],
        compiler_params=PARAMS,
        cost_estimate=cost(3),
        name="band",
    )(meta, slash_offsets, q, k, before, after)

    k_pieces, v_pieces = gather_columns(*sides, payload)

    width = out_weight.shape[1] // tp
    depth = out_weight.shape[0]
    slabs = {}
    for shifts, earlier in (((0, 1, 3), v_pieces[0]), ((2,), mask)):
        cut = pl.pallas_call(
            functools.partial(slab_kernel, tp, shifts),
            grid=(depth // 128,),
            out_shape=[shape((depth, width), BF16)] * len(shifts),
            in_specs=[SMEM(), pl.BlockSpec((128, out_weight.shape[1]), lambda i: (i, 0)), ANY()],
            out_specs=[pl.BlockSpec((128, width), lambda i: (i, 0))] * len(shifts),
            compiler_params=PARAMS,
            cost_estimate=cost(len(shifts)),
            name=f"slabs{shifts[0]}",
        )(tp_index.reshape(1).astype(i32), out_weight, earlier)
        slabs.update(zip(shifts, cut))
    slabs = [slabs[0]] + [from_ahead(slabs[shift], "tp", shift) for shift in range(1, tp)]

    columns, top = pl.pallas_call(
        top_kernel,
        out_shape=[shape((ROOM, BLOCK, HEAD), BF16), shape((2, HEADS, STRETCH, BLOCK), F32)],
        in_specs=[SMEM(), SMEM(), SMEM(), VMEM(), VMEM()] + [VMEM()] * len(k_pieces),
        out_specs=[VMEM(), VMEM()],
        compiler_params=PARAMS,
        cost_estimate=cost(9),
        name="top",
    )(meta, blk, key_at, q, top, *k_pieces)

    mixed = column_vals = None
    for st in range(2):
        first = st == 0
        extra = [*v_pieces, slabs[1], slabs[3]] if first else [column_vals]
        result = pl.pallas_call(
            functools.partial(out_kernel, ctx_count, st, len(v_pieces) if first else 0),
            grid=(1,),
            out_shape=[shape((STRETCH, HEADS * HEAD), BF16)] + [shape((ROOM, BLOCK, HEAD), BF16)] * first,
            in_specs=[
                SMEM(), SMEM(), SMEM(),
                pl.BlockSpec((1, STRETCH, HEADS * HEAD), lambda i, st=st: (st, 0, 0)),
                VMEM(),
                pl.BlockSpec((1, HEADS, STRETCH, BLOCK), lambda i, st=st: (st, 0, 0, 0)),
                VMEM(), VMEM(), VMEM(), VMEM(), VMEM(),
            ] + ([VMEM()] * len(v_pieces) + [ANY()] * 2 if first else [VMEM()]),
            out_specs=[VMEM()] * (1 + first),
            scratch_shapes=[
                pltpu.VMEM((HEADS, STRETCH, BLOCK), F32),
                pltpu.VMEM((HEADS, STRETCH, HEAD), F32),
            ],
            compiler_params=PARAMS,
            cost_estimate=cost(8),
            name=f"attend{st}",
        )(meta, blk, val_at, q, columns, top, mask, k, v, before, after, *extra)
        head_out = result[0]
        if first:
            column_vals = result[1]
        parts = [head_out] + [from_ahead(head_out, "tp", shift) for shift in range(1, tp)]
        tile = width // 4
        mixed = pl.pallas_call(
            mix_kernel,
            grid=(width // tile,),
            out_shape=shape((2, STRETCH, width), BF16),
            in_specs=[VMEM()] * 4
            + [pl.BlockSpec((HEADS * HEAD, tile), lambda i: (0, i))] * 4
            + ([ANY()] if st else []),
            out_specs=pl.BlockSpec((1, STRETCH, tile), lambda i, st=st: (st, 0, i)),
            input_output_aliases={8: 0} if st else {},
            compiler_params=PARAMS,
            cost_estimate=cost(3),
            name=f"mix{st}",
        )(*parts, *slabs, *([mixed] if st else []))
    return mixed[None]


def solution(mesh):
    in_specs = (
        P("ctx", None, None, "tp"),
        P("ctx", None, None, "tp"),
        P("ctx", None, None, "tp"),
        P("tp", None),
        P("tp", None),
        P("tp", None),
    )
    out_specs = P("ctx", None, None, "tp")
    return jax.shard_map(
        per_device, mesh=mesh, in_specs=in_specs, out_specs=out_specs, check_vma=False
    )
```

```python
import functools
import math

import jax
import jax.numpy as jnp
from jax import lax
from jax.experimental import pallas as pl
from jax.experimental.pallas import tpu as pltpu
from jax.sharding import PartitionSpec as P

HEAD = 128
BLOCK = 128
STRETCH = 256
CAP = 2
GROUP = 8
SPAN = GROUP * BLOCK
LISTED = 64
ROOM = LISTED + 1
UNROLL = 4
X_CHIPS = 4
HEADS = 4
EXP_SCALE = math.log2(math.e) * HEAD ** (-0.5)
VMEM_LIMIT = 48 * 1024 * 1024

SMEM = functools.partial(pl.BlockSpec, memory_space=pltpu.SMEM)
VMEM = functools.partial(pl.BlockSpec, memory_space=pltpu.VMEM)
ANY = functools.partial(pl.BlockSpec, memory_space=pl.ANY)
PARAMS = pltpu.CompilerParams(vmem_limit_bytes=VMEM_LIMIT)
F32 = jnp.float32
BF16 = jnp.bfloat16


def dot_t(a, b):
    return lax.dot_general(a, b, (((1,), (1,)), ((), ())), preferred_element_type=F32)


def pack_kernel(ctx_count, me_ref, table_ref, k_ref, v_ref, pay_ref, ahead_ref, back_ref):
    me = me_ref[0]
    table = table_ref[...]
    owner = owned(table, ctx_count)
    local = jnp.where(table // 2 < ctx_count, 0, 2) + table % 2
    at = lax.broadcasted_iota(jnp.int32, table.shape, 1)
    mine = owner == me
    for slot in range(CAP):
        found = jnp.min(jnp.where(mine, at, LISTED))
        loc = jnp.sum(jnp.where(at == found, local, 0))
        mine = mine & (at > found)
        pay_ref[0, slot] = k_ref[loc]
        pay_ref[1, slot] = v_ref[loc]
    for half, ref in ((0, ahead_ref), (1, back_ref)):
        for part in range(2):
            ref[0, part * BLOCK : (part + 1) * BLOCK] = k_ref[2 * half + part]
            ref[1, part * BLOCK : (part + 1) * BLOCK] = v_ref[2 * half + part]


def owned(table, ctx_count):
    stretch = table // 2
    return jnp.where(stretch < ctx_count, stretch, 2 * ctx_count - 1 - stretch)


def plan_kernel(ctx_count, sides, me_ref, row_ref, col_ref, blk_ref, key_at_ref, val_at_ref, meta_ref):
    me = me_ref[0]
    row, col = row_ref[...], col_ref[...]
    square = (LISTED, LISTED)
    iota = lax.broadcasted_iota
    total = functools.partial(jnp.sum, keepdims=True)
    pick = lambda test, value, axis: total(jnp.where(test, value, 0), axis=axis)
    place = pick(row < col, jnp.int32(1), 1)
    earlier = iota(jnp.int32, square, 1) < iota(jnp.int32, square, 0)
    owner = owned(col, ctx_count)
    rank = pick((owned(row, ctx_count) == owner) & earlier, jnp.int32(1), 1)
    blk_ref[...] = pick(place == iota(jnp.int32, square, 1), col, 0)
    for halves, ref in ((True, key_at_ref), (False, val_at_ref)):
        entry = arrivals(*sides, halves, me, iota(jnp.int32, (1, CAP * ctx_count), 1))
        ref[...] = LISTED + pick(owner * CAP + rank == entry, place - LISTED, 0)
    lane = iota(jnp.int32, (1, 16), 1)
    meta = jnp.where(lane % 8 == 3, me, 0)
    for st, s in enumerate((me, 2 * ctx_count - 1 - me)):
        found = [jnp.sum(jnp.where(row < 2 * s, 1, 0)), jnp.sum(jnp.where(row <= 2 * s + 1, 1, 0)), s]
        for n, value in enumerate(found):
            meta = jnp.where(lane == 8 * st + n, value, meta)
        for n in range(4):
            b = 2 * (s - 1) + n
            free = 1 - jnp.max(jnp.where(row == b, 1, 0))
            meta = jnp.where(lane == 8 * st + 4 + n, jnp.where(b >= 0, free, 0), meta)
    meta_ref[...] = meta


def band_halves(own_ref, ahead_ref, back_ref, which, st, me, ctx_count):
    if st == 0:
        return ahead_ref[which]
    return jnp.where(me == ctx_count - 1, own_ref[0], back_ref[which])


def band_kernel(ctx_count, meta_ref, slash_ref, q_ref, k_ref, ahead_ref, back_ref, mask_ref, top_ref):
    behind = STRETCH - lax.broadcasted_iota(jnp.int32, (8, 2 * STRETCH), 1)
    for h in range(HEADS):
        def listed(n, hit):
            return hit | (behind == slash_ref[h, n])

        hit = behind == 0
        for n in range(LISTED):
            hit = listed(n, hit)
        row = jnp.where(hit, 1.0, 0.0).astype(F32)[:1]
        spread = jnp.broadcast_to(row, (STRETCH, 2 * STRETCH))
        mask_ref[h] = pltpu.roll(spread, 0, 1, stride=1, stride_axis=0)
    me = meta_ref[0, 3]
    for st in range(2):
        before = band_halves(k_ref, ahead_ref, back_ref, 0, st, me, ctx_count)
        for h in range(HEADS):
            q = q_ref[st, :, h * HEAD : (h + 1) * HEAD]
            top = jnp.full((STRETCH, BLOCK), -jnp.inf, F32)
            for n in range(4):
                part = before if n < 2 else k_ref[st]
                s = dot_t(q, part[(n % 2) * BLOCK : (n % 2 + 1) * BLOCK])
                ok = (mask_ref[h, :, n * BLOCK : (n + 1) * BLOCK] > 0.5) & (meta_ref[0, 8 * st + 4 + n] > 0)
                top = jnp.maximum(top, jnp.where(ok, s, -jnp.inf))
            top_ref[st, h] = top


def fetch(at_ref, pieces, target_ref):
    base = 0
    for ref in pieces:
        def copy(i, _, ref=ref, base=base):
            for n in range(UNROLL):
                target_ref[at_ref[0, base + i * UNROLL + n]] = ref[i * UNROLL + n]
            return 0

        lax.fori_loop(0, ref.shape[0] // UNROLL, copy, 0)
        base += ref.shape[0]


def causal(blk_ref, s, g):
    lead = lax.broadcasted_iota(jnp.int32, (STRETCH, BLOCK), 1) - lax.broadcasted_iota(jnp.int32, (STRETCH, BLOCK), 0)
    return [lead <= s * STRETCH - blk_ref[0, g * GROUP + n] * BLOCK for n in range(GROUP)]


def top_kernel(meta_ref, blk_ref, at_ref, q_ref, top_in_ref, *refs):
    pieces, (keys_ref, top_ref) = refs[:-2], refs[-2:]
    fetch(at_ref, pieces, keys_ref)
    for st in range(2):
        full, seen, s = meta_ref[0, 8 * st], meta_ref[0, 8 * st + 1], meta_ref[0, 8 * st + 2]
        plain, groups = full // GROUP, (seen + GROUP - 1) // GROUP
        for h in range(HEADS):
            top_ref[st, h] = top_in_ref[st, h]

        def step(masked, g, _):
            keys = keys_ref[pl.ds(g * GROUP, GROUP)].reshape(SPAN, HEAD)
            ok = causal(blk_ref, s, g) if masked else None
            for h in range(HEADS):
                scores = dot_t(q_ref[st, :, h * HEAD : (h + 1) * HEAD], keys)
                tops = []
                for n in range(GROUP):
                    part = scores[:, n * BLOCK : (n + 1) * BLOCK]
                    tops.append(jnp.where(ok[n], part, -jnp.inf) if masked else part)
                top = functools.reduce(jnp.maximum, tops)
                top_ref[st, h] = jnp.maximum(top_ref[st, h], top)
            return 0

        lax.fori_loop(0, plain, functools.partial(step, False), 0)
        lax.fori_loop(plain, groups, functools.partial(step, True), 0)
        for h in range(HEADS):
            row = jnp.max(top_ref[st, h], axis=1, keepdims=True)
            top_ref[st, h] = jnp.broadcast_to(row, (STRETCH, BLOCK))


def out_kernel(ctx_count, st, arriving, meta_ref, blk_ref, at_ref, q_ref, keys_ref, top_ref, mask_ref, k_ref, v_ref, ahead_ref, back_ref, *refs):
    full, seen, s = meta_ref[0, 8 * st], meta_ref[0, 8 * st + 1], meta_ref[0, 8 * st + 2]
    me = meta_ref[0, 8 * st + 3]
    plain, groups = full // GROUP, (seen + GROUP - 1) // GROUP
    if arriving:
        pieces, (out_ref, vals, total, acc) = refs[:arriving], refs[-4:]
        fetch(at_ref, pieces, vals)
    else:
        vals, out_ref, total, acc = refs
    k_before = band_halves(k_ref, ahead_ref, back_ref, 0, st, me, ctx_count)
    v_before = band_halves(v_ref, ahead_ref, back_ref, 1, st, me, ctx_count)

    for h in range(HEADS):
        q = q_ref[0, :, h * HEAD : (h + 1) * HEAD]
        scores = [dot_t(q, k_before), dot_t(q, k_ref[st])]
        expos = []
        for n in range(4):
            part = scores[n // 2][:, (n % 2) * BLOCK : (n % 2 + 1) * BLOCK]
            ok = (mask_ref[h, :, n * BLOCK : (n + 1) * BLOCK] > 0.5) & (meta_ref[0, 8 * st + 4 + n] > 0)
            expos.append(jnp.where(ok, jnp.exp2((part - top_ref[0, h]) * EXP_SCALE), 0.0))
        total[h] = (expos[0] + expos[1]) + (expos[2] + expos[3])
        weights = [e.astype(BF16) for e in expos]
        acc[h] = jnp.dot(
            jnp.concatenate(weights[:2], axis=1), v_before, preferred_element_type=F32
        ) + jnp.dot(jnp.concatenate(weights[2:], axis=1), v_ref[st], preferred_element_type=F32)

    def step(masked, g, _):
        keys = keys_ref[pl.ds(g * GROUP, GROUP)].reshape(SPAN, HEAD)
        values = vals[pl.ds(g * GROUP, GROUP)].reshape(SPAN, HEAD)
        ok = causal(blk_ref, s, g) if masked else None
        for h in range(HEADS):
            scores = dot_t(q_ref[0, :, h * HEAD : (h + 1) * HEAD], keys)
            expos = []
            for n in range(GROUP):
                part = jnp.exp2((scores[:, n * BLOCK : (n + 1) * BLOCK] - top_ref[0, h]) * EXP_SCALE)
                expos.append(jnp.where(ok[n], part, 0.0) if masked else part)
            total[h] += functools.reduce(jnp.add, expos)
            weights = jnp.concatenate([e.astype(BF16) for e in expos], axis=1)
            acc[h] += jnp.dot(weights, values, preferred_element_type=F32)
        return 0

    lax.fori_loop(0, plain, functools.partial(step, False), 0)
    lax.fori_loop(plain, groups, functools.partial(step, True), 0)
    for h in range(HEADS):
        row = jnp.sum(total[h], axis=1, keepdims=True)
        out_ref[:, h * HEAD : (h + 1) * HEAD] = (acc[h] / row).astype(BF16)


def mix_kernel(a0, a1, a2, a3, w0, w1, w2, w3, *refs):
    out_ref = refs[-1]
    sums = [jnp.dot(a[...], w[...], preferred_element_type=F32) for a, w in ((a0, w0), (a1, w1), (a2, w2), (a3, w3))]
    out_ref[0] = ((sums[0] + sums[1]) + (sums[2] + sums[3])).astype(BF16)


def from_ahead(x, axis, shift):
    n = lax.axis_size(axis)
    return lax.ppermute(x, axis, [((i + shift) % n, i) for i in range(n)])


def line_kernel(*refs):
    pieces, out_ref = refs[:X_CHIPS], refs[-1]
    for n, ref in enumerate(pieces):
        for which in range(2):
            out_ref[which, n * CAP : (n + 1) * CAP] = ref[which]


def chip_kernel(which, own_ref, other_ref, *refs):
    count = own_ref.shape[1]
    refs[-1][:count] = own_ref[which]
    refs[-1][count:] = other_ref[which]


def copy_kernel(source_ref, *refs):
    refs[-1][...] = source_ref[...]


def gather_columns(nx, nz, payload, later):
    place = lambda x, z, c: ((x % nx) * nz + z % nz) * 2 + c
    every = [(x, z, c) for x in range(nx) for z in range(nz) for c in range(2)]
    route = lambda f: [(place(*d), place(*f(*d))) for d in every]
    across = route(lambda x, z, c: (x, z, 1 - c))
    along = route(lambda x, z, c: (x, z + 1 - 2 * c, c))
    send = lambda a, r: lax.ppermute(a, "ctx", r)

    shape = jax.ShapeDtypeStruct
    call = functools.partial(pl.pallas_call, compiler_params=PARAMS)
    size = nx * CAP
    line = [payload] + [send(payload, route(lambda x, z, c, n=n: (x - n, z, c))) for n in range(1, nx)]
    own = call(
        line_kernel,
        out_shape=shape((2, size, BLOCK, HEAD), BF16),
        in_specs=[VMEM()] * nx,
        out_specs=VMEM(),
        name="line",
    )(*line)
    other = send(own, across)
    pieces = []
    waited = []
    for which in range(2):
        moving = call(
            functools.partial(chip_kernel, which),
            out_shape=shape((2 * size, BLOCK, HEAD), BF16),
            in_specs=[VMEM()] * 2 + [ANY()] * len(waited),
            out_specs=VMEM(),
            name=f"chip{which}",
        )(own, other, *waited)
        held = [moving]
        for n in range(1, nz // 2 + 1):
            last = n == nz // 2
            if which == 0 and last:
                moving = call(
                    copy_kernel,
                    grid=(1,),
                    out_shape=shape((size, BLOCK, HEAD), BF16),
                    in_specs=[pl.BlockSpec((size, BLOCK, HEAD), lambda i: (0, 0, 0))] + [ANY()] * len(later),
                    out_specs=VMEM(),
                    name="half",
                )(moving, *later)
            moving = send(moving, along)
            held += [moving] + ([] if which == 1 and last else [send(moving, across)])
            if n == 1:
                waited = [moving]
        pieces.append(held)
    return pieces


def arrivals(nx, nz, halves, me, entry):
    x, z, c = lax.div(me, 2 * nz), lax.rem(lax.div(me, 2), nz), lax.rem(me, 2)
    size = nx * CAP
    at = entry % (2 * size)
    piece = entry // (2 * size)
    hops = jnp.where(piece == 0, 0, (piece + 1) // 2)
    mirrored = jnp.where(piece == 0, 0, (piece + 1) % 2)
    half = at // size
    if halves:
        last = piece == nz - 1
        mirrored, half = jnp.where(last, half, mirrored), jnp.where(last, 0, half)
    side = jnp.where(mirrored == 1, 1 - 2 * c, 2 * c - 1) * hops
    core = jnp.where(mirrored == half, c, 1 - c)
    line = at % size // CAP
    return (((x + line) % nx * nz + (z + nz + side) % nz) * 2 + core) * CAP + at % CAP


def slab_kernel(tp, index_ref, weight_ref, *refs):
    width = weight_ref.shape[1] // tp
    for shift, ref in enumerate(refs[-tp:]):
        target = lax.rem(index_ref[0] + tp - shift, tp)
        ref[...] = weight_ref[:, pl.ds(pl.multiple_of(target * width, width), width)]


def cost(us):
    return pl.CostEstimate(flops=0, bytes_accessed=int(us * 3.0e6), transcendentals=0)


def per_device(queries, keys, values, column_block_table, slash_offsets, out_weight):
    ctx_count = lax.axis_size("ctx")
    tp = lax.axis_size("tp")
    me = lax.axis_index("ctx").reshape(1).astype(jnp.int32)
    tp_index = lax.axis_index("tp")
    q, k, v = queries[0], keys[0], values[0]
    shape = jax.ShapeDtypeStruct
    i32 = jnp.int32

    payload, ahead, back = pl.pallas_call(
        functools.partial(pack_kernel, ctx_count),
        out_shape=[shape((2, CAP, BLOCK, HEAD), BF16)] + [shape((2, STRETCH, HEAD), BF16)] * 2,
        in_specs=[SMEM(), VMEM(), VMEM(), VMEM()],
        out_specs=[VMEM()] * 3,
        compiler_params=PARAMS,
        name="pack",
    )(me, column_block_table, k.reshape(4, BLOCK, HEAD), v.reshape(4, BLOCK, HEAD))

    sides = (X_CHIPS, ctx_count // (2 * X_CHIPS))
    blk, key_at, val_at, meta = pl.pallas_call(
        functools.partial(plan_kernel, ctx_count, sides),
        out_shape=[shape((1, LISTED), i32)] + [shape((1, CAP * ctx_count), i32)] * 2 + [shape((1, 16), i32)],
        in_specs=[SMEM(), VMEM(), VMEM()],
        out_specs=[VMEM()] * 4,
        compiler_params=PARAMS,
        cost_estimate=cost(2),
        name="plan",
    )(me, column_block_table, column_block_table.reshape(LISTED, 1))

    steps = range(ctx_count - 1)
    before = lax.ppermute(ahead, "ctx", [(i, i + 1) for i in steps])
    after = lax.ppermute(back, "ctx", [(i + 1, i) for i in steps])

    mask, top = pl.pallas_call(
        functools.partial(band_kernel, ctx_count),
        out_shape=[shape((HEADS, STRETCH, 2 * STRETCH), F32), shape((2, HEADS, STRETCH, BLOCK), F32)],
        in_specs=[SMEM(), SMEM(), VMEM(), VMEM(), VMEM(), VMEM()],
        out_specs=[VMEM(), VMEM()],
        compiler_params=PARAMS,
        cost_estimate=cost(3),
        name="band",
    )(meta, slash_offsets, q, k, before, after)

    k_pieces, v_pieces = gather_columns(*sides, payload, [mask])

    width = out_weight.shape[1] // tp
    depth = out_weight.shape[0]
    slabs = pl.pallas_call(
        functools.partial(slab_kernel, tp),
        grid=(depth // 128,),
        out_shape=[shape((depth, width), BF16)] * tp,
        in_specs=[SMEM(), pl.BlockSpec((128, out_weight.shape[1]), lambda i: (i, 0))] + [ANY()] * 3,
        out_specs=[pl.BlockSpec((128, width), lambda i: (i, 0))] * tp,
        compiler_params=PARAMS,
        cost_estimate=cost(3),
        name="slabs",
    )(tp_index.reshape(1).astype(i32), out_weight, v_pieces[0], before, after)
    slabs = [slabs[0]] + [from_ahead(slabs[shift], "tp", shift) for shift in range(1, tp)]

    columns, top = pl.pallas_call(
        top_kernel,
        out_shape=[shape((ROOM, BLOCK, HEAD), BF16), shape((2, HEADS, STRETCH, BLOCK), F32)],
        in_specs=[SMEM(), SMEM(), SMEM(), VMEM(), VMEM()] + [VMEM()] * len(k_pieces),
        out_specs=[VMEM(), VMEM()],
        compiler_params=PARAMS,
        cost_estimate=cost(9),
        name="top",
    )(meta, blk, key_at, q, top, *k_pieces)

    mixed = column_vals = None
    for st in range(2):
        first = st == 0
        extra = [*v_pieces, slabs[1], slabs[3]] if first else [column_vals]
        result = pl.pallas_call(
            functools.partial(out_kernel, ctx_count, st, len(v_pieces) if first else 0),
            grid=(1,),
            out_shape=[shape((STRETCH, HEADS * HEAD), BF16)] + [shape((ROOM, BLOCK, HEAD), BF16)] * first,
            in_specs=[
                SMEM(), SMEM(), SMEM(),
                pl.BlockSpec((1, STRETCH, HEADS * HEAD), lambda i, st=st: (st, 0, 0)),
                VMEM(),
                pl.BlockSpec((1, HEADS, STRETCH, BLOCK), lambda i, st=st: (st, 0, 0, 0)),
                VMEM(), VMEM(), VMEM(), VMEM(), VMEM(),
            ] + ([VMEM()] * len(v_pieces) + [ANY()] * 2 if first else [VMEM()]),
            out_specs=[VMEM()] * (1 + first),
            scratch_shapes=[
                pltpu.VMEM((HEADS, STRETCH, BLOCK), F32),
                pltpu.VMEM((HEADS, STRETCH, HEAD), F32),
            ],
            compiler_params=PARAMS,
            cost_estimate=cost(8),
            name=f"attend{st}",
        )(meta, blk, val_at, q, columns, top, mask, k, v, before, after, *extra)
        head_out = result[0]
        if first:
            column_vals = result[1]
        parts = [head_out] + [from_ahead(head_out, "tp", shift) for shift in range(1, tp)]
        tile = width // 4
        mixed = pl.pallas_call(
            mix_kernel,
            grid=(width // tile,),
            out_shape=shape((2, STRETCH, width), BF16),
            in_specs=[VMEM()] * 4
            + [pl.BlockSpec((HEADS * HEAD, tile), lambda i: (0, i))] * 4
            + ([ANY()] if st else []),
            out_specs=pl.BlockSpec((1, STRETCH, tile), lambda i, st=st: (st, 0, i)),
            input_output_aliases={8: 0} if st else {},
            compiler_params=PARAMS,
            cost_estimate=cost(3),
            name=f"mix{st}",
        )(*parts, *slabs, *([mixed] if st else []))
    return mixed[None]


def solution(mesh):
    in_specs = (
        P("ctx", None, None, "tp"),
        P("ctx", None, None, "tp"),
        P("ctx", None, None, "tp"),
        P("tp", None),
        P("tp", None),
        P("tp", None),
    )
    out_specs = P("ctx", None, None, "tp")
    return jax.shard_map(
        per_device, mesh=mesh, in_specs=in_specs, out_specs=out_specs, check_vma=False
    )
```

```python
import functools
import math

import jax
import jax.numpy as jnp
from jax import lax
from jax.experimental import pallas as pl
from jax.experimental.pallas import tpu as pltpu
from jax.sharding import PartitionSpec as P

HEAD = 128
BLOCK = 128
STRETCH = 256
CAP = 2
GROUP = 8
SPAN = GROUP * BLOCK
LISTED = 64
ROOM = LISTED + 1
UNROLL = 4
X_CHIPS = 4
HEADS = 4
EXP_SCALE = math.log2(math.e) * HEAD ** (-0.5)
VMEM_LIMIT = 24 * 1024 * 1024

SMEM = functools.partial(pl.BlockSpec, memory_space=pltpu.SMEM)
VMEM = functools.partial(pl.BlockSpec, memory_space=pltpu.VMEM)
ANY = functools.partial(pl.BlockSpec, memory_space=pl.ANY)
PARAMS = pltpu.CompilerParams(vmem_limit_bytes=VMEM_LIMIT)
F32 = jnp.float32
BF16 = jnp.bfloat16


def dot_t(a, b):
    return lax.dot_general(a, b, (((1,), (1,)), ((), ())), preferred_element_type=F32)


def pack_kernel(ctx_count, me_ref, table_ref, k_ref, v_ref, pay_ref, ahead_ref, back_ref):
    me = me_ref[0]
    table = table_ref[...]
    owner = owned(table, ctx_count)
    local = jnp.where(table // 2 < ctx_count, 0, 2) + table % 2
    at = lax.broadcasted_iota(jnp.int32, table.shape, 1)
    mine = owner == me
    for slot in range(CAP):
        found = jnp.min(jnp.where(mine, at, LISTED))
        loc = jnp.sum(jnp.where(at == found, local, 0))
        mine = mine & (at > found)
        pay_ref[0, slot] = k_ref[loc]
        pay_ref[1, slot] = v_ref[loc]
    for half, ref in ((0, ahead_ref), (1, back_ref)):
        for part in range(2):
            ref[0, part * BLOCK : (part + 1) * BLOCK] = k_ref[2 * half + part]
            ref[1, part * BLOCK : (part + 1) * BLOCK] = v_ref[2 * half + part]


def owned(table, ctx_count):
    stretch = table // 2
    return jnp.where(stretch < ctx_count, stretch, 2 * ctx_count - 1 - stretch)


def plan_kernel(ctx_count, sides, me_ref, row_ref, col_ref, blk_ref, key_at_ref, val_at_ref, meta_ref):
    me = me_ref[0]
    row, col = row_ref[...], col_ref[...]
    square = (LISTED, LISTED)
    iota = lax.broadcasted_iota
    total = functools.partial(jnp.sum, keepdims=True)
    pick = lambda test, value, axis: total(jnp.where(test, value, 0), axis=axis)
    place = pick(row < col, jnp.int32(1), 1)
    earlier = iota(jnp.int32, square, 1) < iota(jnp.int32, square, 0)
    owner = owned(col, ctx_count)
    rank = pick((owned(row, ctx_count) == owner) & earlier, jnp.int32(1), 1)
    blk_ref[...] = pick(place == iota(jnp.int32, square, 1), col, 0)
    for halves, ref in ((True, key_at_ref), (False, val_at_ref)):
        entry = arrivals(*sides, halves, me, iota(jnp.int32, (1, CAP * ctx_count), 1))
        ref[...] = LISTED + pick(owner * CAP + rank == entry, place - LISTED, 0)
    lane = iota(jnp.int32, (1, 16), 1)
    meta = jnp.where(lane % 8 == 3, me, 0)
    for st, s in enumerate((me, 2 * ctx_count - 1 - me)):
        found = [jnp.sum(jnp.where(row < 2 * s, 1, 0)), jnp.sum(jnp.where(row <= 2 * s + 1, 1, 0)), s]
        for n, value in enumerate(found):
            meta = jnp.where(lane == 8 * st + n, value, meta)
        for n in range(4):
            b = 2 * (s - 1) + n
            free = 1 - jnp.max(jnp.where(row == b, 1, 0))
            meta = jnp.where(lane == 8 * st + 4 + n, jnp.where(b >= 0, free, 0), meta)
    meta_ref[...] = meta


def band_halves(own_ref, ahead_ref, back_ref, which, st, me, ctx_count):
    if st == 0:
        return ahead_ref[which]
    return jnp.where(me == ctx_count - 1, own_ref[0], back_ref[which])


def band_kernel(ctx_count, meta_ref, slash_ref, q_ref, k_ref, ahead_ref, back_ref, mask_ref, top_ref):
    behind = STRETCH - lax.broadcasted_iota(jnp.int32, (8, 2 * STRETCH), 1)
    for h in range(HEADS):
        def listed(n, hit):
            return hit | (behind == slash_ref[h, n])

        hit = behind == 0
        for n in range(LISTED):
            hit = listed(n, hit)
        row = jnp.where(hit, 1.0, 0.0).astype(F32)[:1]
        spread = jnp.broadcast_to(row, (STRETCH, 2 * STRETCH))
        mask_ref[h] = pltpu.roll(spread, 0, 1, stride=1, stride_axis=0)
    me = meta_ref[0, 3]
    for st in range(2):
        before = band_halves(k_ref, ahead_ref, back_ref, 0, st, me, ctx_count)
        for h in range(HEADS):
            q = q_ref[st, :, h * HEAD : (h + 1) * HEAD]
            top = jnp.full((STRETCH, BLOCK), -jnp.inf, F32)
            for n in range(4):
                part = before if n < 2 else k_ref[st]
                s = dot_t(q, part[(n % 2) * BLOCK : (n % 2 + 1) * BLOCK])
                ok = (mask_ref[h, :, n * BLOCK : (n + 1) * BLOCK] > 0.5) & (meta_ref[0, 8 * st + 4 + n] > 0)
                top = jnp.maximum(top, jnp.where(ok, s, -jnp.inf))
            top_ref[st, h] = top


def fetch(at_ref, pieces, target_ref):
    base = 0
    for ref in pieces:
        def copy(i, _, ref=ref, base=base):
            for n in range(UNROLL):
                target_ref[at_ref[0, base + i * UNROLL + n]] = ref[i * UNROLL + n]
            return 0

        lax.fori_loop(0, ref.shape[0] // UNROLL, copy, 0)
        base += ref.shape[0]


def causal(blk_ref, s, g):
    lead = lax.broadcasted_iota(jnp.int32, (STRETCH, BLOCK), 1) - lax.broadcasted_iota(jnp.int32, (STRETCH, BLOCK), 0)
    return [lead <= s * STRETCH - blk_ref[0, g * GROUP + n] * BLOCK for n in range(GROUP)]


def top_kernel(meta_ref, blk_ref, at_ref, q_ref, top_in_ref, *refs):
    pieces, (keys_ref, top_ref) = refs[:-2], refs[-2:]
    fetch(at_ref, pieces, keys_ref)
    for st in range(2):
        full, seen, s = meta_ref[0, 8 * st], meta_ref[0, 8 * st + 1], meta_ref[0, 8 * st + 2]
        plain, groups = full // GROUP, (seen + GROUP - 1) // GROUP
        for h in range(HEADS):
            top_ref[st, h] = top_in_ref[st, h]

        def step(masked, g, _):
            keys = keys_ref[pl.ds(g * GROUP, GROUP)].reshape(SPAN, HEAD)
            ok = causal(blk_ref, s, g) if masked else None
            for h in range(HEADS):
                scores = dot_t(q_ref[st, :, h * HEAD : (h + 1) * HEAD], keys)
                tops = []
                for n in range(GROUP):
                    part = scores[:, n * BLOCK : (n + 1) * BLOCK]
                    tops.append(jnp.where(ok[n], part, -jnp.inf) if masked else part)
                top = functools.reduce(jnp.maximum, tops)
                top_ref[st, h] = jnp.maximum(top_ref[st, h], top)
            return 0

        lax.fori_loop(0, plain, functools.partial(step, False), 0)
        lax.fori_loop(plain, groups, functools.partial(step, True), 0)
        for h in range(HEADS):
            row = jnp.max(top_ref[st, h], axis=1, keepdims=True)
            top_ref[st, h] = jnp.broadcast_to(row, (STRETCH, BLOCK))


def out_kernel(ctx_count, st, arriving, meta_ref, blk_ref, at_ref, q_ref, keys_ref, top_ref, mask_ref, k_ref, v_ref, ahead_ref, back_ref, *refs):
    full, seen, s = meta_ref[0, 8 * st], meta_ref[0, 8 * st + 1], meta_ref[0, 8 * st + 2]
    me = meta_ref[0, 8 * st + 3]
    plain, groups = full // GROUP, (seen + GROUP - 1) // GROUP
    if arriving:
        pieces, (out_ref, vals, total, acc) = refs[:arriving], refs[-4:]
        fetch(at_ref, pieces, vals)
    else:
        vals, out_ref, total, acc = refs
    k_before = band_halves(k_ref, ahead_ref, back_ref, 0, st, me, ctx_count)
    v_before = band_halves(v_ref, ahead_ref, back_ref, 1, st, me, ctx_count)

    for h in range(HEADS):
        q = q_ref[0, :, h * HEAD : (h + 1) * HEAD]
        scores = [dot_t(q, k_before), dot_t(q, k_ref[st])]
        expos = []
        for n in range(4):
            part = scores[n // 2][:, (n % 2) * BLOCK : (n % 2 + 1) * BLOCK]
            ok = (mask_ref[h, :, n * BLOCK : (n + 1) * BLOCK] > 0.5) & (meta_ref[0, 8 * st + 4 + n] > 0)
            expos.append(jnp.where(ok, jnp.exp2((part - top_ref[0, h]) * EXP_SCALE), 0.0))
        total[h] = (expos[0] + expos[1]) + (expos[2] + expos[3])
        weights = [e.astype(BF16) for e in expos]
        acc[h] = jnp.dot(
            jnp.concatenate(weights[:2], axis=1), v_before, preferred_element_type=F32
        ) + jnp.dot(jnp.concatenate(weights[2:], axis=1), v_ref[st], preferred_element_type=F32)

    def step(masked, g, _):
        keys = keys_ref[pl.ds(g * GROUP, GROUP)].reshape(SPAN, HEAD)
        values = vals[pl.ds(g * GROUP, GROUP)].reshape(SPAN, HEAD)
        ok = causal(blk_ref, s, g) if masked else None
        for h in range(HEADS):
            scores = dot_t(q_ref[0, :, h * HEAD : (h + 1) * HEAD], keys)
            expos = []
            for n in range(GROUP):
                part = jnp.exp2((scores[:, n * BLOCK : (n + 1) * BLOCK] - top_ref[0, h]) * EXP_SCALE)
                expos.append(jnp.where(ok[n], part, 0.0) if masked else part)
            total[h] += functools.reduce(jnp.add, expos)
            weights = jnp.concatenate([e.astype(BF16) for e in expos], axis=1)
            acc[h] += jnp.dot(weights, values, preferred_element_type=F32)
        return 0

    lax.fori_loop(0, plain, functools.partial(step, False), 0)
    lax.fori_loop(plain, groups, functools.partial(step, True), 0)
    for h in range(HEADS):
        row = jnp.sum(total[h], axis=1, keepdims=True)
        out_ref[:, h * HEAD : (h + 1) * HEAD] = (acc[h] / row).astype(BF16)


def mix_kernel(a0, a1, a2, a3, w0, w1, w2, w3, *refs):
    out_ref = refs[-1]
    sums = [jnp.dot(a[...], w[...], preferred_element_type=F32) for a, w in ((a0, w0), (a1, w1), (a2, w2), (a3, w3))]
    out_ref[0] = ((sums[0] + sums[1]) + (sums[2] + sums[3])).astype(BF16)


def from_ahead(x, axis, shift):
    n = lax.axis_size(axis)
    return lax.ppermute(x, axis, [((i + shift) % n, i) for i in range(n)])


def line_kernel(*refs):
    pieces, out_ref = refs[:X_CHIPS], refs[-1]
    for n, ref in enumerate(pieces):
        for which in range(2):
            out_ref[which, n * CAP : (n + 1) * CAP] = ref[which]


def chip_kernel(which, own_ref, other_ref, *refs):
    count = own_ref.shape[1]
    refs[-1][:count] = own_ref[which]
    refs[-1][count:] = other_ref[which]


def copy_kernel(source_ref, out_ref):
    out_ref[...] = source_ref[...]


def gather_columns(nx, nz, payload, later):
    place = lambda x, z, c: ((x % nx) * nz + z % nz) * 2 + c
    every = [(x, z, c) for x in range(nx) for z in range(nz) for c in range(2)]
    route = lambda f: [(place(*d), place(*f(*d))) for d in every]
    across = route(lambda x, z, c: (x, z, 1 - c))
    along = route(lambda x, z, c: (x, z + 1 - 2 * c, c))
    send = lambda a, r: lax.ppermute(a, "ctx", r)

    shape = jax.ShapeDtypeStruct
    call = functools.partial(pl.pallas_call, compiler_params=PARAMS)
    size = nx * CAP
    line = [payload] + [send(payload, route(lambda x, z, c, n=n: (x - n, z, c))) for n in range(1, nx)]
    own = call(
        line_kernel,
        out_shape=shape((2, size, BLOCK, HEAD), BF16),
        in_specs=[VMEM()] * nx,
        out_specs=VMEM(),
        name="line",
    )(*line)
    other = send(own, across)
    pieces = []
    waited = []
    for which in range(2):
        moving = call(
            functools.partial(chip_kernel, which),
            out_shape=shape((2 * size, BLOCK, HEAD), BF16),
            in_specs=[VMEM()] * 2 + [ANY()] * len(waited),
            out_specs=VMEM(),
            name=f"chip{which}",
        )(own, other, *waited)
        held = [moving]
        for n in range(1, nz // 2 + 1):
            last = n == nz // 2
            if which == 0 and last:
                moving = call(
                    copy_kernel,
                    grid=(1,),
                    out_shape=shape((size, BLOCK, HEAD), BF16),
                    in_specs=[pl.BlockSpec((size, BLOCK, HEAD), lambda i: (0, 0, 0))],
                    out_specs=VMEM(),
                    name="half",
                )(moving)
            moving = send(moving, along)
            held += [moving] + ([] if which == 1 and last else [send(moving, across)])
            if n == 1:
                waited = [moving, *later]
        pieces.append(held)
    return pieces


def arrivals(nx, nz, halves, me, entry):
    x, z, c = lax.div(me, 2 * nz), lax.rem(lax.div(me, 2), nz), lax.rem(me, 2)
    size = nx * CAP
    at = entry % (2 * size)
    piece = entry // (2 * size)
    hops = jnp.where(piece == 0, 0, (piece + 1) // 2)
    mirrored = jnp.where(piece == 0, 0, (piece + 1) % 2)
    half = at // size
    if halves:
        last = piece == nz - 1
        mirrored, half = jnp.where(last, half, mirrored), jnp.where(last, 0, half)
    side = jnp.where(mirrored == 1, 1 - 2 * c, 2 * c - 1) * hops
    core = jnp.where(mirrored == half, c, 1 - c)
    line = at % size // CAP
    return (((x + line) % nx * nz + (z + nz + side) % nz) * 2 + core) * CAP + at % CAP


def slab_kernel(tp, index_ref, weight_ref, *refs):
    width = weight_ref.shape[1] // tp
    for shift, ref in enumerate(refs[1:]):
        target = lax.rem(index_ref[0] + tp - shift, tp)
        ref[...] = weight_ref[:, pl.ds(pl.multiple_of(target * width, width), width)]


def cost(us):
    return pl.CostEstimate(flops=0, bytes_accessed=int(us * 3.0e6), transcendentals=0)


def per_device(queries, keys, values, column_block_table, slash_offsets, out_weight):
    ctx_count = lax.axis_size("ctx")
    tp = lax.axis_size("tp")
    me = lax.axis_index("ctx").reshape(1).astype(jnp.int32)
    tp_index = lax.axis_index("tp")
    q, k, v = queries[0], keys[0], values[0]
    shape = jax.ShapeDtypeStruct
    i32 = jnp.int32

    payload, ahead, back = pl.pallas_call(
        functools.partial(pack_kernel, ctx_count),
        out_shape=[shape((2, CAP, BLOCK, HEAD), BF16)] + [shape((2, STRETCH, HEAD), BF16)] * 2,
        in_specs=[SMEM(), VMEM(), VMEM(), VMEM()],
        out_specs=[VMEM()] * 3,
        compiler_params=PARAMS,
        name="pack",
    )(me, column_block_table, k.reshape(4, BLOCK, HEAD), v.reshape(4, BLOCK, HEAD))

    sides = (X_CHIPS, ctx_count // (2 * X_CHIPS))
    blk, key_at, val_at, meta = pl.pallas_call(
        functools.partial(plan_kernel, ctx_count, sides),
        out_shape=[shape((1, LISTED), i32)] + [shape((1, CAP * ctx_count), i32)] * 2 + [shape((1, 16), i32)],
        in_specs=[SMEM(), VMEM(), VMEM()],
        out_specs=[VMEM()] * 4,
        compiler_params=PARAMS,
        cost_estimate=cost(2),
        name="plan",
    )(me, column_block_table, column_block_table.reshape(LISTED, 1))

    steps = range(ctx_count - 1)
    before = lax.ppermute(ahead, "ctx", [(i, i + 1) for i in steps])
    after = lax.ppermute(back, "ctx", [(i + 1, i) for i in steps])

    mask, top = pl.pallas_call(
        functools.partial(band_kernel, ctx_count),
        out_shape=[shape((HEADS, STRETCH, 2 * STRETCH), F32), shape((2, HEADS, STRETCH, BLOCK), F32)],
        in_specs=[SMEM(), SMEM(), VMEM(), VMEM(), VMEM(), VMEM()],
        out_specs=[VMEM(), VMEM()],
        compiler_params=PARAMS,
        cost_estimate=cost(3),
        name="band",
    )(meta, slash_offsets, q, k, before, after)

    k_pieces, v_pieces = gather_columns(*sides, payload, [mask])

    width = out_weight.shape[1] // tp
    depth = out_weight.shape[0]
    slabs = pl.pallas_call(
        functools.partial(slab_kernel, tp),
        grid=(depth // 128,),
        out_shape=[shape((depth, width), BF16)] * tp,
        in_specs=[SMEM(), pl.BlockSpec((128, out_weight.shape[1]), lambda i: (i, 0)), ANY()],
        out_specs=[pl.BlockSpec((128, width), lambda i: (i, 0))] * tp,
        compiler_params=PARAMS,
        cost_estimate=cost(3),
        name="slabs",
    )(tp_index.reshape(1).astype(i32), out_weight, v_pieces[0])
    slabs = [slabs[0]] + [from_ahead(slabs[shift], "tp", shift) for shift in range(1, tp)]

    columns, top = pl.pallas_call(
        top_kernel,
        out_shape=[shape((ROOM, BLOCK, HEAD), BF16), shape((2, HEADS, STRETCH, BLOCK), F32)],
        in_specs=[SMEM(), SMEM(), SMEM(), VMEM(), VMEM()] + [VMEM()] * len(k_pieces),
        out_specs=[VMEM(), VMEM()],
        compiler_params=PARAMS,
        cost_estimate=cost(9),
        name="top",
    )(meta, blk, key_at, q, top, *k_pieces)

    mixed = column_vals = None
    for st in range(2):
        first = st == 0
        extra = [*v_pieces, slabs[1], slabs[3]] if first else [column_vals]
        result = pl.pallas_call(
            functools.partial(out_kernel, ctx_count, st, len(v_pieces) if first else 0),
            grid=(1,),
            out_shape=[shape((STRETCH, HEADS * HEAD), BF16)] + [shape((ROOM, BLOCK, HEAD), BF16)] * first,
            in_specs=[
                SMEM(), SMEM(), SMEM(),
                pl.BlockSpec((1, STRETCH, HEADS * HEAD), lambda i, st=st: (st, 0, 0)),
                VMEM(),
                pl.BlockSpec((1, HEADS, STRETCH, BLOCK), lambda i, st=st: (st, 0, 0, 0)),
                VMEM(), VMEM(), VMEM(), VMEM(), VMEM(),
            ] + ([VMEM()] * len(v_pieces) + [ANY()] * 2 if first else [VMEM()]),
            out_specs=[VMEM()] * (1 + first),
            scratch_shapes=[
                pltpu.VMEM((HEADS, STRETCH, BLOCK), F32),
                pltpu.VMEM((HEADS, STRETCH, HEAD), F32),
            ],
            compiler_params=PARAMS,
            cost_estimate=cost(8),
            name=f"attend{st}",
        )(meta, blk, val_at, q, columns, top, mask, k, v, before, after, *extra)
        head_out = result[0]
        if first:
            column_vals = result[1]
        parts = [head_out] + [from_ahead(head_out, "tp", shift) for shift in range(1, tp)]
        tile = width // 4
        mixed = pl.pallas_call(
            mix_kernel,
            grid=(width // tile,),
            out_shape=shape((2, STRETCH, width), BF16),
            in_specs=[VMEM()] * 4
            + [pl.BlockSpec((HEADS * HEAD, tile), lambda i: (0, i))] * 4
            + ([ANY()] if st else []),
            out_specs=pl.BlockSpec((1, STRETCH, tile), lambda i, st=st: (st, 0, i)),
            input_output_aliases={8: 0} if st else {},
            compiler_params=PARAMS,
            cost_estimate=cost(3),
            name=f"mix{st}",
        )(*parts, *slabs, *([mixed] if st else []))
    return mixed[None]


def solution(mesh):
    in_specs = (
        P("ctx", None, None, "tp"),
        P("ctx", None, None, "tp"),
        P("ctx", None, None, "tp"),
        P("tp", None),
        P("tp", None),
        P("tp", None),
    )
    out_specs = P("ctx", None, None, "tp")
    return jax.shard_map(
        per_device, mesh=mesh, in_specs=in_specs, out_specs=out_specs, check_vma=False
    )
```

```python
import functools
import math

import jax
import jax.numpy as jnp
from jax import lax
from jax.experimental import pallas as pl
from jax.experimental.pallas import tpu as pltpu
from jax.sharding import PartitionSpec as P

HEAD = 128
BLOCK = 128
STRETCH = 256
CAP = 2
GROUP = 8
SPAN = GROUP * BLOCK
LISTED = 64
ROOM = LISTED + 1
UNROLL = 4
X_CHIPS = 4
HEADS = 4
EXP_SCALE = math.log2(math.e) * HEAD ** (-0.5)
VMEM_LIMIT = 24 * 1024 * 1024

SMEM = functools.partial(pl.BlockSpec, memory_space=pltpu.SMEM)
VMEM = functools.partial(pl.BlockSpec, memory_space=pltpu.VMEM)
ANY = functools.partial(pl.BlockSpec, memory_space=pl.ANY)
PARAMS = pltpu.CompilerParams(vmem_limit_bytes=VMEM_LIMIT)
F32 = jnp.float32
BF16 = jnp.bfloat16


def dot_t(a, b):
    return lax.dot_general(a, b, (((1,), (1,)), ((), ())), preferred_element_type=F32)


def pack_kernel(ctx_count, me_ref, table_ref, k_ref, v_ref, pay_ref, ahead_ref, back_ref):
    me = me_ref[0]
    table = table_ref[...]
    owner = owned(table, ctx_count)
    local = jnp.where(table // 2 < ctx_count, 0, 2) + table % 2
    at = lax.broadcasted_iota(jnp.int32, table.shape, 1)
    mine = owner == me
    for slot in range(CAP):
        found = jnp.min(jnp.where(mine, at, LISTED))
        loc = jnp.sum(jnp.where(at == found, local, 0))
        mine = mine & (at > found)
        pay_ref[0, slot] = k_ref[loc]
        pay_ref[1, slot] = v_ref[loc]
    for half, ref in ((0, ahead_ref), (1, back_ref)):
        for part in range(2):
            ref[0, part * BLOCK : (part + 1) * BLOCK] = k_ref[2 * half + part]
            ref[1, part * BLOCK : (part + 1) * BLOCK] = v_ref[2 * half + part]


def owned(table, ctx_count):
    stretch = table // 2
    return jnp.where(stretch < ctx_count, stretch, 2 * ctx_count - 1 - stretch)


def plan_kernel(ctx_count, sides, me_ref, row_ref, col_ref, blk_ref, key_at_ref, val_at_ref, meta_ref):
    me = me_ref[0]
    row, col = row_ref[...], col_ref[...]
    square = (LISTED, LISTED)
    iota = lax.broadcasted_iota
    total = functools.partial(jnp.sum, keepdims=True)
    pick = lambda test, value, axis: total(jnp.where(test, value, 0), axis=axis)
    place = pick(row < col, jnp.int32(1), 1)
    earlier = iota(jnp.int32, square, 1) < iota(jnp.int32, square, 0)
    owner = owned(col, ctx_count)
    rank = pick((owned(row, ctx_count) == owner) & earlier, jnp.int32(1), 1)
    blk_ref[...] = pick(place == iota(jnp.int32, square, 1), col, 0)
    for halves, ref in ((True, key_at_ref), (False, val_at_ref)):
        entry = arrivals(*sides, halves, me, iota(jnp.int32, (1, CAP * ctx_count), 1))
        ref[...] = LISTED + pick(owner * CAP + rank == entry, place - LISTED, 0)
    lane = iota(jnp.int32, (1, 16), 1)
    meta = jnp.where(lane % 8 == 3, me, 0)
    for st, s in enumerate((me, 2 * ctx_count - 1 - me)):
        found = [jnp.sum(jnp.where(row < 2 * s, 1, 0)), jnp.sum(jnp.where(row <= 2 * s + 1, 1, 0)), s]
        for n, value in enumerate(found):
            meta = jnp.where(lane == 8 * st + n, value, meta)
        for n in range(4):
            b = 2 * (s - 1) + n
            free = 1 - jnp.max(jnp.where(row == b, 1, 0))
            meta = jnp.where(lane == 8 * st + 4 + n, jnp.where(b >= 0, free, 0), meta)
    meta_ref[...] = meta


def band_halves(own_ref, ahead_ref, back_ref, which, st, me, ctx_count):
    if st == 0:
        return ahead_ref[which]
    return jnp.where(me == ctx_count - 1, own_ref[0], back_ref[which])


def band_kernel(ctx_count, meta_ref, slash_ref, q_ref, k_ref, ahead_ref, back_ref, mask_ref, top_ref):
    behind = STRETCH - lax.broadcasted_iota(jnp.int32, (8, 2 * STRETCH), 1)
    for h in range(HEADS):
        def listed(n, hit):
            return hit | (behind == slash_ref[h, n])

        hit = behind == 0
        for n in range(LISTED):
            hit = listed(n, hit)
        row = jnp.where(hit, 1.0, 0.0).astype(F32)[:1]
        spread = jnp.broadcast_to(row, (STRETCH, 2 * STRETCH))
        mask_ref[h] = pltpu.roll(spread, 0, 1, stride=1, stride_axis=0)
    me = meta_ref[0, 3]
    for st in range(2):
        before = band_halves(k_ref, ahead_ref, back_ref, 0, st, me, ctx_count)
        for h in range(HEADS):
            q = q_ref[st, :, h * HEAD : (h + 1) * HEAD]
            top = jnp.full((STRETCH, BLOCK), -jnp.inf, F32)
            for n in range(4):
                part = before if n < 2 else k_ref[st]
                s = dot_t(q, part[(n % 2) * BLOCK : (n % 2 + 1) * BLOCK])
                ok = (mask_ref[h, :, n * BLOCK : (n + 1) * BLOCK] > 0.5) & (meta_ref[0, 8 * st + 4 + n] > 0)
                top = jnp.maximum(top, jnp.where(ok, s, -jnp.inf))
            top_ref[st, h] = top


def fetch(at_ref, pieces, target_ref):
    base = 0
    for ref in pieces:
        def copy(i, _, ref=ref, base=base):
            for n in range(UNROLL):
                target_ref[at_ref[0, base + i * UNROLL + n]] = ref[i * UNROLL + n]
            return 0

        lax.fori_loop(0, ref.shape[0] // UNROLL, copy, 0)
        base += ref.shape[0]


def causal(blk_ref, s, g):
    lead = lax.broadcasted_iota(jnp.int32, (STRETCH, BLOCK), 1) - lax.broadcasted_iota(jnp.int32, (STRETCH, BLOCK), 0)
    return [lead <= s * STRETCH - blk_ref[0, g * GROUP + n] * BLOCK for n in range(GROUP)]


def top_kernel(meta_ref, blk_ref, at_ref, q_ref, top_in_ref, *refs):
    pieces, (keys_ref, top_ref) = refs[:-2], refs[-2:]
    fetch(at_ref, pieces, keys_ref)
    for st in range(2):
        full, seen, s = meta_ref[0, 8 * st], meta_ref[0, 8 * st + 1], meta_ref[0, 8 * st + 2]
        plain, groups = full // GROUP, (seen + GROUP - 1) // GROUP
        for h in range(HEADS):
            top_ref[st, h] = top_in_ref[st, h]

        def step(masked, g, _):
            keys = keys_ref[pl.ds(g * GROUP, GROUP)].reshape(SPAN, HEAD)
            ok = causal(blk_ref, s, g) if masked else None
            for h in range(HEADS):
                scores = dot_t(q_ref[st, :, h * HEAD : (h + 1) * HEAD], keys)
                tops = []
                for n in range(GROUP):
                    part = scores[:, n * BLOCK : (n + 1) * BLOCK]
                    tops.append(jnp.where(ok[n], part, -jnp.inf) if masked else part)
                top = functools.reduce(jnp.maximum, tops)
                top_ref[st, h] = jnp.maximum(top_ref[st, h], top)
            return 0

        lax.fori_loop(0, plain, functools.partial(step, False), 0)
        lax.fori_loop(plain, groups, functools.partial(step, True), 0)
        for h in range(HEADS):
            row = jnp.max(top_ref[st, h], axis=1, keepdims=True)
            top_ref[st, h] = jnp.broadcast_to(row, (STRETCH, BLOCK))


def out_kernel(ctx_count, st, arriving, meta_ref, blk_ref, at_ref, q_ref, keys_ref, top_ref, mask_ref, k_ref, v_ref, ahead_ref, back_ref, *refs):
    full, seen, s = meta_ref[0, 8 * st], meta_ref[0, 8 * st + 1], meta_ref[0, 8 * st + 2]
    me = meta_ref[0, 8 * st + 3]
    plain, groups = full // GROUP, (seen + GROUP - 1) // GROUP
    if arriving:
        pieces, (out_ref, vals, total, acc) = refs[:arriving], refs[-4:]
        fetch(at_ref, pieces, vals)
    else:
        vals, out_ref, total, acc = refs
    k_before = band_halves(k_ref, ahead_ref, back_ref, 0, st, me, ctx_count)
    v_before = band_halves(v_ref, ahead_ref, back_ref, 1, st, me, ctx_count)

    for h in range(HEADS):
        q = q_ref[0, :, h * HEAD : (h + 1) * HEAD]
        scores = [dot_t(q, k_before), dot_t(q, k_ref[st])]
        expos = []
        for n in range(4):
            part = scores[n // 2][:, (n % 2) * BLOCK : (n % 2 + 1) * BLOCK]
            ok = (mask_ref[h, :, n * BLOCK : (n + 1) * BLOCK] > 0.5) & (meta_ref[0, 8 * st + 4 + n] > 0)
            expos.append(jnp.where(ok, jnp.exp2((part - top_ref[0, h]) * EXP_SCALE), 0.0))
        total[h] = (expos[0] + expos[1]) + (expos[2] + expos[3])
        weights = [e.astype(BF16) for e in expos]
        acc[h] = jnp.dot(
            jnp.concatenate(weights[:2], axis=1), v_before, preferred_element_type=F32
        ) + jnp.dot(jnp.concatenate(weights[2:], axis=1), v_ref[st], preferred_element_type=F32)

    def step(masked, g, _):
        keys = keys_ref[pl.ds(g * GROUP, GROUP)].reshape(SPAN, HEAD)
        values = vals[pl.ds(g * GROUP, GROUP)].reshape(SPAN, HEAD)
        ok = causal(blk_ref, s, g) if masked else None
        for h in range(HEADS):
            scores = dot_t(q_ref[0, :, h * HEAD : (h + 1) * HEAD], keys)
            expos = []
            for n in range(GROUP):
                part = jnp.exp2((scores[:, n * BLOCK : (n + 1) * BLOCK] - top_ref[0, h]) * EXP_SCALE)
                expos.append(jnp.where(ok[n], part, 0.0) if masked else part)
            total[h] += functools.reduce(jnp.add, expos)
            weights = jnp.concatenate([e.astype(BF16) for e in expos], axis=1)
            acc[h] += jnp.dot(weights, values, preferred_element_type=F32)
        return 0

    lax.fori_loop(0, plain, functools.partial(step, False), 0)
    lax.fori_loop(plain, groups, functools.partial(step, True), 0)
    for h in range(HEADS):
        row = jnp.sum(total[h], axis=1, keepdims=True)
        out_ref[:, h * HEAD : (h + 1) * HEAD] = (acc[h] / row).astype(BF16)


def mix_kernel(a0, a1, a2, a3, w0, w1, w2, w3, *refs):
    out_ref = refs[-1]
    sums = [jnp.dot(a[...], w[...], preferred_element_type=F32) for a, w in ((a0, w0), (a1, w1), (a2, w2), (a3, w3))]
    out_ref[0] = ((sums[0] + sums[1]) + (sums[2] + sums[3])).astype(BF16)


def from_ahead(x, axis, shift):
    n = lax.axis_size(axis)
    return lax.ppermute(x, axis, [((i + shift) % n, i) for i in range(n)])


def line_kernel(*refs):
    pieces, out_ref = refs[:X_CHIPS], refs[-1]
    for n, ref in enumerate(pieces):
        for which in range(2):
            out_ref[which, n * CAP : (n + 1) * CAP] = ref[which]


def chip_kernel(which, own_ref, other_ref, *refs):
    count = own_ref.shape[1]
    refs[-1][:count] = own_ref[which]
    refs[-1][count:] = other_ref[which]


def copy_kernel(source_ref, *refs):
    refs[-1][...] = source_ref[...]


def gather_columns(nx, nz, payload, later):
    place = lambda x, z, c: ((x % nx) * nz + z % nz) * 2 + c
    every = [(x, z, c) for x in range(nx) for z in range(nz) for c in range(2)]
    route = lambda f: [(place(*d), place(*f(*d))) for d in every]
    across = route(lambda x, z, c: (x, z, 1 - c))
    along = route(lambda x, z, c: (x, z + 1 - 2 * c, c))
    send = lambda a, r: lax.ppermute(a, "ctx", r)

    shape = jax.ShapeDtypeStruct
    call = functools.partial(pl.pallas_call, compiler_params=PARAMS)
    size = nx * CAP
    line = [payload] + [send(payload, route(lambda x, z, c, n=n: (x - n, z, c))) for n in range(1, nx)]
    own = call(
        line_kernel,
        out_shape=shape((2, size, BLOCK, HEAD), BF16),
        in_specs=[VMEM()] * nx,
        out_specs=VMEM(),
        name="line",
    )(*line)
    other = send(own, across)
    pieces = []
    waited = []
    for which in range(2):
        moving = call(
            functools.partial(chip_kernel, which),
            out_shape=shape((2 * size, BLOCK, HEAD), BF16),
            in_specs=[VMEM()] * 2 + [ANY()] * len(waited),
            out_specs=VMEM(),
            name=f"chip{which}",
        )(own, other, *waited)
        held = [moving]
        for n in range(1, nz // 2 + 1):
            last = n == nz // 2
            if which == 0 and last:
                moving = call(
                    copy_kernel,
                    grid=(1,),
                    out_shape=shape((size, BLOCK, HEAD), BF16),
                    in_specs=[pl.BlockSpec((size, BLOCK, HEAD), lambda i: (0, 0, 0))] + [ANY()] * len(later),
                    out_specs=VMEM(),
                    name="half",
                )(moving, *later)
            moving = send(moving, along)
            held += [moving] + ([] if which == 1 and last else [send(moving, across)])
            if n == 1:
                waited = [moving]
        pieces.append(held)
    return pieces


def arrivals(nx, nz, halves, me, entry):
    x, z, c = lax.div(me, 2 * nz), lax.rem(lax.div(me, 2), nz), lax.rem(me, 2)
    size = nx * CAP
    at = entry % (2 * size)
    piece = entry // (2 * size)
    hops = jnp.where(piece == 0, 0, (piece + 1) // 2)
    mirrored = jnp.where(piece == 0, 0, (piece + 1) % 2)
    half = at // size
    if halves:
        last = piece == nz - 1
        mirrored, half = jnp.where(last, half, mirrored), jnp.where(last, 0, half)
    side = jnp.where(mirrored == 1, 1 - 2 * c, 2 * c - 1) * hops
    core = jnp.where(mirrored == half, c, 1 - c)
    line = at % size // CAP
    return (((x + line) % nx * nz + (z + nz + side) % nz) * 2 + core) * CAP + at % CAP


def slab_kernel(tp, index_ref, weight_ref, *refs):
    width = weight_ref.shape[1] // tp
    for shift, ref in enumerate(refs[-tp:]):
        target = lax.rem(index_ref[0] + tp - shift, tp)
        ref[...] = weight_ref[:, pl.ds(pl.multiple_of(target * width, width), width)]


def cost(us):
    return pl.CostEstimate(flops=0, bytes_accessed=int(us * 3.0e6), transcendentals=0)


def per_device(queries, keys, values, column_block_table, slash_offsets, out_weight):
    ctx_count = lax.axis_size("ctx")
    tp = lax.axis_size("tp")
    me = lax.axis_index("ctx").reshape(1).astype(jnp.int32)
    tp_index = lax.axis_index("tp")
    q, k, v = queries[0], keys[0], values[0]
    shape = jax.ShapeDtypeStruct
    i32 = jnp.int32

    payload, ahead, back = pl.pallas_call(
        functools.partial(pack_kernel, ctx_count),
        out_shape=[shape((2, CAP, BLOCK, HEAD), BF16)] + [shape((2, STRETCH, HEAD), BF16)] * 2,
        in_specs=[SMEM(), VMEM(), VMEM(), VMEM()],
        out_specs=[VMEM()] * 3,
        compiler_params=PARAMS,
        name="pack",
    )(me, column_block_table, k.reshape(4, BLOCK, HEAD), v.reshape(4, BLOCK, HEAD))

    sides = (X_CHIPS, ctx_count // (2 * X_CHIPS))
    blk, key_at, val_at, meta = pl.pallas_call(
        functools.partial(plan_kernel, ctx_count, sides),
        out_shape=[shape((1, LISTED), i32)] + [shape((1, CAP * ctx_count), i32)] * 2 + [shape((1, 16), i32)],
        in_specs=[SMEM(), VMEM(), VMEM()],
        out_specs=[VMEM()] * 4,
        compiler_params=PARAMS,
        cost_estimate=cost(2),
        name="plan",
    )(me, column_block_table, column_block_table.reshape(LISTED, 1))

    steps = range(ctx_count - 1)
    before = lax.ppermute(ahead, "ctx", [(i, i + 1) for i in steps])
    after = lax.ppermute(back, "ctx", [(i + 1, i) for i in steps])

    mask, top = pl.pallas_call(
        functools.partial(band_kernel, ctx_count),
        out_shape=[shape((HEADS, STRETCH, 2 * STRETCH), F32), shape((2, HEADS, STRETCH, BLOCK), F32)],
        in_specs=[SMEM(), SMEM(), VMEM(), VMEM(), VMEM(), VMEM()],
        out_specs=[VMEM(), VMEM()],
        compiler_params=PARAMS,
        cost_estimate=cost(3),
        name="band",
    )(meta, slash_offsets, q, k, before, after)

    k_pieces, v_pieces = gather_columns(*sides, payload, [mask])

    width = out_weight.shape[1] // tp
    depth = out_weight.shape[0]
    slabs = pl.pallas_call(
        functools.partial(slab_kernel, tp),
        grid=(depth // 128,),
        out_shape=[shape((depth, width), BF16)] * tp,
        in_specs=[SMEM(), pl.BlockSpec((128, out_weight.shape[1]), lambda i: (i, 0))] + [ANY()] * 3,
        out_specs=[pl.BlockSpec((128, width), lambda i: (i, 0))] * tp,
        compiler_params=PARAMS,
        cost_estimate=cost(3),
        name="slabs",
    )(tp_index.reshape(1).astype(i32), out_weight, v_pieces[0], before, after)
    slabs = [slabs[0]] + [from_ahead(slabs[shift], "tp", shift) for shift in range(1, tp)]

    columns, top = pl.pallas_call(
        top_kernel,
        out_shape=[shape((ROOM, BLOCK, HEAD), BF16), shape((2, HEADS, STRETCH, BLOCK), F32)],
        in_specs=[SMEM(), SMEM(), SMEM(), VMEM(), VMEM()] + [VMEM()] * len(k_pieces),
        out_specs=[VMEM(), VMEM()],
        compiler_params=PARAMS,
        cost_estimate=cost(9),
        name="top",
    )(meta, blk, key_at, q, top, *k_pieces)

    mixed = column_vals = None
    for st in range(2):
        first = st == 0
        extra = [*v_pieces, slabs[1], slabs[3]] if first else [column_vals]
        result = pl.pallas_call(
            functools.partial(out_kernel, ctx_count, st, len(v_pieces) if first else 0),
            grid=(1,),
            out_shape=[shape((STRETCH, HEADS * HEAD), BF16)] + [shape((ROOM, BLOCK, HEAD), BF16)] * first,
            in_specs=[
                SMEM(), SMEM(), SMEM(),
                pl.BlockSpec((1, STRETCH, HEADS * HEAD), lambda i, st=st: (st, 0, 0)),
                VMEM(),
                pl.BlockSpec((1, HEADS, STRETCH, BLOCK), lambda i, st=st: (st, 0, 0, 0)),
                VMEM(), VMEM(), VMEM(), VMEM(), VMEM(),
            ] + ([VMEM()] * len(v_pieces) + [ANY()] * 2 if first else [VMEM()]),
            out_specs=[VMEM()] * (1 + first),
            scratch_shapes=[
                pltpu.VMEM((HEADS, STRETCH, BLOCK), F32),
                pltpu.VMEM((HEADS, STRETCH, HEAD), F32),
            ],
            compiler_params=PARAMS,
            cost_estimate=cost(8),
            name=f"attend{st}",
        )(meta, blk, val_at, q, columns, top, mask, k, v, before, after, *extra)
        head_out = result[0]
        if first:
            column_vals = result[1]
        parts = [head_out] + [from_ahead(head_out, "tp", shift) for shift in range(1, tp)]
        tile = width // 4
        mixed = pl.pallas_call(
            mix_kernel,
            grid=(width // tile,),
            out_shape=shape((2, STRETCH, width), BF16),
            in_specs=[VMEM()] * 4
            + [pl.BlockSpec((HEADS * HEAD, tile), lambda i: (0, i))] * 4
            + ([ANY()] if st else []),
            out_specs=pl.BlockSpec((1, STRETCH, tile), lambda i, st=st: (st, 0, i)),
            input_output_aliases={8: 0} if st else {},
            compiler_params=PARAMS,
            cost_estimate=cost(3),
            name=f"mix{st}",
        )(*parts, *slabs, *([mixed] if st else []))
    return mixed[None]


def solution(mesh):
    in_specs = (
        P("ctx", None, None, "tp"),
        P("ctx", None, None, "tp"),
        P("ctx", None, None, "tp"),
        P("tp", None),
        P("tp", None),
        P("tp", None),
    )
    out_specs = P("ctx", None, None, "tp")
    return jax.shard_map(
        per_device, mesh=mesh, in_specs=in_specs, out_specs=out_specs, check_vma=False
    )
```
